256 devices in a mesh: seq: 32 (over y, z), grp: 8 (over x, core).
Axes of the slice: x: 4, y: 4, z: 8, core: 2. Of those that a mesh axis runs over, the one named last changes fastest.
Arguments:
- queries: bfloat16 [8, 128, 8192], P('grp', None, 'seq'), may hold values from -64 to 64
- kv_cache: bfloat16 [8, 32768, 1024], P('grp', 'seq'), may hold values from -40 to 40
- kv_scale: float32 [8, 256, 8], P('grp', 'seq'), may hold values from 0.5 to 2
- block_mask: int32 [8, 1, 256], P('grp'), may hold values from 0 to 1, as said below
- resid: bfloat16 [8, 128, 4096], P('grp', 'seq'), may hold values from -4 to 4
- w_out: bfloat16 [8192, 4096], P('seq'), may hold values from -0.0625 to 0.0625
- norm_gain: float32 [4096], replicated, may hold values from 0.5 to 1.5
- expert_ids: int32 [8, 128, 8], P('grp'), may hold values from 0 to 31, all different within a row; in each aligned block of 128 rows (0 to 127, 128 to 255, ..., all dimensions but the last counted through in order) at most 64 rows name the same one
- gate_weights: float32 [8, 128, 8], P('grp'), may hold values from 0.05 to 1
- w_gate: bfloat16 [8, 6144, 4096], P('grp', 'seq'), may hold values from -0.09375 to 0.09375
- w_up: bfloat16 [8, 6144, 4096], P('grp', 'seq'), may hold values from -0.09375 to 0.09375
- w_down: bfloat16 [8, 6144, 4096], P('grp', 'seq'), may hold values from -0.15625 to 0.15625
Outputs:
- out: bfloat16 [8, 128, 4096], P('grp', 'seq')
The draws below stay inside these ranges and needn't reach their ends.
Inputs may be any that keep to these rules, and one draw needn't show every extreme that they name: `block_mask`: every block of window rows may read the first key block and its own. `expert_ids`: each token names 8 different experts; in every trajectory no expert is named by more than 64 tokens, a bound that some block reaches.
All inputs are finite; a program needn't handle non-finite values.
Results may differ from the reference program's by a relative error of at most 0.038.
Values may be sent and summed in bfloat16 or wider, within the bound.
No kernel may reach another device: no remote copies, remote signals or barrier semaphores. Data moves between devices by JAX's collectives and lax.ppermute only.
A program may use at most 128 MiB of HBM per device.

```python
import math
import jax
import jax.numpy as jnp
import numpy as np
from jax import lax

D = 4096
HEADS = 64
KV_HEADS = 4
HEAD_DIM = 128
FF_E = 1536
TOPK = 8
BLOCK = 128
E_SUB = 4
WIN = 128
TRAJ = 8
CTX = 32768
EXPERTS = 32
CAP = 64
N_SEQ = 32
N_GRP = 8


def cache_base(key):
    raw_values = jax.random.normal(jax.random.fold_in(key, 11), (TRAJ, CTX, 2 * KV_HEADS * HEAD_DIM), jnp.float32)
    raw_values = jnp.clip(raw_values, -4.0, 4.0)
    scales = jax.random.uniform(jax.random.fold_in(key, 12), (TRAJ, CTX // BLOCK, 2 * KV_HEADS), jnp.float32, 0.5, 2.0)
    return (raw_values, scales)


def draw_kv_cache(key, part):
    raw_values, scales = cache_base(key)
    return raw_values.astype(jnp.bfloat16)


def draw_kv_scale(key, part):
    raw_values, scales = cache_base(key)
    return scales


def draw_queries(key, part):
    key = jax.random.fold_in(key, 5)
    query = jnp.clip(jax.random.normal(key, (TRAJ, WIN, HEADS * HEAD_DIM), jnp.float32), -5.0, 5.0)
    return query.astype(jnp.bfloat16)


def draw_block_mask(key, part):
    key = jax.random.fold_in(key, 7)
    blocks_all = CTX // BLOCK
    row_blocks = WIN // BLOCK
    first_row = blocks_all - row_blocks
    key_block = jnp.arange(blocks_all, dtype=jnp.int32)[None, None, :]
    query_block = (first_row + jnp.arange(row_blocks, dtype=jnp.int32))[None, :, None]
    keys_split = jax.random.split(key, 2)
    back = jax.random.randint(keys_split[0], (TRAJ, 1, 1), 0, 3)
    stale = jax.random.randint(keys_split[1], (TRAJ, 1, blocks_all), 0, 5) == 0
    prompt = key_block < 2
    own_turn = key_block >= first_row - back
    kept = prompt | own_turn | jnp.logical_not(stale)
    allowed = kept & (key_block <= query_block)
    return allowed.astype(jnp.int32)


def level_of(own_key, dims, cuts, low, largest):
    factor_of = 1.0
    for dim, parts in cuts:
        draws = jax.random.uniform(jax.random.fold_in(jax.random.fold_in(own_key, 6), dim), (parts,), jnp.float32, low / len(cuts), largest / len(cuts))
        factor_of = factor_of * jnp.repeat(jnp.exp(draws), dims[dim] // parts).reshape((-1,) + (1,) * (len(dims) - 1 - dim))
    return factor_of


def assign_block(stream_key, own, number, rows, amount, top, most, slope):
    sequence = jax.random.permutation(stream_key, amount)
    crowded, usual = shares(amount, rows * top, most, slope, True), shares(amount, rows * top, most, slope, False)
    places = jnp.arange(amount)

    def named(lengths, offset_by):
        used = int((lengths > 0).sum())
        fixed = max(1, used // 4)
        passed = fixed + (places - fixed + offset_by * (used - fixed)) % max(1, amount - fixed)
        return jnp.zeros((amount,), jnp.int32).at[sequence[jnp.where(places < fixed, places, passed)]].set(jnp.asarray(lengths, jnp.int32))

    lengths = jnp.where(number % 4 == 0, named(crowded, number // 4), named(usual, number - number // 4 - 1))
    mixed = jax.random.permutation(jax.random.fold_in(own, 3), amount)
    source_of, receiver = mixed[0:amount // 2 * 2:2], mixed[1:amount // 2 * 2:2]
    room = jnp.minimum(lengths[source_of] - 1, most - lengths[receiver]) // 2
    room = jnp.where((source_of == sequence[0]) | (receiver == sequence[0]) | (lengths[receiver] == 0), 0, jnp.maximum(room, 0))
    passed = jax.random.randint(jax.random.fold_in(own, 4), (amount // 2,), 0, 1 << 20) % (room + 1)
    lengths = lengths.at[source_of].add(-passed).at[receiver].add(passed)
    members = jnp.searchsorted(jnp.cumsum(lengths), jnp.arange(rows * top), side="right").astype(jnp.int32)
    table = members.reshape(top, rows).T
    table = table[jax.random.permutation(jax.random.fold_in(own, 1), rows)]
    offset_by = jax.random.randint(jax.random.fold_in(own, 2), (rows, 1), 0, top)
    return jnp.take_along_axis(table, (jnp.arange(top)[None, :] + offset_by) % top, axis=1)


def shares(amount, total, bound, lean, full):
    weights = [(1 << 20) // math.isqrt(rank ** lean) + 1 for rank in range(1, amount + 1)]
    largest = bound if full else min(bound, max(-(-total // amount), total * weights[0] // sum(weights)))
    least = 1 if total - largest >= amount - 1 else 0
    holding, spare = [largest] + [least] * (amount - 1), total - largest - least * (amount - 1)
    while spare > 0:
        candidates = [i for i in range(1, amount) if holding[i] < largest] or [i for i in range(1, amount) if holding[i] < bound]
        pool, remaining = sum([weights[i] for i in candidates]), spare
        for i in candidates:
            more = min(bound - holding[i], max(1, remaining * weights[i] // pool), spare)
            holding[i] = holding[i] + more
            spare = spare - more
    return np.array(holding)


def normal_values(rng, shape, scale, limit, cuts=(), kind=jnp.bfloat16):
    values = scale * jax.random.normal(rng, shape, jnp.float32)
    if cuts:
        values = values * level_of(rng, shape, cuts, -0.22, 0.18)
    return jnp.clip(values, -limit, limit).astype(kind)


def setup_inputs(seed: int = 0) -> dict:
    seeds = jax.random.split(jax.random.key(seed), 13)
    queries = draw_queries(jax.random.fold_in(seeds[12], 71), 0)
    kv_cache = draw_kv_cache(jax.random.fold_in(seeds[12], 71), 0)
    kv_scale = draw_kv_scale(jax.random.fold_in(seeds[12], 71), 0)
    block_mask = draw_block_mask(jax.random.fold_in(seeds[12], 71), 0)
    resid = normal_values(seeds[4], (TRAJ, WIN, D), 0.5, 4.0, ((0, 8), (1, 32)))
    w_out = normal_values(seeds[5], (HEADS * HEAD_DIM, D), (HEADS * HEAD_DIM) ** -0.5, 0.0625, ((0, 32),))
    norm_gain = jnp.clip(1.0 + 0.1 * jax.random.normal(seeds[6], (D,), jnp.float32), 0.5, 1.5)
    expert_ids_keys = jax.random.split(jax.random.fold_in(seeds[7], 1), TRAJ * WIN // WIN)
    expert_ids_turns = jax.random.permutation(jax.random.fold_in(seeds[7], 3), TRAJ * WIN // WIN)
    expert_ids = jax.vmap(lambda own, number: assign_block(jax.random.fold_in(seeds[7], 2), own, number, WIN, EXPERTS, TOPK, CAP, 2))(expert_ids_keys, expert_ids_turns).reshape((TRAJ, WIN, TOPK))
    gate_weights = jnp.clip(0.05 + 0.95 * jax.random.uniform(seeds[8], (TRAJ, WIN, TOPK), jnp.float32) ** level_of(seeds[8], (TRAJ, WIN, TOPK), ((0, 8),), -0.2, 0.2), 0.05, 1.0)
    w_gate = normal_values(seeds[9], (N_GRP, E_SUB * FF_E, D), D ** -0.5, 0.09375, ((0, 8), (1, 32)))
    w_up = normal_values(seeds[10], (N_GRP, E_SUB * FF_E, D), D ** -0.5, 0.09375, ((0, 8), (1, 32)))
    w_down = normal_values(seeds[11], (N_GRP, E_SUB * FF_E, D), FF_E ** -0.5, 0.15625, ((0, 8), (1, 32)))
    return dict(queries=queries, kv_cache=kv_cache, kv_scale=kv_scale, block_mask=block_mask, resid=resid, w_out=w_out, norm_gain=norm_gain, expert_ids=expert_ids, gate_weights=gate_weights, w_gate=w_gate, w_up=w_up, w_down=w_down)


def dequantize(values, scales):
    spread = jnp.repeat(jnp.repeat(scales, BLOCK, axis=0), HEAD_DIM, axis=1)
    return (values.astype(jnp.float32) * spread).astype(jnp.bfloat16)

def rms_norm(stream, gain):
    rows_wide = lax.optimization_barrier(stream).astype(jnp.float32)
    factor = lax.rsqrt(lax.optimization_barrier(jnp.mean(rows_wide * rows_wide, axis=-1, keepdims=True)) + 1e-06)
    return (rows_wide * factor * gain).astype(jnp.bfloat16)

def attend(bundle):
    query, values, scales, blocks = bundle
    keyvals = lax.optimization_barrier(dequantize(values, scales)).astype(jnp.float32)
    per_kv = HEADS // KV_HEADS
    rows_index = jnp.arange(WIN, dtype=jnp.int32)
    cols_index = jnp.arange(CTX, dtype=jnp.int32)
    block_rows = jnp.repeat(jnp.repeat(blocks, BLOCK, axis=0), BLOCK, axis=1) == 1
    allowed = block_rows & (cols_index[None, :] <= CTX - WIN + rows_index[:, None])
    score_scale = 1.0 / math.sqrt(HEAD_DIM)
    pieces = []
    for kv_head in range(KV_HEADS):
        query_block = query[:, kv_head * per_kv * HEAD_DIM:(kv_head + 1) * per_kv * HEAD_DIM]
        query_block = query_block.reshape(WIN, per_kv, HEAD_DIM).astype(jnp.float32)
        key_block = keyvals[:, kv_head * HEAD_DIM:(kv_head + 1) * HEAD_DIM]
        value_block = keyvals[:, (KV_HEADS + kv_head) * HEAD_DIM:(KV_HEADS + kv_head + 1) * HEAD_DIM]
        scores = jnp.einsum('wgd,kd->gwk', query_block, key_block) * score_scale
        masked = jnp.where(allowed[None], scores, -jnp.inf)
        highest = lax.optimization_barrier(jnp.max(masked, axis=-1, keepdims=True))
        weights = jnp.exp(masked - highest)
        denominator = lax.optimization_barrier(jnp.sum(weights, axis=-1))
        rounded = lax.optimization_barrier(weights.astype(jnp.bfloat16)).astype(jnp.float32)
        summed = jnp.einsum('gwk,kd->wgd', rounded, value_block)
        pieces.append((summed / jnp.transpose(denominator)[:, :, None]).reshape(WIN, per_kv * HEAD_DIM))
    return jnp.concatenate(pieces, axis=1).astype(jnp.bfloat16)

def reference(queries, kv_cache, kv_scale, block_mask, resid, w_out, norm_gain, expert_ids, gate_weights, w_gate, w_up, w_down):
    attended = lax.map(attend, (queries, kv_cache, kv_scale, block_mask))
    projected = jnp.dot(attended.reshape(TRAJ * WIN, HEADS * HEAD_DIM), w_out, preferred_element_type=jnp.float32)
    stream = (resid.astype(jnp.float32) + projected.reshape(TRAJ, WIN, D)).astype(jnp.bfloat16)
    stream_wide = lax.optimization_barrier(stream).astype(jnp.float32)
    normed = rms_norm(stream, norm_gain)
    normed_wide = lax.optimization_barrier(normed).astype(jnp.float32)
    slices = N_SEQ // E_SUB
    part_units = FF_E // slices
    gate_all = w_gate.reshape(EXPERTS, FF_E, D)
    up_all = w_up.reshape(EXPERTS, FF_E, D)
    down_all = w_down.reshape(EXPERTS, FF_E, D)
    slot_range = jnp.arange(CAP, dtype=jnp.int32)

    def expert_step(total, expert):
        matches = expert_ids == expert
        chosen = jnp.any(matches, axis=-1)
        weight = lax.optimization_barrier(jnp.sum(jnp.where(matches, gate_weights, 0.0), axis=-1))
        slot_index = jnp.cumsum(chosen.astype(jnp.int32), axis=1) - 1
        onehot = (chosen[:, None, :] & (slot_index[:, None, :] == slot_range[None, :, None])).astype(jnp.float32)
        inputs = jnp.einsum('tcw,twd->tcd', onehot, normed_wide)
        gate_part = jnp.einsum('tcd,hd->tch', inputs, gate_all[expert].astype(jnp.float32))
        up_part = jnp.einsum('tcd,hd->tch', inputs, up_all[expert].astype(jnp.float32))
        hidden = (jax.nn.silu(gate_part) * up_part).astype(jnp.bfloat16)
        hidden = lax.optimization_barrier(hidden).astype(jnp.float32)
        hidden = hidden.reshape(TRAJ, CAP, slices, part_units)
        down_parts = down_all[expert].astype(jnp.float32).reshape(slices, part_units, D)
        pieces = jnp.einsum('tcsh,shd->tcsd', hidden, down_parts).astype(jnp.bfloat16)
        pieces = lax.optimization_barrier(pieces).astype(jnp.float32)
        result = lax.optimization_barrier(jnp.sum(pieces, axis=2))
        spread = jnp.einsum('tcw,tcd->twd', onehot, result)
        return (total + spread * weight[:, :, None], None)
    start = jnp.zeros((TRAJ, WIN, D), jnp.float32)
    mixture, unused = lax.scan(expert_step, start, jnp.arange(EXPERTS, dtype=jnp.int32))
    return (stream_wide + mixture).astype(jnp.bfloat16)
```

```python
import math

import jax
import jax.numpy as jnp
from jax import lax
from jax.experimental import pallas as pl
from jax.experimental.pallas import tpu as pltpu
from jax.sharding import Mesh
from jax.sharding import PartitionSpec as P

HEADS = 64
KV_HEADS = 4
HEAD_DIM = 128
BLOCK = 128
E_SUB = 4
CAP = 64
N_Y, N_Z, N_X, N_C = 4, 8, 4, 2
N_GRP = N_X * N_C
WIN = 128
D = 4096
COLS = D // N_Z
CTX_LOCAL = 1024
HIDDEN = 192
STAT_ROWS = 16
MASKED = -1e30
SCALE2 = math.log2(math.e) / math.sqrt(HEAD_DIM)
VMEM = 56 * 1024 * 1024

f32 = jnp.float32
bf16 = jnp.bfloat16


def params():
    return pltpu.CompilerParams(vmem_limit_bytes=VMEM)


def attention_kernel(q_ref, kv_ref, bias_ref, causal_ref, out_ref, s_ref):
    q_pair = jnp.concatenate([q_ref[0, :, :HEAD_DIM], q_ref[0, :, HEAD_DIM:]], axis=0)
    peak = jnp.full((2 * WIN, BLOCK), -jnp.inf, f32)
    for src in range(N_Y):
        s = lax.dot_general(
            q_pair, kv_ref[src, 0], (((1,), (1,)), ((), ())), preferred_element_type=f32
        )
        s = s + bias_ref[src]
        if src == N_Y - 1:
            s = jnp.concatenate(
                [s[:, : CTX_LOCAL - BLOCK], s[:, CTX_LOCAL - BLOCK :] + causal_ref[...]], axis=1
            )
        s_ref[:, src * CTX_LOCAL : (src + 1) * CTX_LOCAL] = s
        for b in range(CTX_LOCAL // BLOCK):
            peak = jnp.maximum(peak, s[:, b * BLOCK : (b + 1) * BLOCK])
    m = jnp.max(peak, axis=1, keepdims=True)
    total = jnp.zeros((2 * WIN, BLOCK), f32)
    acc = jnp.zeros((2 * WIN, HEAD_DIM), f32)
    for src in range(N_Y):
        s = s_ref[:, src * CTX_LOCAL : (src + 1) * CTX_LOCAL]
        p = jnp.exp2((s - m) * SCALE2)
        for b in range(CTX_LOCAL // BLOCK):
            total = total + p[:, b * BLOCK : (b + 1) * BLOCK]
        acc = acc + jnp.dot(p.astype(bf16), kv_ref[src, 1], preferred_element_type=f32)
    l = jnp.sum(total, axis=1, keepdims=True)
    out_ref[0, : 2 * WIN, :] = acc.astype(bf16)
    lane = lax.broadcasted_iota(jnp.int32, (2 * WIN, 128), 1)
    stats = jnp.zeros((2 * WIN, 128), f32)
    for i, value in enumerate((m, l)):
        rest = value
        for j in range(3):
            term = rest.astype(bf16).astype(f32)
            rest = rest - term
            stats = jnp.where(lane == i + 2 * j, term, stats)
    rows = jnp.transpose(stats)
    out_ref[0, 2 * WIN :, :] = jnp.concatenate([rows[:8, :WIN], rows[:8, WIN:]], axis=0).astype(
        bf16
    )


def attention(queries, keyvals, bias, causal):
    return pl.pallas_call(
        attention_kernel,
        grid=(N_Z,),
        in_specs=[
            pl.BlockSpec((1, WIN, 2 * HEAD_DIM), lambda i: (i, 0, 0)),
            pl.BlockSpec((N_Y, 2, CTX_LOCAL, HEAD_DIM), lambda i: (0, 0, 0, 0)),
            pl.BlockSpec((N_Y, 1, CTX_LOCAL), lambda i: (0, 0, 0)),
            pl.BlockSpec((2 * WIN, BLOCK), lambda i: (0, 0)),
        ],
        out_specs=pl.BlockSpec((1, 2 * WIN + STAT_ROWS, HEAD_DIM), lambda i: (i, 0, 0)),
        out_shape=jax.ShapeDtypeStruct((N_Z, 2 * WIN + STAT_ROWS, HEAD_DIM), bf16),
        scratch_shapes=[pltpu.VMEM((2 * WIN, N_Y * CTX_LOCAL), f32)],
        compiler_params=params(),
        name="attention",
    )(queries, keyvals, bias, causal)


def combine_kernel(in_ref, out_ref):
    stats = in_ref[:, 2 * WIN :, :].astype(f32)
    for head in range(2):
        st = stats[:, 8 * head : 8 * head + 8]
        m = st[:, 0] + st[:, 2] + st[:, 4]
        l = st[:, 1] + st[:, 3] + st[:, 5]
        w = jnp.exp2((m - jnp.max(m, axis=0, keepdims=True)) * SCALE2)
        w = w / jnp.sum(w * l, axis=0, keepdims=True)
        wide = jnp.concatenate([w, jnp.zeros((WIN - N_Z, WIN), f32)], axis=0)
        cols = jnp.transpose(wide)
        total = jnp.zeros((WIN, HEAD_DIM), f32)
        for z in range(N_Z):
            part = in_ref[z, head * WIN : (head + 1) * WIN, :].astype(f32)
            total = total + part * cols[:, z : z + 1]
        done = total.astype(bf16)
        for z in range(N_Z):
            out_ref[z, :, head * HEAD_DIM : (head + 1) * HEAD_DIM] = done


def combine(parts):
    return pl.pallas_call(
        combine_kernel,
        out_shape=jax.ShapeDtypeStruct((N_Z, WIN, 2 * HEAD_DIM), bf16),
        compiler_params=params(),
        name="combine",
    )(parts)


def project_kernel(a_ref, w_ref, resid_ref, out_ref):
    acc = resid_ref[...].astype(f32)
    for z in range(N_Z):
        acc = acc + jnp.dot(a_ref[z], w_ref[z], preferred_element_type=f32)
    done = acc.astype(bf16)
    for y in range(N_Y):
        out_ref[y] = done


def project(attended, w_cols, resid_rows):
    return pl.pallas_call(
        project_kernel,
        out_shape=jax.ShapeDtypeStruct((N_Y, WIN, COLS), bf16),
        compiler_params=params(),
        name="project",
    )(attended, w_cols, resid_rows)


def dispatch_kernel(parts_ref, table_ref, stream_ref, out_ref):
    total = parts_ref[0].astype(f32)
    for y in range(1, N_Y):
        total = total + parts_ref[y].astype(f32)
    stream = total.astype(bf16)
    stream_ref[...] = stream
    out_ref[...] = jnp.dot(table_ref[...], stream, preferred_element_type=f32).astype(bf16)


def dispatch(parts, table):
    return pl.pallas_call(
        dispatch_kernel,
        out_shape=(
            jax.ShapeDtypeStruct((WIN, COLS), bf16),
            jax.ShapeDtypeStruct((N_GRP * CAP, COLS), bf16),
        ),
        compiler_params=params(),
        name="dispatch",
    )(parts, table)


def experts_kernel(x_ref, gain_ref, wg_ref, wu_ref, wd_ref, out_ref):
    tokens = x_ref.shape[1]
    squares = jnp.zeros((tokens, COLS), f32)
    for z in range(N_Z):
        wide = x_ref[z].astype(f32)
        squares = squares + wide * wide
    factor = lax.rsqrt(jnp.sum(squares, axis=1, keepdims=True) * (1.0 / D) + 1e-06)
    gate = jnp.zeros((tokens, HIDDEN), f32)
    up = jnp.zeros((tokens, HIDDEN), f32)
    contract = (((1,), (1,)), ((), ()))
    for z in range(N_Z):
        cols = slice(z * COLS, (z + 1) * COLS)
        normed = (x_ref[z].astype(f32) * factor * gain_ref[:, cols]).astype(bf16)
        gate = gate + lax.dot_general(
            normed, wg_ref[:, cols], contract, preferred_element_type=f32
        )
        up = up + lax.dot_general(normed, wu_ref[:, cols], contract, preferred_element_type=f32)
    hidden = (gate / (1.0 + jnp.exp(-gate)) * up).astype(bf16)
    for z in range(N_Z):
        cols = slice(z * COLS, (z + 1) * COLS)
        out_ref[:, cols] = jnp.dot(
            hidden, wd_ref[:, cols], preferred_element_type=f32
        ).astype(bf16)


def experts(x, gain, w_gate, w_up, w_down, tile=128):
    tokens = x.shape[1]
    whole = pl.BlockSpec((HIDDEN, D), lambda i: (0, 0))
    return pl.pallas_call(
        experts_kernel,
        grid=(tokens // tile,),
        in_specs=[
            pl.BlockSpec((N_Z, tile, COLS), lambda i: (0, i, 0)),
            pl.BlockSpec((1, D), lambda i: (0, 0)),
            whole,
            whole,
            whole,
        ],
        out_specs=pl.BlockSpec((tile, D), lambda i: (i, 0)),
        out_shape=jax.ShapeDtypeStruct((tokens, D), bf16),
        compiler_params=params(),
        name="experts",
    )(x, gain, w_gate, w_up, w_down)


def mix_kernel(table_ref, parts_ref, out_ref):
    out_ref[...] = jnp.dot(
        table_ref[...], parts_ref[...], preferred_element_type=f32
    ).astype(bf16)


def mix(table, parts):
    tile = 1024
    return pl.pallas_call(
        mix_kernel,
        grid=(D // tile,),
        in_specs=[
            pl.BlockSpec(table.shape, lambda i: (0, 0)),
            pl.BlockSpec((parts.shape[0], tile), lambda i: (0, i)),
        ],
        out_specs=pl.BlockSpec((WIN, tile), lambda i: (0, i)),
        out_shape=jax.ShapeDtypeStruct((WIN, D), bf16),
        compiler_params=params(),
        name="mix",
    )(table, parts)


def per_device(
    queries,
    kv_cache,
    kv_scale,
    block_mask,
    resid,
    w_out,
    norm_gain,
    expert_ids,
    gate_weights,
    w_gate,
    w_up,
    w_down,
):
    y_pos = lax.axis_index("y")
    z_pos = lax.axis_index("z")

    blocks = CTX_LOCAL // BLOCK
    spread = kv_scale[0].reshape(blocks, 2, KV_HEADS).transpose(2, 1, 0)
    raw = kv_cache[0].reshape(blocks, BLOCK, 2, KV_HEADS, HEAD_DIM).transpose(3, 2, 0, 1, 4)
    keyvals = (raw.astype(f32) * spread[:, :, :, None, None]).astype(bf16)
    keyvals = keyvals.reshape(KV_HEADS, 2, CTX_LOCAL, HEAD_DIM)
    keyvals = lax.all_to_all(keyvals, "y", 0, 0, tiled=True)
    queries_mine = lax.all_to_all(
        jnp.broadcast_to(queries, (N_Z,) + queries.shape[1:]), "z", 0, 0, tiled=True
    )

    mask = block_mask[0, 0].reshape(N_Y, N_Z, blocks)
    mask = lax.dynamic_slice_in_dim(mask, z_pos, 1, 1)[:, 0]
    bias = jnp.where(mask == 1, 0.0, MASKED).astype(f32)
    bias = jnp.repeat(bias, BLOCK, axis=1)[:, None, :]
    place = jnp.arange(BLOCK, dtype=jnp.int32)
    later = (place[None, :] > place[:, None]) & (z_pos == N_Z - 1)
    causal = jnp.where(later, MASKED, 0.0).astype(f32)
    causal = jnp.concatenate([causal, causal], axis=0)

    w_cols = w_out.reshape(2 * HEAD_DIM, N_Z, COLS).transpose(1, 0, 2)
    w_cols = lax.all_to_all(w_cols, "z", 0, 0, tiled=True)
    resid_cols = resid[0].reshape(-1, N_Z, COLS).transpose(1, 0, 2)
    resid_cols = lax.all_to_all(resid_cols, "z", 0, 0, tiled=True).reshape(-1, COLS)
    rows = WIN // N_Y
    resid_rows = lax.dynamic_update_slice_in_dim(
        jnp.zeros((WIN, COLS), bf16), resid_cols, y_pos * rows, 0
    )

    owners = jnp.arange(N_GRP, dtype=jnp.int32) * E_SUB + y_pos
    matches = expert_ids[0][None, :, :] == owners[:, None, None]
    chosen = jnp.any(matches, axis=-1)
    weight = jnp.sum(jnp.where(matches, gate_weights[0][None, :, :], 0.0), axis=-1)
    slot = jnp.cumsum(chosen.astype(jnp.int32), axis=1) - 1
    in_slot = chosen[:, None, :] & (
        slot[:, None, :] == jnp.arange(CAP, dtype=jnp.int32)[None, :, None]
    )
    out_table = in_slot.astype(bf16).reshape(N_GRP * CAP, WIN)
    back_table = jnp.where(in_slot, weight[:, None, :], 0.0).astype(bf16)
    back_table = back_table.reshape(N_GRP * CAP, WIN).T

    parts = attention(queries_mine, keyvals, bias, causal)
    parts = lax.all_to_all(parts, "z", 0, 0, tiled=True)
    attended = lax.all_to_all(combine(parts), "z", 0, 0, tiled=True)
    projected = lax.all_to_all(project(attended, w_cols, resid_rows), "y", 0, 0, tiled=True)
    stream, outgoing = dispatch(projected, out_table)

    arrivals = lax.all_to_all(
        outgoing.reshape(N_GRP, CAP, COLS), ("x", "c"), 0, 0, tiled=True
    ).reshape(N_GRP * CAP, COLS)
    arrivals = lax.all_gather(arrivals, "z", axis=0, tiled=False)
    pieces = experts(arrivals, norm_gain[None], w_gate[0], w_up[0], w_down[0])
    returned = lax.all_to_all(
        pieces.reshape(N_GRP, CAP, D), ("x", "c"), 0, 0, tiled=True
    ).reshape(N_GRP * CAP, D)
    mixture = mix(back_table, returned).reshape(N_Y, rows, D)

    mixture = lax.all_to_all(mixture, "y", 0, 0, tiled=True)
    mixture = jnp.sum(mixture.astype(f32), axis=0).astype(bf16).reshape(N_Z, -1, D)
    mixture = lax.all_to_all(mixture, "z", 0, 0, tiled=True)
    mixture = jnp.sum(mixture.astype(f32), axis=0)
    stream_rows = lax.dynamic_slice_in_dim(stream, y_pos * rows, rows, 0)
    stream_rows = lax.all_to_all(
        stream_rows.reshape(N_Z, -1, COLS), "z", 0, 0, tiled=True
    )
    stream_rows = stream_rows.transpose(1, 0, 2).reshape(-1, D)
    return (stream_rows.astype(f32) + mixture).astype(bf16)[None]


def solution(mesh):
    fine = Mesh(mesh.devices.reshape(N_Y, N_Z, N_X, N_C), ("y", "z", "x", "c"))
    seq, grp = ("y", "z"), ("x", "c")
    in_specs = (
        P(grp, None, seq),
        P(grp, seq, None),
        P(grp, seq, None),
        P(grp, None, None),
        P(grp, seq, None),
        P(seq, None),
        P(),
        P(grp, None, None),
        P(grp, None, None),
        P(grp, seq, None),
        P(grp, seq, None),
        P(grp, seq, None),
    )
    return jax.shard_map(
        per_device, mesh=fine, in_specs=in_specs, out_specs=P(grp, seq, None), check_vma=False
    )
```

```python
import math

import jax
import jax.numpy as jnp
from jax import lax
from jax.experimental import pallas as pl
from jax.experimental.pallas import tpu as pltpu
from jax.sharding import Mesh
from jax.sharding import PartitionSpec as P

HEADS = 64
KV_HEADS = 4
HEAD_DIM = 128
BLOCK = 128
E_SUB = 4
CAP = 64
N_Y, N_Z, N_X, N_C = 4, 8, 4, 2
N_GRP = N_X * N_C
WIN = 128
D = 4096
COLS = D // N_Z
CTX_LOCAL = 1024
HIDDEN = 192
STAT_ROWS = 16
MASKED = -1e30
SCALE2 = math.log2(math.e) / math.sqrt(HEAD_DIM)
VMEM = 56 * 1024 * 1024

f32 = jnp.float32
bf16 = jnp.bfloat16


def params():
    return pltpu.CompilerParams(vmem_limit_bytes=VMEM)


def dequantize_kernel(y_ref, scale_ref, cache_ref, *out_refs):
    step = pl.program_id(0)
    for d, out_ref in enumerate(out_refs):
        head = lax.rem(y_ref[0] + d, N_Y)
        for part in range(2):
            column = part * KV_HEADS + head
            lanes = pl.ds(pl.multiple_of(column * HEAD_DIM, HEAD_DIM), HEAD_DIM)
            for b in range(2):
                rows = slice(b * BLOCK, (b + 1) * BLOCK)
                raw = cache_ref[rows, lanes].astype(f32)
                out_ref[part, rows, :] = (raw * scale_ref[2 * step + b, column]).astype(bf16)


def dequantize(y_pos, scale, cache):
    shape = jax.ShapeDtypeStruct((2, CTX_LOCAL, HEAD_DIM), bf16)
    return pl.pallas_call(
        dequantize_kernel,
        grid_spec=pltpu.PrefetchScalarGridSpec(
            num_scalar_prefetch=2,
            grid=(CTX_LOCAL // (2 * BLOCK),),
            in_specs=[pl.BlockSpec((2 * BLOCK, 2 * KV_HEADS * HEAD_DIM), lambda i, *_: (i, 0))],
            out_specs=[pl.BlockSpec((2, 2 * BLOCK, HEAD_DIM), lambda i, *_: (0, i, 0))] * N_Y,
        ),
        out_shape=[shape] * N_Y,
        compiler_params=params(),
        cost_estimate=pl.CostEstimate(flops=1 << 20, bytes_accessed=4 << 20, transcendentals=0),
        name="dequantize",
    )(y_pos, scale, cache)


def attend_chunks(q_ref, kv_refs, bias_ref, last_ref, s_ref, order):
    q_pair = jnp.concatenate([q_ref[0, :, :HEAD_DIM], q_ref[0, :, HEAD_DIM:]], axis=0)
    peak = jnp.full((2 * WIN, BLOCK), -jnp.inf, f32)
    row = lax.broadcasted_iota(jnp.int32, (2 * WIN, BLOCK), 0)
    row = jnp.where(row >= WIN, row - WIN, row)
    later = lax.broadcasted_iota(jnp.int32, (2 * WIN, BLOCK), 1) > row
    for i, (kv_ref, d) in enumerate(zip(kv_refs, order)):
        s = lax.dot_general(
            q_pair, kv_ref[0], (((1,), (1,)), ((), ())), preferred_element_type=f32
        )
        s = s + bias_ref[d]
        cut = jnp.where(later & (last_ref[d] == 1), MASKED, 0.0)
        end = CTX_LOCAL - BLOCK
        s_ref[:, i * CTX_LOCAL : i * CTX_LOCAL + end] = s[:, :end]
        tail = s[:, end:] + cut
        s_ref[:, i * CTX_LOCAL + end : (i + 1) * CTX_LOCAL] = tail
        for b in range(CTX_LOCAL // BLOCK - 1):
            peak = jnp.maximum(peak, s[:, b * BLOCK : (b + 1) * BLOCK])
        peak = jnp.maximum(peak, tail)
    return jnp.max(peak, axis=1, keepdims=True)


def weigh_chunks(kv_refs, s_ref, m):
    total = jnp.zeros((2 * WIN, BLOCK), f32)
    acc = jnp.zeros((2 * WIN, HEAD_DIM), f32)
    for i, kv_ref in enumerate(kv_refs):
        s = s_ref[:, i * CTX_LOCAL : (i + 1) * CTX_LOCAL]
        p = jnp.exp2((s - m) * SCALE2)
        for b in range(CTX_LOCAL // BLOCK):
            total = total + p[:, b * BLOCK : (b + 1) * BLOCK]
        acc = acc + jnp.dot(p.astype(bf16), kv_ref[1], preferred_element_type=f32)
    return jnp.sum(total, axis=1, keepdims=True), acc


def near_kernel(last_ref, q_ref, bias_ref, kv0, kv1, kv3, acc_ref, stat_ref, s_ref):
    kv_refs = (kv0, kv1, kv3)
    m = attend_chunks(q_ref, kv_refs, bias_ref, last_ref, s_ref, (0, 1, 3))
    l, acc = weigh_chunks(kv_refs, s_ref, m)
    acc_ref[0] = acc
    lane = lax.broadcasted_iota(jnp.int32, (2 * WIN, 128), 1)
    stat_ref[0] = jnp.where(lane == 0, m, l)


def far_kernel(last_ref, q_ref, bias_ref, kv2, acc_ref, stat_ref, out_ref, s_ref):
    m = attend_chunks(q_ref, (kv2,), bias_ref, last_ref, s_ref, (2,))
    before = stat_ref[0, :, :1]
    m = jnp.maximum(m, before)
    l, acc = weigh_chunks((kv2,), s_ref, m)
    keep = jnp.exp2((before - m) * SCALE2)
    l = l + stat_ref[0, :, 1:2] * keep
    out_ref[0, : 2 * WIN, :] = (acc + acc_ref[0] * keep).astype(bf16)
    lane = lax.broadcasted_iota(jnp.int32, (2 * WIN, 128), 1)
    stats = jnp.zeros((2 * WIN, 128), f32)
    for i, value in enumerate((m, l)):
        rest = value
        for j in range(3):
            term = rest.astype(bf16).astype(f32)
            rest = rest - term
            stats = jnp.where(lane == i + 2 * j, term, stats)
    rows = jnp.transpose(stats)
    out_ref[0, 2 * WIN :, :] = jnp.concatenate([rows[:8, :WIN], rows[:8, WIN:]], axis=0).astype(
        bf16
    )


def attention_specs(extra, outs, chunks):
    whole = pl.BlockSpec((2, CTX_LOCAL, HEAD_DIM), lambda i, *_: (0, 0, 0))
    return pltpu.PrefetchScalarGridSpec(
        num_scalar_prefetch=1,
        grid=(N_Z,),
        in_specs=[
            pl.BlockSpec((1, WIN, 2 * HEAD_DIM), lambda i, *_: (i, 0, 0)),
            pl.BlockSpec((N_Y, 1, CTX_LOCAL), lambda i, *_: (0, 0, 0)),
        ]
        + [whole] * chunks
        + [pl.BlockSpec((1,) + e, lambda i, *_: (i, 0, 0)) for e in extra],
        out_specs=[pl.BlockSpec((1,) + o, lambda i, *_: (i, 0, 0)) for o in outs],
        scratch_shapes=[pltpu.VMEM((2 * WIN, chunks * CTX_LOCAL), f32)],
    )


def near_attention(last, queries, bias, kv0, kv1, kv3):
    square = (2 * WIN, HEAD_DIM)
    return pl.pallas_call(
        near_kernel,
        grid_spec=attention_specs([], [square, square], 3),
        out_shape=[jax.ShapeDtypeStruct((N_Z,) + square, f32)] * 2,
        compiler_params=params(),
        cost_estimate=pl.CostEstimate(
            flops=8 << 30, bytes_accessed=8 << 20, transcendentals=6 << 20
        ),
        name="near_attention",
    )(last, queries, bias, kv0, kv1, kv3)


def far_attention(last, queries, bias, kv2, acc, stat):
    square = (2 * WIN, HEAD_DIM)
    message = (2 * WIN + STAT_ROWS, HEAD_DIM)
    return pl.pallas_call(
        far_kernel,
        grid_spec=attention_specs([square, square], [message], 1),
        out_shape=[jax.ShapeDtypeStruct((N_Z,) + message, bf16)],
        compiler_params=params(),
        cost_estimate=pl.CostEstimate(
            flops=3 << 30, bytes_accessed=8 << 20, transcendentals=2 << 20
        ),
        name="far_attention",
    )(last, queries, bias, kv2, acc, stat)[0]


def combine_kernel(in_ref, out_ref):
    stats = in_ref[:, 2 * WIN :, :].astype(f32)
    for head in range(2):
        st = stats[:, 8 * head : 8 * head + 8]
        m = st[:, 0] + st[:, 2] + st[:, 4]
        l = st[:, 1] + st[:, 3] + st[:, 5]
        w = jnp.exp2((m - jnp.max(m, axis=0, keepdims=True)) * SCALE2)
        w = w / jnp.sum(w * l, axis=0, keepdims=True)
        wide = jnp.concatenate([w, jnp.zeros((WIN - N_Z, WIN), f32)], axis=0)
        cols = jnp.transpose(wide)
        total = jnp.zeros((WIN, HEAD_DIM), f32)
        for z in range(N_Z):
            part = in_ref[z, head * WIN : (head + 1) * WIN, :].astype(f32)
            total = total + part * cols[:, z : z + 1]
        done = total.astype(bf16)
        for z in range(N_Z):
            out_ref[z, :, head * HEAD_DIM : (head + 1) * HEAD_DIM] = done


def combine(parts):
    return pl.pallas_call(
        combine_kernel,
        out_shape=jax.ShapeDtypeStruct((N_Z, WIN, 2 * HEAD_DIM), bf16),
        compiler_params=params(),
        name="combine",
    )(parts)


def project_kernel(a_ref, w_ref, resid_ref, out_ref):
    acc = resid_ref[...].astype(f32)
    for z in range(N_Z):
        w_rows = jnp.concatenate([w_ref[g, z] for g in range(N_GRP)], axis=0)
        acc = acc + jnp.dot(a_ref[z], w_rows, preferred_element_type=f32)
    done = acc.astype(bf16)
    for y in range(N_Y):
        out_ref[y] = done


def project(attended, w_cols, resid_rows):
    return pl.pallas_call(
        project_kernel,
        out_shape=jax.ShapeDtypeStruct((N_Y, WIN, COLS), bf16),
        compiler_params=params(),
        name="project",
    )(attended, w_cols, resid_rows)


def dispatch_kernel(parts_ref, table_ref, stream_ref, out_ref):
    total = parts_ref[0].astype(f32)
    for y in range(1, N_Y):
        total = total + parts_ref[y].astype(f32)
    stream = total.astype(bf16)
    stream_ref[...] = stream
    out_ref[...] = jnp.dot(table_ref[...], stream, preferred_element_type=f32).astype(bf16)


def dispatch(parts, table):
    return pl.pallas_call(
        dispatch_kernel,
        out_shape=(
            jax.ShapeDtypeStruct((WIN, COLS), bf16),
            jax.ShapeDtypeStruct((N_GRP * CAP, COLS), bf16),
        ),
        compiler_params=params(),
        name="dispatch",
    )(parts, table)


def experts_kernel(x_ref, gain_ref, wg_ref, wu_ref, wd_ref, out_ref):
    tokens = x_ref.shape[1]
    squares = jnp.zeros((tokens, COLS), f32)
    for z in range(N_Z):
        wide = x_ref[z].astype(f32)
        squares = squares + wide * wide
    factor = lax.rsqrt(jnp.sum(squares, axis=1, keepdims=True) * (1.0 / D) + 1e-06)
    gate = jnp.zeros((tokens, HIDDEN), f32)
    up = jnp.zeros((tokens, HIDDEN), f32)
    contract = (((1,), (1,)), ((), ()))
    for z in range(N_Z):
        cols = slice(z * COLS, (z + 1) * COLS)
        normed = (x_ref[z].astype(f32) * factor * gain_ref[:, cols]).astype(bf16)
        gate = gate + lax.dot_general(
            normed, wg_ref[:, cols], contract, preferred_element_type=f32
        )
        up = up + lax.dot_general(normed, wu_ref[:, cols], contract, preferred_element_type=f32)
    hidden = (gate / (1.0 + jnp.exp(-gate)) * up).astype(bf16)
    for z in range(N_Z):
        cols = slice(z * COLS, (z + 1) * COLS)
        out_ref[:, cols] = jnp.dot(
            hidden, wd_ref[:, cols], preferred_element_type=f32
        ).astype(bf16)


def experts(x, gain, w_gate, w_up, w_down, tile=128):
    tokens = x.shape[1]
    whole = pl.BlockSpec((HIDDEN, D), lambda i: (0, 0))
    return pl.pallas_call(
        experts_kernel,
        grid=(tokens // tile,),
        in_specs=[
            pl.BlockSpec((N_Z, tile, COLS), lambda i: (0, i, 0)),
            pl.BlockSpec((1, D), lambda i: (0, 0)),
            whole,
            whole,
            whole,
        ],
        out_specs=pl.BlockSpec((tile, D), lambda i: (i, 0)),
        out_shape=jax.ShapeDtypeStruct((tokens, D), bf16),
        compiler_params=params(),
        name="experts",
    )(x, gain, w_gate, w_up, w_down)


def mix_kernel(table_ref, parts_ref, out_ref):
    out_ref[...] = jnp.dot(
        table_ref[...], parts_ref[...], preferred_element_type=f32
    ).astype(bf16)


def mix(table, parts):
    tile = 1024
    return pl.pallas_call(
        mix_kernel,
        grid=(D // tile,),
        in_specs=[
            pl.BlockSpec(table.shape, lambda i: (0, 0)),
            pl.BlockSpec((parts.shape[0], tile), lambda i: (0, i)),
        ],
        out_specs=pl.BlockSpec((WIN, tile), lambda i: (0, i)),
        out_shape=jax.ShapeDtypeStruct((WIN, D), bf16),
        compiler_params=params(),
        name="mix",
    )(table, parts)


def per_device(
    queries,
    kv_cache,
    kv_scale,
    block_mask,
    resid,
    w_out,
    norm_gain,
    expert_ids,
    gate_weights,
    w_gate,
    w_up,
    w_down,
):
    y_pos = lax.axis_index("y")
    z_pos = lax.axis_index("z")

    queries_mine = lax.all_to_all(
        jnp.broadcast_to(queries, (N_Z,) + queries.shape[1:]), "z", 0, 0, tiled=True
    )
    chunks = dequantize(y_pos[None], kv_scale[0], kv_cache[0])
    kv_own = chunks[0]
    kv_from = {
        d: lax.ppermute(chunks[d], "y", [(i, (i + d) % N_Y) for i in range(N_Y)])
        for d in (1, 3, 2)
    }

    blocks = CTX_LOCAL // BLOCK
    source = (y_pos - jnp.arange(N_Y, dtype=jnp.int32)) % N_Y
    mask = block_mask[0, 0].reshape(N_Y, N_Z, blocks)
    mask = lax.dynamic_slice_in_dim(mask, z_pos, 1, 1)[:, 0]
    mask = jnp.take(mask, source, axis=0)
    bias = jnp.where(mask == 1, 0.0, MASKED).astype(f32)
    bias = jnp.repeat(bias, BLOCK, axis=1)[:, None, :]
    last = ((source == N_Y - 1) & (z_pos == N_Z - 1)).astype(jnp.int32)

    rows = WIN // N_Y
    part = 2 * HEAD_DIM // N_GRP
    own_rows = resid.shape[1]
    grp_pos = lax.axis_index("x") * N_C + lax.axis_index("c")
    w_mine = lax.dynamic_slice_in_dim(w_out, grp_pos * part, part, 0)
    early = jnp.concatenate([w_mine, resid[0]], axis=0)
    early = early.reshape(part + own_rows, N_Z, COLS).transpose(1, 0, 2)
    early, queries_mine = lax.optimization_barrier((early, queries_mine))
    early = lax.all_to_all(early, "z", 0, 0, tiled=True)

    owners = jnp.arange(N_GRP, dtype=jnp.int32) * E_SUB + y_pos
    matches = expert_ids[0][None, :, :] == owners[:, None, None]
    chosen = jnp.any(matches, axis=-1)
    weight = jnp.sum(jnp.where(matches, gate_weights[0][None, :, :], 0.0), axis=-1)
    slot = jnp.cumsum(chosen.astype(jnp.int32), axis=1) - 1
    in_slot = chosen[:, None, :] & (
        slot[:, None, :] == jnp.arange(CAP, dtype=jnp.int32)[None, :, None]
    )
    out_table = in_slot.astype(bf16).reshape(N_GRP * CAP, WIN)
    back_table = jnp.where(in_slot, weight[:, None, :], 0.0).astype(bf16)
    back_table = back_table.reshape(N_GRP * CAP, WIN).T

    acc, stat = near_attention(last, queries_mine, bias, kv_own, kv_from[1], kv_from[3])
    parts = far_attention(last, queries_mine, bias, kv_from[2], acc, stat)
    parts, early = lax.optimization_barrier((parts, early))
    resid_rows = lax.dynamic_update_slice_in_dim(
        jnp.zeros((WIN, COLS), bf16), early[:, part:].reshape(rows, COLS), y_pos * rows, 0
    )
    w_cols = lax.all_gather(early[:, :part], ("x", "c"), axis=0, tiled=False)
    parts = lax.all_to_all(parts, "z", 0, 0, tiled=True)
    attended = lax.all_to_all(combine(parts), "z", 0, 0, tiled=True)
    projected = lax.all_to_all(project(attended, w_cols, resid_rows), "y", 0, 0, tiled=True)
    stream, outgoing = dispatch(projected, out_table)

    arrivals = lax.all_to_all(
        outgoing.reshape(N_GRP, CAP, COLS), ("x", "c"), 0, 0, tiled=True
    ).reshape(N_GRP * CAP, COLS)
    arrivals = lax.all_gather(arrivals, "z", axis=0, tiled=False)
    pieces = experts(arrivals, norm_gain[None], w_gate[0], w_up[0], w_down[0])
    returned = lax.all_to_all(
        pieces.reshape(N_GRP, CAP, D), ("x", "c"), 0, 0, tiled=True
    ).reshape(N_GRP * CAP, D)
    mixture = mix(back_table, returned).reshape(N_Y, rows, D)

    stream_rows = lax.dynamic_slice_in_dim(stream, y_pos * rows, rows, 0)
    stream_rows = lax.dynamic_update_slice_in_dim(
        jnp.zeros((rows, D), bf16), stream_rows, z_pos * COLS, 1
    )
    mixture = lax.all_to_all(mixture, "y", 0, 0, tiled=True)
    mixture = jnp.sum(mixture.astype(f32), axis=0) + stream_rows.astype(f32)
    mixture = lax.all_to_all(mixture.astype(bf16).reshape(N_Z, -1, D), "z", 0, 0, tiled=True)
    return jnp.sum(mixture.astype(f32), axis=0).astype(bf16)[None]


def solution(mesh):
    fine = Mesh(mesh.devices.reshape(N_Y, N_Z, N_X, N_C), ("y", "z", "x", "c"))
    seq, grp = ("y", "z"), ("x", "c")
    in_specs = (
        P(grp, None, seq),
        P(grp, seq, None),
        P(grp, seq, None),
        P(grp, None, None),
        P(grp, seq, None),
        P(seq, None),
        P(),
        P(grp, None, None),
        P(grp, None, None),
        P(grp, seq, None),
        P(grp, seq, None),
        P(grp, seq, None),
    )
    return jax.shard_map(
        per_device, mesh=fine, in_specs=in_specs, out_specs=P(grp, seq, None), check_vma=False
    )
```

```python
import math

import jax
import jax.numpy as jnp
from jax import lax
from jax.experimental import pallas as pl
from jax.experimental.pallas import tpu as pltpu
from jax.sharding import Mesh
from jax.sharding import PartitionSpec as P

HEADS = 64
KV_HEADS = 4
HEAD_DIM = 128
BLOCK = 128
E_SUB = 4
CAP = 64
N_Y, N_Z, N_X, N_C = 4, 8, 4, 2
N_GRP = N_X * N_C
WIN = 128
D = 4096
COLS = D // N_Z
HALF = COLS // 2
CTX_LOCAL = 1024
HIDDEN = 192
STAT_ROWS = 16
MASKED = -1e30
SCALE2 = math.log2(math.e) / math.sqrt(HEAD_DIM)
VMEM = 56 * 1024 * 1024

f32 = jnp.float32
bf16 = jnp.bfloat16


def params():
    return pltpu.CompilerParams(vmem_limit_bytes=VMEM)


def dequantize_kernel(y_ref, scale_ref, cache_ref, *out_refs):
    step = pl.program_id(0)
    for d, out_ref in enumerate(out_refs):
        head = lax.rem(y_ref[0] + d, N_Y)
        for part in range(2):
            column = part * KV_HEADS + head
            lanes = pl.ds(pl.multiple_of(column * HEAD_DIM, HEAD_DIM), HEAD_DIM)
            for b in range(2):
                rows = slice(b * BLOCK, (b + 1) * BLOCK)
                raw = cache_ref[rows, lanes].astype(f32)
                out_ref[part, rows, :] = (raw * scale_ref[2 * step + b, column]).astype(bf16)


def dequantize(y_pos, scale, cache):
    shape = jax.ShapeDtypeStruct((2, CTX_LOCAL, HEAD_DIM), bf16)
    return pl.pallas_call(
        dequantize_kernel,
        grid_spec=pltpu.PrefetchScalarGridSpec(
            num_scalar_prefetch=2,
            grid=(CTX_LOCAL // (2 * BLOCK),),
            in_specs=[pl.BlockSpec((2 * BLOCK, 2 * KV_HEADS * HEAD_DIM), lambda i, *_: (i, 0))],
            out_specs=[pl.BlockSpec((2, 2 * BLOCK, HEAD_DIM), lambda i, *_: (0, i, 0))] * N_Y,
        ),
        out_shape=[shape] * N_Y,
        compiler_params=params(),
        cost_estimate=pl.CostEstimate(flops=1 << 20, bytes_accessed=4 << 20, transcendentals=0),
        name="dequantize",
    )(y_pos, scale, cache)


def attend_chunks(q_ref, kv_refs, bias_ref, last_ref, s_ref, order):
    q_pair = jnp.concatenate([q_ref[0, :, :HEAD_DIM], q_ref[0, :, HEAD_DIM:]], axis=0)
    peak = jnp.full((2 * WIN, BLOCK), -jnp.inf, f32)
    row = lax.broadcasted_iota(jnp.int32, (2 * WIN, BLOCK), 0)
    row = jnp.where(row >= WIN, row - WIN, row)
    later = lax.broadcasted_iota(jnp.int32, (2 * WIN, BLOCK), 1) > row
    for i, (kv_ref, d) in enumerate(zip(kv_refs, order)):
        s = lax.dot_general(
            q_pair, kv_ref[0], (((1,), (1,)), ((), ())), preferred_element_type=f32
        )
        s = s + bias_ref[d]
        cut = jnp.where(later & (last_ref[d] == 1), MASKED, 0.0)
        end = CTX_LOCAL - BLOCK
        s_ref[:, i * CTX_LOCAL : i * CTX_LOCAL + end] = s[:, :end]
        tail = s[:, end:] + cut
        s_ref[:, i * CTX_LOCAL + end : (i + 1) * CTX_LOCAL] = tail
        for b in range(CTX_LOCAL // BLOCK - 1):
            peak = jnp.maximum(peak, s[:, b * BLOCK : (b + 1) * BLOCK])
        peak = jnp.maximum(peak, tail)
    return jnp.max(peak, axis=1, keepdims=True)


def weigh_chunks(kv_refs, s_ref, m):
    total = jnp.zeros((2 * WIN, BLOCK), f32)
    acc = jnp.zeros((2 * WIN, HEAD_DIM), f32)
    for i, kv_ref in enumerate(kv_refs):
        s = s_ref[:, i * CTX_LOCAL : (i + 1) * CTX_LOCAL]
        p = jnp.exp2((s - m) * SCALE2)
        for b in range(CTX_LOCAL // BLOCK):
            total = total + p[:, b * BLOCK : (b + 1) * BLOCK]
        acc = acc + jnp.dot(p.astype(bf16), kv_ref[1], preferred_element_type=f32)
    return jnp.sum(total, axis=1, keepdims=True), acc


def near_kernel(last_ref, q_ref, bias_ref, kv0, kv1, kv3, acc_ref, stat_ref, s_ref):
    kv_refs = (kv0, kv1, kv3)
    m = attend_chunks(q_ref, kv_refs, bias_ref, last_ref, s_ref, (0, 1, 3))
    l, acc = weigh_chunks(kv_refs, s_ref, m)
    acc_ref[0] = acc
    lane = lax.broadcasted_iota(jnp.int32, (2 * WIN, 128), 1)
    stat_ref[0] = jnp.where(lane == 0, m, l)


def far_kernel(last_ref, q_ref, bias_ref, kv2, acc_ref, stat_ref, out_ref, s_ref):
    m = attend_chunks(q_ref, (kv2,), bias_ref, last_ref, s_ref, (2,))
    before = stat_ref[0, :, :1]
    m = jnp.maximum(m, before)
    l, acc = weigh_chunks((kv2,), s_ref, m)
    keep = jnp.exp2((before - m) * SCALE2)
    l = l + stat_ref[0, :, 1:2] * keep
    out_ref[0, : 2 * WIN, :] = (acc + acc_ref[0] * keep).astype(bf16)
    lane = lax.broadcasted_iota(jnp.int32, (2 * WIN, 128), 1)
    stats = jnp.zeros((2 * WIN, 128), f32)
    for i, value in enumerate((m, l)):
        rest = value
        for j in range(3):
            term = rest.astype(bf16).astype(f32)
            rest = rest - term
            stats = jnp.where(lane == i + 2 * j, term, stats)
    rows = jnp.transpose(stats)
    out_ref[0, 2 * WIN :, :] = jnp.concatenate([rows[:8, :WIN], rows[:8, WIN:]], axis=0).astype(
        bf16
    )


def attention_specs(extra, outs, chunks):
    whole = pl.BlockSpec((2, CTX_LOCAL, HEAD_DIM), lambda i, *_: (0, 0, 0))
    return pltpu.PrefetchScalarGridSpec(
        num_scalar_prefetch=1,
        grid=(N_Z,),
        in_specs=[
            pl.BlockSpec((1, WIN, 2 * HEAD_DIM), lambda i, *_: (i, 0, 0)),
            pl.BlockSpec((N_Y, 1, CTX_LOCAL), lambda i, *_: (0, 0, 0)),
        ]
        + [whole] * chunks
        + [pl.BlockSpec((1,) + e, lambda i, *_: (i, 0, 0)) for e in extra],
        out_specs=[pl.BlockSpec((1,) + o, lambda i, *_: (i, 0, 0)) for o in outs],
        scratch_shapes=[pltpu.VMEM((2 * WIN, chunks * CTX_LOCAL), f32)],
    )


def near_attention(last, queries, bias, kv0, kv1, kv3):
    square = (2 * WIN, HEAD_DIM)
    return pl.pallas_call(
        near_kernel,
        grid_spec=attention_specs([], [square, square], 3),
        out_shape=[jax.ShapeDtypeStruct((N_Z,) + square, f32)] * 2,
        compiler_params=params(),
        cost_estimate=pl.CostEstimate(
            flops=8 << 30, bytes_accessed=8 << 20, transcendentals=6 << 20
        ),
        name="near_attention",
    )(last, queries, bias, kv0, kv1, kv3)


def far_attention(last, queries, bias, kv2, acc, stat):
    square = (2 * WIN, HEAD_DIM)
    message = (2 * WIN + STAT_ROWS, HEAD_DIM)
    return pl.pallas_call(
        far_kernel,
        grid_spec=attention_specs([square, square], [message], 1),
        out_shape=[jax.ShapeDtypeStruct((N_Z,) + message, bf16)],
        compiler_params=params(),
        cost_estimate=pl.CostEstimate(
            flops=3 << 30, bytes_accessed=8 << 20, transcendentals=2 << 20
        ),
        name="far_attention",
    )(last, queries, bias, kv2, acc, stat)[0]


def combine_kernel(in_ref, out_ref):
    stats = in_ref[:, 2 * WIN :, :].astype(f32)
    for head in range(2):
        st = stats[:, 8 * head : 8 * head + 8]
        m = st[:, 0] + st[:, 2] + st[:, 4]
        l = st[:, 1] + st[:, 3] + st[:, 5]
        w = jnp.exp2((m - jnp.max(m, axis=0, keepdims=True)) * SCALE2)
        w = w / jnp.sum(w * l, axis=0, keepdims=True)
        wide = jnp.concatenate([w, jnp.zeros((WIN - N_Z, WIN), f32)], axis=0)
        cols = jnp.transpose(wide)
        total = jnp.zeros((WIN, HEAD_DIM), f32)
        for z in range(N_Z):
            part = in_ref[z, head * WIN : (head + 1) * WIN, :].astype(f32)
            total = total + part * cols[:, z : z + 1]
        done = total.astype(bf16)
        for z in range(N_Z):
            out_ref[z, :, head * HEAD_DIM : (head + 1) * HEAD_DIM] = done


def combine(parts):
    return pl.pallas_call(
        combine_kernel,
        out_shape=jax.ShapeDtypeStruct((N_Z, WIN, 2 * HEAD_DIM), bf16),
        compiler_params=params(),
        name="combine",
    )(parts)


def project_kernel(a_ref, w_ref, resid_ref, out_ref):
    acc = resid_ref[...].astype(f32)
    for z in range(N_Z):
        w_rows = jnp.concatenate([w_ref[g, z] for g in range(N_GRP)], axis=0)
        acc = acc + jnp.dot(a_ref[z], w_rows, preferred_element_type=f32)
    done = acc.astype(bf16)
    for y in range(N_Y):
        out_ref[y] = done


def project(attended, w_cols, resid_rows):
    return pl.pallas_call(
        project_kernel,
        out_shape=jax.ShapeDtypeStruct((N_Y, WIN, COLS), bf16),
        compiler_params=params(),
        name="project",
    )(attended, w_cols, resid_rows)


def dispatch_kernel(parts_ref, table_ref, stream_ref, out_ref):
    total = parts_ref[0].astype(f32)
    for y in range(1, N_Y):
        total = total + parts_ref[y].astype(f32)
    stream = total.astype(bf16)
    stream_ref[...] = stream
    out_ref[...] = jnp.dot(table_ref[...], stream, preferred_element_type=f32).astype(bf16)


def dispatch(parts, table):
    return pl.pallas_call(
        dispatch_kernel,
        out_shape=(
            jax.ShapeDtypeStruct((WIN, COLS), bf16),
            jax.ShapeDtypeStruct((N_GRP * CAP, COLS), bf16),
        ),
        compiler_params=params(),
        name="dispatch",
    )(parts, table)


def experts_kernel(x_ref, gain_ref, wg_ref, wu_ref, wd_ref, by_z_ref, by_x_ref):
    tokens = x_ref.shape[1]
    squares = jnp.zeros((tokens, COLS), f32)
    for z in range(N_Z):
        wide = x_ref[z].astype(f32)
        squares = squares + wide * wide
    factor = lax.rsqrt(jnp.sum(squares, axis=1, keepdims=True) * (1.0 / D) + 1e-06)
    gate = jnp.zeros((tokens, HIDDEN), f32)
    up = jnp.zeros((tokens, HIDDEN), f32)
    contract = (((1,), (1,)), ((), ()))
    for z in range(N_Z):
        cols = slice(z * COLS, (z + 1) * COLS)
        normed = (x_ref[z].astype(f32) * factor * gain_ref[:, cols]).astype(bf16)
        gate = gate + lax.dot_general(
            normed, wg_ref[:, cols], contract, preferred_element_type=f32
        )
        up = up + lax.dot_general(normed, wu_ref[:, cols], contract, preferred_element_type=f32)
    hidden = (gate / (1.0 + jnp.exp(-gate)) * up).astype(bf16)
    for z in range(N_Z):
        cols = slice(z * COLS, (z + 1) * COLS)
        done = jnp.dot(hidden, wd_ref[:, cols], preferred_element_type=f32).astype(bf16)
        by_z_ref[z] = done[:, :HALF]
        by_x_ref[:, z * HALF : (z + 1) * HALF] = done[:, HALF:]


def experts(x, gain, w_gate, w_up, w_down, tile=128):
    tokens = x.shape[1]
    whole = pl.BlockSpec((HIDDEN, D), lambda i: (0, 0))
    return pl.pallas_call(
        experts_kernel,
        grid=(tokens // tile,),
        in_specs=[
            pl.BlockSpec((N_Z, tile, COLS), lambda i: (0, i, 0)),
            pl.BlockSpec((1, D), lambda i: (0, 0)),
            whole,
            whole,
            whole,
        ],
        out_specs=[
            pl.BlockSpec((N_Z, tile, HALF), lambda i: (0, i, 0)),
            pl.BlockSpec((tile, D // 2), lambda i: (i, 0)),
        ],
        out_shape=[
            jax.ShapeDtypeStruct((N_Z, tokens, HALF), bf16),
            jax.ShapeDtypeStruct((tokens, D // 2), bf16),
        ],
        compiler_params=params(),
        name="experts",
    )(x, gain, w_gate, w_up, w_down)


def mix_kernel(table_ref, parts_ref, out_ref):
    out_ref[...] = jnp.dot(
        table_ref[...], parts_ref[...], preferred_element_type=f32
    ).astype(bf16)


def mix(table, parts):
    tile = 512
    return pl.pallas_call(
        mix_kernel,
        grid=(parts.shape[1] // tile,),
        in_specs=[
            pl.BlockSpec(table.shape, lambda i: (0, 0)),
            pl.BlockSpec((parts.shape[0], tile), lambda i: (0, i)),
        ],
        out_specs=pl.BlockSpec((WIN, tile), lambda i: (0, i)),
        out_shape=jax.ShapeDtypeStruct((WIN, parts.shape[1]), bf16),
        compiler_params=params(),
        cost_estimate=pl.CostEstimate(flops=1 << 28, bytes_accessed=4 << 20, transcendentals=0),
        name="mix",
    )(table, parts)


def mix_rest_kernel(table_ref, parts_ref, mixed_ref, out_ref):
    out_ref[:, : D // 2] = mixed_ref[...]
    out_ref[:, D // 2 :] = jnp.dot(
        table_ref[...], parts_ref[...], preferred_element_type=f32
    ).astype(bf16)


def mix_rest(table, parts, mixed):
    return pl.pallas_call(
        mix_rest_kernel,
        out_shape=jax.ShapeDtypeStruct((WIN, D // 2 + HALF), bf16),
        compiler_params=params(),
        name="mix_rest",
    )(table, parts, mixed)


def finish_kernel(in_ref, out_ref):
    summed = in_ref[0, :, : D // 2].astype(f32)
    for z in range(1, N_Z):
        summed = summed + in_ref[z, :, : D // 2].astype(f32)
    for z in range(N_Z):
        mine = in_ref[z, :, D // 2 :].astype(f32)
        first = mine[:, HALF : 2 * HALF] + mine[:, :HALF]
        second = mine[:, 2 * HALF :] + summed[:, z * HALF : (z + 1) * HALF]
        out_ref[:, z * COLS : z * COLS + HALF] = first.astype(bf16)
        out_ref[:, z * COLS + HALF : (z + 1) * COLS] = second.astype(bf16)


def finish(parts):
    return pl.pallas_call(
        finish_kernel,
        out_shape=jax.ShapeDtypeStruct((parts.shape[1], D), bf16),
        compiler_params=params(),
        name="finish",
    )(parts)


def per_device(
    queries,
    kv_cache,
    kv_scale,
    block_mask,
    resid,
    w_out,
    norm_gain,
    expert_ids,
    gate_weights,
    w_gate,
    w_up,
    w_down,
):
    y_pos = lax.axis_index("y")
    z_pos = lax.axis_index("z")

    chunks = dequantize(y_pos[None], kv_scale[0], kv_cache[0])
    kv_own, queries = lax.optimization_barrier((chunks[0], queries))
    queries_mine = lax.all_to_all(
        jnp.broadcast_to(queries, (N_Z,) + queries.shape[1:]), "z", 0, 0, tiled=True
    )
    kv_from = {
        d: lax.ppermute(chunks[d], "y", [(i, (i + d) % N_Y) for i in range(N_Y)])
        for d in (1, 3, 2)
    }

    blocks = CTX_LOCAL // BLOCK
    source = (y_pos - jnp.arange(N_Y, dtype=jnp.int32)) % N_Y
    mask = block_mask[0, 0].reshape(N_Y, N_Z, blocks)
    mask = lax.dynamic_slice_in_dim(mask, z_pos, 1, 1)[:, 0]
    mask = jnp.take(mask, source, axis=0)
    bias = jnp.where(mask == 1, 0.0, MASKED).astype(f32)
    bias = jnp.repeat(bias, BLOCK, axis=1)[:, None, :]
    last = ((source == N_Y - 1) & (z_pos == N_Z - 1)).astype(jnp.int32)

    rows = WIN // N_Y
    part = 2 * HEAD_DIM // N_GRP
    own_rows = resid.shape[1]
    grp_pos = lax.axis_index("x") * N_C + lax.axis_index("c")
    w_mine = lax.dynamic_slice_in_dim(w_out, grp_pos * part, part, 0)
    early = jnp.concatenate([w_mine, resid[0]], axis=0)
    early = early.reshape(part + own_rows, N_Z, COLS).transpose(1, 0, 2)
    early, queries_mine = lax.optimization_barrier((early, queries_mine))
    early = lax.all_to_all(early, "z", 0, 0, tiled=True)

    owners = jnp.arange(N_GRP, dtype=jnp.int32) * E_SUB + y_pos
    matches = expert_ids[0][None, :, :] == owners[:, None, None]
    chosen = jnp.any(matches, axis=-1)
    weight = jnp.sum(jnp.where(matches, gate_weights[0][None, :, :], 0.0), axis=-1)
    slot = jnp.cumsum(chosen.astype(jnp.int32), axis=1) - 1
    in_slot = chosen[:, None, :] & (
        slot[:, None, :] == jnp.arange(CAP, dtype=jnp.int32)[None, :, None]
    )
    out_table = in_slot.astype(bf16).reshape(N_GRP * CAP, WIN)
    back_table = jnp.where(in_slot, weight[:, None, :], 0.0).astype(bf16)
    back_table = back_table.reshape(N_GRP * CAP, WIN).T

    acc, stat = near_attention(last, queries_mine, bias, kv_own, kv_from[1], kv_from[3])
    parts = far_attention(last, queries_mine, bias, kv_from[2], acc, stat)
    parts, early = lax.optimization_barrier((parts, early))
    resid_rows = lax.dynamic_update_slice_in_dim(
        jnp.zeros((WIN, COLS), bf16), early[:, part:].reshape(rows, COLS), y_pos * rows, 0
    )
    w_cols = lax.all_gather(early[:, :part], ("x", "c"), axis=0, tiled=False)
    parts = lax.all_to_all(parts, "z", 0, 0, tiled=True)
    attended = lax.all_to_all(combine(parts), "z", 0, 0, tiled=True)
    projected = lax.all_to_all(project(attended, w_cols, resid_rows), "y", 0, 0, tiled=True)
    stream, outgoing = dispatch(projected, out_table)

    arrivals = lax.all_to_all(
        outgoing.reshape(N_GRP, CAP, COLS), ("x", "c"), 0, 0, tiled=True
    ).reshape(N_GRP * CAP, COLS)
    arrivals = lax.all_gather(arrivals, "z", axis=0, tiled=False)
    by_z, by_x = experts(arrivals, norm_gain[None], w_gate[0], w_up[0], w_down[0])
    by_z = lax.psum_scatter(
        by_z.reshape(N_Z * N_GRP * CAP, HALF), "z", scatter_dimension=0, tiled=True
    )
    by_x = lax.all_to_all(
        by_x.reshape(N_GRP, CAP, D // 2), ("x", "c"), 0, 0, tiled=True
    ).reshape(N_GRP * CAP, D // 2)
    mixed = mix(back_table, by_x)
    by_z, by_x = lax.optimization_barrier((by_z, by_x))
    by_z = lax.all_to_all(
        by_z.reshape(N_GRP, CAP, HALF), ("x", "c"), 0, 0, tiled=True
    ).reshape(N_GRP * CAP, HALF)
    mixture = mix_rest(back_table, by_z, mixed).reshape(N_Y, rows, -1)

    stream_rows = lax.dynamic_slice_in_dim(stream, y_pos * rows, rows, 0)
    mixture = lax.all_to_all(mixture, "y", 0, 0, tiled=True)
    mixture = jnp.sum(mixture.astype(f32), axis=0).astype(bf16)
    tail = jnp.concatenate([mixture, stream_rows], axis=1).reshape(N_Z, own_rows, -1)
    return finish(lax.all_to_all(tail, "z", 0, 0, tiled=True))[None]


def solution(mesh):
    fine = Mesh(mesh.devices.reshape(N_Y, N_Z, N_X, N_C), ("y", "z", "x", "c"))
    seq, grp = ("y", "z"), ("x", "c")
    in_specs = (
        P(grp, None, seq),
        P(grp, seq, None),
        P(grp, seq, None),
        P(grp, None, None),
        P(grp, seq, None),
        P(seq, None),
        P(),
        P(grp, None, None),
        P(grp, None, None),
        P(grp, seq, None),
        P(grp, seq, None),
        P(grp, seq, None),
    )
    return jax.shard_map(
        per_device, mesh=fine, in_specs=in_specs, out_specs=P(grp, seq, None), check_vma=False
    )
```

```python
import math

import jax
import jax.numpy as jnp
from jax import lax
from jax.experimental import pallas as pl
from jax.experimental.pallas import tpu as pltpu
from jax.sharding import Mesh
from jax.sharding import PartitionSpec as P

HEADS = 64
KV_HEADS = 4
HEAD_DIM = 128
BLOCK = 128
E_SUB = 4
CAP = 64
N_Y, N_Z, N_X, N_C = 4, 8, 4, 2
N_GRP = N_X * N_C
WIN = 128
D = 4096
COLS = D // N_Z
HALF = COLS // 2
CTX_LOCAL = 1024
HIDDEN = 192
STAT_ROWS = 16
PAIRS = 2
MASKED = -1e30
SCALE2 = math.log2(math.e) / math.sqrt(HEAD_DIM)
VMEM = 56 * 1024 * 1024

f32 = jnp.float32
bf16 = jnp.bfloat16


def params():
    return pltpu.CompilerParams(vmem_limit_bytes=VMEM)


def dequantize_kernel(y_ref, scale_ref, cache_ref, *out_refs):
    step = pl.program_id(0)
    for d, out_ref in enumerate(out_refs):
        head = lax.rem(y_ref[0] + d, N_Y)
        for part in range(2):
            column = part * KV_HEADS + head
            lanes = pl.ds(pl.multiple_of(column * HEAD_DIM, HEAD_DIM), HEAD_DIM)
            for b in range(2):
                rows = slice(b * BLOCK, (b + 1) * BLOCK)
                raw = cache_ref[rows, lanes].astype(f32)
                out_ref[part, rows, :] = (raw * scale_ref[2 * step + b, column]).astype(bf16)


def dequantize(y_pos, scale, cache):
    shape = jax.ShapeDtypeStruct((2, CTX_LOCAL, HEAD_DIM), bf16)
    return pl.pallas_call(
        dequantize_kernel,
        grid_spec=pltpu.PrefetchScalarGridSpec(
            num_scalar_prefetch=2,
            grid=(CTX_LOCAL // (2 * BLOCK),),
            in_specs=[pl.BlockSpec((2 * BLOCK, 2 * KV_HEADS * HEAD_DIM), lambda i, *_: (i, 0))],
            out_specs=[pl.BlockSpec((2, 2 * BLOCK, HEAD_DIM), lambda i, *_: (0, i, 0))] * N_Y,
        ),
        out_shape=[shape] * N_Y,
        compiler_params=params(),
        cost_estimate=pl.CostEstimate(flops=1 << 20, bytes_accessed=4 << 20, transcendentals=0),
        name="dequantize",
    )(y_pos, scale, cache)


def attend_chunks(q_ref, kv_refs, bias_ref, last_ref, s_ref, pair, order):
    q_pair = jnp.concatenate([q_ref[pair, :, :HEAD_DIM], q_ref[pair, :, HEAD_DIM:]], axis=0)
    peak = jnp.full((2 * WIN, BLOCK), -jnp.inf, f32)
    row = lax.broadcasted_iota(jnp.int32, (2 * WIN, BLOCK), 0)
    row = jnp.where(row >= WIN, row - WIN, row)
    later = lax.broadcasted_iota(jnp.int32, (2 * WIN, BLOCK), 1) > row
    for i, (kv_ref, d) in enumerate(zip(kv_refs, order)):
        s = lax.dot_general(
            q_pair, kv_ref[0], (((1,), (1,)), ((), ())), preferred_element_type=f32
        )
        s = s + bias_ref[d]
        cut = jnp.where(later & (last_ref[d] == 1), MASKED, 0.0)
        end = CTX_LOCAL - BLOCK
        s_ref[pair, :, i * CTX_LOCAL : i * CTX_LOCAL + end] = s[:, :end]
        tail = s[:, end:] + cut
        s_ref[pair, :, i * CTX_LOCAL + end : (i + 1) * CTX_LOCAL] = tail
        for b in range(CTX_LOCAL // BLOCK - 1):
            peak = jnp.maximum(peak, s[:, b * BLOCK : (b + 1) * BLOCK])
        peak = jnp.maximum(peak, tail)
    return jnp.max(peak, axis=1, keepdims=True)


def weigh_chunks(kv_refs, s_ref, pair, m):
    total = jnp.zeros((2 * WIN, BLOCK), f32)
    acc = jnp.zeros((2 * WIN, HEAD_DIM), f32)
    for i, kv_ref in enumerate(kv_refs):
        s = s_ref[pair, :, i * CTX_LOCAL : (i + 1) * CTX_LOCAL]
        p = jnp.exp2((s - m) * SCALE2)
        for b in range(CTX_LOCAL // BLOCK):
            total = total + p[:, b * BLOCK : (b + 1) * BLOCK]
        acc = acc + jnp.dot(p.astype(bf16), kv_ref[1], preferred_element_type=f32)
    return jnp.sum(total, axis=1, keepdims=True), acc


def own_kernel(last_ref, q_ref, bias_ref, kv0, acc_ref, stat_ref, s_ref):
    lane = lax.broadcasted_iota(jnp.int32, (2 * WIN, 128), 1)
    maxima = [
        attend_chunks(q_ref, (kv0,), bias_ref, last_ref, s_ref, pair, (0,))
        for pair in range(PAIRS)
    ]
    for pair, m in enumerate(maxima):
        l, acc = weigh_chunks((kv0,), s_ref, pair, m)
        acc_ref[pair] = acc
        stat_ref[pair] = jnp.where(lane == 0, m, l)


def rest_kernel(last_ref, q_ref, bias_ref, kv1, kv3, kv2, acc_ref, stat_ref, out_ref, s_ref):
    kv_refs = (kv1, kv3, kv2)
    lane = lax.broadcasted_iota(jnp.int32, (2 * WIN, 128), 1)
    row = lax.broadcasted_iota(jnp.int32, (8, 2 * WIN), 0)
    maxima = [
        attend_chunks(q_ref, kv_refs, bias_ref, last_ref, s_ref, pair, (1, 3, 2))
        for pair in range(PAIRS)
    ]
    for pair, highest in enumerate(maxima):
        before = stat_ref[pair, :, :1]
        m = jnp.maximum(highest, before)
        l, acc = weigh_chunks(kv_refs, s_ref, pair, m)
        keep = jnp.exp2((before - m) * SCALE2)
        l = l + stat_ref[pair, :, 1:2] * keep
        out_ref[pair, : 2 * WIN, :] = (acc + acc_ref[pair] * keep).astype(bf16)
        turned = jnp.transpose(jnp.where(lane % 2 == 0, m, l))[:8]
        high = turned.astype(bf16).astype(f32)
        middle = (turned - high).astype(bf16).astype(f32)
        low = turned - high - middle
        rows = jnp.where(row < 2, high, jnp.where(row < 4, middle, low))
        out_ref[pair, 2 * WIN :, :] = jnp.concatenate(
            [rows[:, :WIN], rows[:, WIN:]], axis=0
        ).astype(bf16)


def attention_specs(extra, outs, chunks):
    whole = pl.BlockSpec((2, CTX_LOCAL, HEAD_DIM), lambda i, *_: (0, 0, 0))
    return pltpu.PrefetchScalarGridSpec(
        num_scalar_prefetch=1,
        grid=(N_Z // PAIRS,),
        in_specs=[
            pl.BlockSpec((PAIRS, WIN, 2 * HEAD_DIM), lambda i, *_: (i, 0, 0)),
            pl.BlockSpec((N_Y, 1, CTX_LOCAL), lambda i, *_: (0, 0, 0)),
        ]
        + [whole] * chunks
        + [pl.BlockSpec((PAIRS,) + e, lambda i, *_: (i, 0, 0)) for e in extra],
        out_specs=[pl.BlockSpec((PAIRS,) + o, lambda i, *_: (i, 0, 0)) for o in outs],
        scratch_shapes=[pltpu.VMEM((PAIRS, 2 * WIN, chunks * CTX_LOCAL), f32)],
    )


def own_attention(last, queries, bias, kv0):
    square = (2 * WIN, HEAD_DIM)
    return pl.pallas_call(
        own_kernel,
        grid_spec=attention_specs([], [square, square], 1),
        out_shape=[jax.ShapeDtypeStruct((N_Z,) + square, f32)] * 2,
        compiler_params=params(),
        cost_estimate=pl.CostEstimate(
            flops=3 << 30, bytes_accessed=8 << 20, transcendentals=2 << 20
        ),
        name="own_attention",
    )(last, queries, bias, kv0)


def rest_attention(last, queries, bias, kv1, kv3, kv2, acc, stat):
    square = (2 * WIN, HEAD_DIM)
    message = (2 * WIN + STAT_ROWS, HEAD_DIM)
    return pl.pallas_call(
        rest_kernel,
        grid_spec=attention_specs([square, square], [message], 3),
        out_shape=[jax.ShapeDtypeStruct((N_Z,) + message, bf16)],
        compiler_params=params(),
        cost_estimate=pl.CostEstimate(
            flops=8 << 30, bytes_accessed=8 << 20, transcendentals=6 << 20
        ),
        name="rest_attention",
    )(last, queries, bias, kv1, kv3, kv2, acc, stat)[0]


def combine_kernel(in_ref, out_ref):
    stats = in_ref[:, 2 * WIN :, :].astype(f32)
    for head in range(2):
        st = stats[:, 8 * head : 8 * head + 8]
        m = st[:, 0] + st[:, 2] + st[:, 4]
        l = st[:, 1] + st[:, 3] + st[:, 5]
        w = jnp.exp2((m - jnp.max(m, axis=0, keepdims=True)) * SCALE2)
        w = w / jnp.sum(w * l, axis=0, keepdims=True)
        wide = jnp.concatenate([w, jnp.zeros((WIN - N_Z, WIN), f32)], axis=0)
        cols = jnp.transpose(wide)
        total = jnp.zeros((WIN, HEAD_DIM), f32)
        for z in range(N_Z):
            part = in_ref[z, head * WIN : (head + 1) * WIN, :].astype(f32)
            total = total + part * cols[:, z : z + 1]
        done = total.astype(bf16)
        for z in range(N_Z):
            out_ref[z, :, head * HEAD_DIM : (head + 1) * HEAD_DIM] = done


def combine(parts):
    return pl.pallas_call(
        combine_kernel,
        out_shape=jax.ShapeDtypeStruct((N_Z, WIN, 2 * HEAD_DIM), bf16),
        compiler_params=params(),
        name="combine",
    )(parts)


def project_kernel(a_ref, w_ref, resid_ref, out_ref):
    acc = resid_ref[...].astype(f32)
    for z in range(N_Z):
        w_rows = jnp.concatenate([w_ref[g, z] for g in range(N_GRP)], axis=0)
        acc = acc + jnp.dot(a_ref[z], w_rows, preferred_element_type=f32)
    done = acc.astype(bf16)
    for y in range(N_Y):
        out_ref[y] = done


def project(attended, w_cols, resid_rows):
    return pl.pallas_call(
        project_kernel,
        out_shape=jax.ShapeDtypeStruct((N_Y, WIN, COLS), bf16),
        compiler_params=params(),
        name="project",
    )(attended, w_cols, resid_rows)


def dispatch_kernel(parts_ref, table_ref, stream_ref, out_ref):
    total = parts_ref[0].astype(f32)
    for y in range(1, N_Y):
        total = total + parts_ref[y].astype(f32)
    stream = total.astype(bf16)
    stream_ref[...] = stream
    out_ref[...] = jnp.dot(table_ref[...], stream, preferred_element_type=f32).astype(bf16)


def dispatch(parts, table):
    return pl.pallas_call(
        dispatch_kernel,
        out_shape=(
            jax.ShapeDtypeStruct((WIN, COLS), bf16),
            jax.ShapeDtypeStruct((N_GRP * CAP, COLS), bf16),
        ),
        compiler_params=params(),
        name="dispatch",
    )(parts, table)


def experts_kernel(x_ref, gain_ref, wg_ref, wu_ref, wd_ref, by_z_ref, by_x_ref):
    tokens = x_ref.shape[1]
    squares = jnp.zeros((tokens, 128), f32)
    gate = jnp.zeros((tokens, HIDDEN), f32)
    up = jnp.zeros((tokens, HIDDEN), f32)
    contract = (((1,), (1,)), ((), ()))
    for z in range(N_Z):
        cols = slice(z * COLS, (z + 1) * COLS)
        wide = x_ref[z].astype(f32)
        for b in range(COLS // 128):
            part = wide[:, b * 128 : (b + 1) * 128]
            squares = squares + part * part
        gained = (wide * gain_ref[:, cols]).astype(bf16)
        gate = gate + lax.dot_general(
            gained, wg_ref[:, cols], contract, preferred_element_type=f32
        )
        up = up + lax.dot_general(gained, wu_ref[:, cols], contract, preferred_element_type=f32)
    factor = lax.rsqrt(jnp.sum(squares, axis=1, keepdims=True) * (1.0 / D) + 1e-06)
    gate = gate * factor
    up = up * factor
    hidden = (gate / (1.0 + jnp.exp(-gate)) * up).astype(bf16)
    for z in range(N_Z):
        cols = slice(z * COLS, (z + 1) * COLS)
        done = jnp.dot(hidden, wd_ref[:, cols], preferred_element_type=f32).astype(bf16)
        by_z_ref[z] = done[:, :HALF]
        by_x_ref[:, z * HALF : (z + 1) * HALF] = done[:, HALF:]


def experts(x, gain, w_gate, w_up, w_down, tile=256):
    tokens = x.shape[1]
    whole = pl.BlockSpec((HIDDEN, D), lambda i: (0, 0))
    return pl.pallas_call(
        experts_kernel,
        grid=(tokens // tile,),
        in_specs=[
            pl.BlockSpec((N_Z, tile, COLS), lambda i: (0, i, 0)),
            pl.BlockSpec((1, D), lambda i: (0, 0)),
            whole,
            whole,
            whole,
        ],
        out_specs=[
            pl.BlockSpec((N_Z, tile, HALF), lambda i: (0, i, 0)),
            pl.BlockSpec((tile, D // 2), lambda i: (i, 0)),
        ],
        out_shape=[
            jax.ShapeDtypeStruct((N_Z, tokens, HALF), bf16),
            jax.ShapeDtypeStruct((tokens, D // 2), bf16),
        ],
        compiler_params=params(),
        name="experts",
    )(x, gain, w_gate, w_up, w_down)


def mix_kernel(table_ref, parts_ref, out_ref):
    out_ref[...] = jnp.dot(
        table_ref[...], parts_ref[...], preferred_element_type=f32
    ).astype(bf16)


def mix(table, parts):
    tile = 512
    return pl.pallas_call(
        mix_kernel,
        grid=(parts.shape[1] // tile,),
        in_specs=[
            pl.BlockSpec(table.shape, lambda i: (0, 0)),
            pl.BlockSpec((parts.shape[0], tile), lambda i: (0, i)),
        ],
        out_specs=pl.BlockSpec((WIN, tile), lambda i: (0, i)),
        out_shape=jax.ShapeDtypeStruct((WIN, parts.shape[1]), bf16),
        compiler_params=params(),
        cost_estimate=pl.CostEstimate(flops=1 << 28, bytes_accessed=4 << 20, transcendentals=0),
        name="mix",
    )(table, parts)


def mix_rest_kernel(table_ref, parts_ref, mixed_ref, out_ref):
    out_ref[:, : D // 2] = mixed_ref[...]
    out_ref[:, D // 2 :] = jnp.dot(
        table_ref[...], parts_ref[...], preferred_element_type=f32
    ).astype(bf16)


def mix_rest(table, parts, mixed):
    return pl.pallas_call(
        mix_rest_kernel,
        out_shape=jax.ShapeDtypeStruct((WIN, D // 2 + HALF), bf16),
        compiler_params=params(),
        name="mix_rest",
    )(table, parts, mixed)


def finish_kernel(in_ref, out_ref):
    summed = in_ref[0, :, : D // 2].astype(f32)
    for z in range(1, N_Z):
        summed = summed + in_ref[z, :, : D // 2].astype(f32)
    for z in range(N_Z):
        mine = in_ref[z, :, D // 2 :].astype(f32)
        first = mine[:, HALF : 2 * HALF] + mine[:, :HALF]
        second = mine[:, 2 * HALF :] + summed[:, z * HALF : (z + 1) * HALF]
        out_ref[:, z * COLS : z * COLS + HALF] = first.astype(bf16)
        out_ref[:, z * COLS + HALF : (z + 1) * COLS] = second.astype(bf16)


def finish(parts):
    return pl.pallas_call(
        finish_kernel,
        out_shape=jax.ShapeDtypeStruct((parts.shape[1], D), bf16),
        compiler_params=params(),
        name="finish",
    )(parts)


def per_device(
    queries,
    kv_cache,
    kv_scale,
    block_mask,
    resid,
    w_out,
    norm_gain,
    expert_ids,
    gate_weights,
    w_gate,
    w_up,
    w_down,
):
    y_pos = lax.axis_index("y")
    z_pos = lax.axis_index("z")

    chunks = dequantize(y_pos[None], kv_scale[0], kv_cache[0])
    kv_own, queries = lax.optimization_barrier((chunks[0], queries))
    queries_mine = lax.all_to_all(
        jnp.broadcast_to(queries, (N_Z,) + queries.shape[1:]), "z", 0, 0, tiled=True
    )
    kv_from = {
        d: lax.ppermute(chunks[d], "y", [(i, (i + d) % N_Y) for i in range(N_Y)])
        for d in (1, 3, 2)
    }

    blocks = CTX_LOCAL // BLOCK
    source = (y_pos - jnp.arange(N_Y, dtype=jnp.int32)) % N_Y
    mask = block_mask[0, 0].reshape(N_Y, N_Z, blocks)
    mask = lax.dynamic_slice_in_dim(mask, z_pos, 1, 1)[:, 0]
    mask = jnp.take(mask, source, axis=0)
    bias = jnp.where(mask == 1, 0.0, MASKED).astype(f32)
    bias = jnp.repeat(bias, BLOCK, axis=1)[:, None, :]
    last = ((source == N_Y - 1) & (z_pos == N_Z - 1)).astype(jnp.int32)

    rows = WIN // N_Y
    part = 2 * HEAD_DIM // N_GRP
    own_rows = resid.shape[1]
    grp_pos = lax.axis_index("x") * N_C + lax.axis_index("c")
    w_mine = lax.dynamic_slice_in_dim(w_out, grp_pos * part, part, 0)
    early = jnp.concatenate([w_mine, resid[0]], axis=0)
    early = early.reshape(part + own_rows, N_Z, COLS).transpose(1, 0, 2)
    early, queries_mine = lax.optimization_barrier((early, queries_mine))
    early = lax.all_to_all(early, "z", 0, 0, tiled=True)

    owners = jnp.arange(N_GRP, dtype=jnp.int32) * E_SUB + y_pos
    matches = expert_ids[0][None, :, :] == owners[:, None, None]
    chosen = jnp.any(matches, axis=-1)
    weight = jnp.sum(jnp.where(matches, gate_weights[0][None, :, :], 0.0), axis=-1)
    slot = jnp.cumsum(chosen.astype(jnp.int32), axis=1) - 1
    in_slot = chosen[:, None, :] & (
        slot[:, None, :] == jnp.arange(CAP, dtype=jnp.int32)[None, :, None]
    )
    out_table = in_slot.astype(bf16).reshape(N_GRP * CAP, WIN)
    back_table = jnp.where(in_slot, weight[:, None, :], 0.0).astype(bf16)
    back_table = back_table.reshape(N_GRP * CAP, WIN).T

    acc, stat = own_attention(last, queries_mine, bias, kv_own)
    parts = rest_attention(
        last, queries_mine, bias, kv_from[1], kv_from[3], kv_from[2], acc, stat
    )
    parts, early = lax.optimization_barrier((parts, early))
    resid_rows = lax.dynamic_update_slice_in_dim(
        jnp.zeros((WIN, COLS), bf16), early[:, part:].reshape(rows, COLS), y_pos * rows, 0
    )
    w_cols = lax.all_gather(early[:, :part], ("x", "c"), axis=0, tiled=False)
    parts = lax.all_to_all(parts, "z", 0, 0, tiled=True)
    attended = lax.all_to_all(combine(parts), "z", 0, 0, tiled=True)
    projected = lax.all_to_all(project(attended, w_cols, resid_rows), "y", 0, 0, tiled=True)
    stream, outgoing = dispatch(projected, out_table)

    arrivals = lax.all_to_all(
        outgoing.reshape(N_GRP, CAP, COLS), ("x", "c"), 0, 0, tiled=True
    ).reshape(N_GRP * CAP, COLS)
    arrivals = lax.all_gather(arrivals, "z", axis=0, tiled=False)
    by_z, by_x = experts(arrivals, norm_gain[None], w_gate[0], w_up[0], w_down[0])
    by_z = lax.psum_scatter(
        by_z.reshape(N_Z * N_GRP * CAP, HALF), "z", scatter_dimension=0, tiled=True
    )
    by_x = lax.all_to_all(
        by_x.reshape(N_GRP, CAP, D // 2), ("x", "c"), 0, 0, tiled=True
    ).reshape(N_GRP * CAP, D // 2)
    mixed = mix(back_table, by_x)
    by_z, by_x = lax.optimization_barrier((by_z, by_x))
    by_z = lax.all_to_all(
        by_z.reshape(N_GRP, CAP, HALF), ("x", "c"), 0, 0, tiled=True
    ).reshape(N_GRP * CAP, HALF)
    mixture = mix_rest(back_table, by_z, mixed).reshape(N_Y, rows, -1)

    stream_rows = lax.dynamic_slice_in_dim(stream, y_pos * rows, rows, 0)
    mixture = lax.all_to_all(mixture, "y", 0, 0, tiled=True)
    mixture = jnp.sum(mixture.astype(f32), axis=0).astype(bf16)
    tail = jnp.concatenate([mixture, stream_rows], axis=1).reshape(N_Z, own_rows, -1)
    return finish(lax.all_to_all(tail, "z", 0, 0, tiled=True))[None]


def solution(mesh):
    fine = Mesh(mesh.devices.reshape(N_Y, N_Z, N_X, N_C), ("y", "z", "x", "c"))
    seq, grp = ("y", "z"), ("x", "c")
    in_specs = (
        P(grp, None, seq),
        P(grp, seq, None),
        P(grp, seq, None),
        P(grp, None, None),
        P(grp, seq, None),
        P(seq, None),
        P(),
        P(grp, None, None),
        P(grp, None, None),
        P(grp, seq, None),
        P(grp, seq, None),
        P(grp, seq, None),
    )
    return jax.shard_map(
        per_device, mesh=fine, in_specs=in_specs, out_specs=P(grp, seq, None), check_vma=False
    )
```

```python
import math

import jax
import jax.numpy as jnp
from jax import lax
from jax.experimental import pallas as pl
from jax.experimental.pallas import tpu as pltpu
from jax.sharding import Mesh
from jax.sharding import PartitionSpec as P

HEADS = 64
KV_HEADS = 4
HEAD_DIM = 128
BLOCK = 128
E_SUB = 4
CAP = 64
N_Y, N_Z, N_X, N_C = 4, 8, 4, 2
N_GRP = N_X * N_C
WIN = 128
D = 4096
COLS = D // N_Z
HALF = COLS // 2
NEAR = 384
FAR = COLS - NEAR
CTX_LOCAL = 1024
HIDDEN = 192
STAT_ROWS = 16
PAIRS = 2
MASKED = -1e30
SCALE2 = math.log2(math.e) / math.sqrt(HEAD_DIM)
VMEM = 56 * 1024 * 1024

f32 = jnp.float32
bf16 = jnp.bfloat16


def params():
    return pltpu.CompilerParams(vmem_limit_bytes=VMEM)


def dequantize_kernel(y_ref, scale_ref, cache_ref, *out_refs):
    step = pl.program_id(0)
    for d, out_ref in enumerate(out_refs):
        head = lax.rem(y_ref[0] + d, N_Y)
        for part in range(2):
            column = part * KV_HEADS + head
            lanes = pl.ds(pl.multiple_of(column * HEAD_DIM, HEAD_DIM), HEAD_DIM)
            for b in range(4):
                rows = slice(b * BLOCK, (b + 1) * BLOCK)
                raw = cache_ref[rows, lanes].astype(f32)
                out_ref[part, rows, :] = (raw * scale_ref[4 * step + b, column]).astype(bf16)


def dequantize(y_pos, scale, cache):
    shape = jax.ShapeDtypeStruct((2, CTX_LOCAL, HEAD_DIM), bf16)
    return pl.pallas_call(
        dequantize_kernel,
        grid_spec=pltpu.PrefetchScalarGridSpec(
            num_scalar_prefetch=2,
            grid=(CTX_LOCAL // (4 * BLOCK),),
            in_specs=[pl.BlockSpec((4 * BLOCK, 2 * KV_HEADS * HEAD_DIM), lambda i, *_: (i, 0))],
            out_specs=[pl.BlockSpec((2, 4 * BLOCK, HEAD_DIM), lambda i, *_: (0, i, 0))] * N_Y,
        ),
        out_shape=[shape] * N_Y,
        compiler_params=params(),
        cost_estimate=pl.CostEstimate(flops=1 << 20, bytes_accessed=4 << 20, transcendentals=0),
        name="dequantize",
    )(y_pos, scale, cache)


def attend_chunks(q_ref, kv_refs, bias_ref, last_ref, s_ref, pair, order):
    q_pair = jnp.concatenate([q_ref[pair, :, :HEAD_DIM], q_ref[pair, :, HEAD_DIM:]], axis=0)
    peak = jnp.full((2 * WIN, BLOCK), -jnp.inf, f32)
    row = lax.broadcasted_iota(jnp.int32, (2 * WIN, BLOCK), 0)
    row = jnp.where(row >= WIN, row - WIN, row)
    later = lax.broadcasted_iota(jnp.int32, (2 * WIN, BLOCK), 1) > row
    for i, (kv_ref, d) in enumerate(zip(kv_refs, order)):
        s = lax.dot_general(
            q_pair, kv_ref[0], (((1,), (1,)), ((), ())), preferred_element_type=f32
        )
        s = s + bias_ref[d]
        cut = jnp.where(later & (last_ref[d] == 1), MASKED, 0.0)
        end = CTX_LOCAL - BLOCK
        s_ref[pair, :, i * CTX_LOCAL : i * CTX_LOCAL + end] = s[:, :end]
        tail = s[:, end:] + cut
        s_ref[pair, :, i * CTX_LOCAL + end : (i + 1) * CTX_LOCAL] = tail
        for b in range(CTX_LOCAL // BLOCK - 1):
            peak = jnp.maximum(peak, s[:, b * BLOCK : (b + 1) * BLOCK])
        peak = jnp.maximum(peak, tail)
    return jnp.max(peak, axis=1, keepdims=True)


def weigh_chunks(kv_refs, s_ref, pair, m):
    total = jnp.zeros((2 * WIN, BLOCK), f32)
    acc = jnp.zeros((2 * WIN, HEAD_DIM), f32)
    for i, kv_ref in enumerate(kv_refs):
        s = s_ref[pair, :, i * CTX_LOCAL : (i + 1) * CTX_LOCAL]
        p = jnp.exp2((s - m) * SCALE2)
        for b in range(CTX_LOCAL // BLOCK):
            total = total + p[:, b * BLOCK : (b + 1) * BLOCK]
        acc = acc + jnp.dot(p.astype(bf16), kv_ref[1], preferred_element_type=f32)
    return jnp.sum(total, axis=1, keepdims=True), acc


def own_kernel(last_ref, q_ref, bias_ref, kv0, acc_ref, stat_ref, s_ref):
    lane = lax.broadcasted_iota(jnp.int32, (2 * WIN, 128), 1)
    maxima = [
        attend_chunks(q_ref, (kv0,), bias_ref, last_ref, s_ref, pair, (0,))
        for pair in range(PAIRS)
    ]
    for pair, m in enumerate(maxima):
        l, acc = weigh_chunks((kv0,), s_ref, pair, m)
        acc_ref[pair] = acc
        stat_ref[pair] = jnp.where(lane == 0, m, l)


def rest_kernel(last_ref, q_ref, bias_ref, kv1, kv3, kv2, acc_ref, stat_ref, out_ref, s_ref):
    kv_refs = (kv1, kv3, kv2)
    lane = lax.broadcasted_iota(jnp.int32, (2 * WIN, 128), 1)
    row = lax.broadcasted_iota(jnp.int32, (8, 2 * WIN), 0)
    maxima = [
        attend_chunks(q_ref, kv_refs, bias_ref, last_ref, s_ref, pair, (1, 3, 2))
        for pair in range(PAIRS)
    ]
    for pair, highest in enumerate(maxima):
        before = stat_ref[pair, :, :1]
        m = jnp.maximum(highest, before)
        l, acc = weigh_chunks(kv_refs, s_ref, pair, m)
        keep = jnp.exp2((before - m) * SCALE2)
        l = l + stat_ref[pair, :, 1:2] * keep
        out_ref[pair, : 2 * WIN, :] = (acc + acc_ref[pair] * keep).astype(bf16)
        turned = jnp.transpose(jnp.where(lane % 2 == 0, m, l))[:8]
        high = turned.astype(bf16).astype(f32)
        middle = (turned - high).astype(bf16).astype(f32)
        low = turned - high - middle
        rows = jnp.where(row < 2, high, jnp.where(row < 4, middle, low))
        out_ref[pair, 2 * WIN :, :] = jnp.concatenate(
            [rows[:, :WIN], rows[:, WIN:]], axis=0
        ).astype(bf16)


def attention_specs(extra, outs, chunks):
    whole = pl.BlockSpec((2, CTX_LOCAL, HEAD_DIM), lambda i, *_: (0, 0, 0))
    return pltpu.PrefetchScalarGridSpec(
        num_scalar_prefetch=1,
        grid=(N_Z // PAIRS,),
        in_specs=[
            pl.BlockSpec((PAIRS, WIN, 2 * HEAD_DIM), lambda i, *_: (i, 0, 0)),
            pl.BlockSpec((N_Y, 1, CTX_LOCAL), lambda i, *_: (0, 0, 0)),
        ]
        + [whole] * chunks
        + [pl.BlockSpec((PAIRS,) + e, lambda i, *_: (i, 0, 0)) for e in extra],
        out_specs=[pl.BlockSpec((PAIRS,) + o, lambda i, *_: (i, 0, 0)) for o in outs],
        scratch_shapes=[pltpu.VMEM((PAIRS, 2 * WIN, chunks * CTX_LOCAL), f32)],
    )


def own_attention(last, queries, bias, kv0):
    square = (2 * WIN, HEAD_DIM)
    return pl.pallas_call(
        own_kernel,
        grid_spec=attention_specs([], [square, square], 1),
        out_shape=[jax.ShapeDtypeStruct((N_Z,) + square, f32)] * 2,
        compiler_params=params(),
        cost_estimate=pl.CostEstimate(
            flops=3 << 30, bytes_accessed=8 << 20, transcendentals=2 << 20
        ),
        name="own_attention",
    )(last, queries, bias, kv0)


def rest_attention(last, queries, bias, kv1, kv3, kv2, acc, stat):
    square = (2 * WIN, HEAD_DIM)
    message = (2 * WIN + STAT_ROWS, HEAD_DIM)
    return pl.pallas_call(
        rest_kernel,
        grid_spec=attention_specs([square, square], [message], 3),
        out_shape=[jax.ShapeDtypeStruct((N_Z,) + message, bf16)],
        compiler_params=params(),
        cost_estimate=pl.CostEstimate(
            flops=8 << 30, bytes_accessed=8 << 20, transcendentals=6 << 20
        ),
        name="rest_attention",
    )(last, queries, bias, kv1, kv3, kv2, acc, stat)[0]


def combine_kernel(in_ref, out_ref):
    stats = in_ref[:, 2 * WIN :, :].astype(f32)
    for head in range(2):
        st = stats[:, 8 * head : 8 * head + 8]
        m = st[:, 0] + st[:, 2] + st[:, 4]
        l = st[:, 1] + st[:, 3] + st[:, 5]
        w = jnp.exp2((m - jnp.max(m, axis=0, keepdims=True)) * SCALE2)
        w = w / jnp.sum(w * l, axis=0, keepdims=True)
        wide = jnp.concatenate([w, jnp.zeros((WIN - N_Z, WIN), f32)], axis=0)
        cols = jnp.transpose(wide)
        total = jnp.zeros((WIN, HEAD_DIM), f32)
        for z in range(N_Z):
            part = in_ref[z, head * WIN : (head + 1) * WIN, :].astype(f32)
            total = total + part * cols[:, z : z + 1]
        done = total.astype(bf16)
        for z in range(N_Z):
            out_ref[z, :, head * HEAD_DIM : (head + 1) * HEAD_DIM] = done


def combine(parts):
    return pl.pallas_call(
        combine_kernel,
        out_shape=jax.ShapeDtypeStruct((N_Z, WIN, 2 * HEAD_DIM), bf16),
        compiler_params=params(),
        name="combine",
    )(parts)


def project_kernel(a_ref, w_ref, resid_ref, out_ref):
    acc = resid_ref[...].astype(f32)
    for z in range(N_Z):
        w_rows = jnp.concatenate([w_ref[g, z] for g in range(N_GRP)], axis=0)
        acc = acc + jnp.dot(a_ref[z], w_rows, preferred_element_type=f32)
    done = acc.astype(bf16)
    for y in range(N_Y):
        out_ref[y] = done


def project(attended, w_cols, resid_rows):
    return pl.pallas_call(
        project_kernel,
        out_shape=jax.ShapeDtypeStruct((N_Y, WIN, COLS), bf16),
        compiler_params=params(),
        name="project",
    )(attended, w_cols, resid_rows)


def dispatch_kernel(parts_ref, table_ref, stream_ref, out_ref, spread_ref):
    total = parts_ref[0].astype(f32)
    for y in range(1, N_Y):
        total = total + parts_ref[y].astype(f32)
    stream = total.astype(bf16)
    stream_ref[...] = stream
    out_ref[...] = jnp.dot(
        table_ref[...], stream[:, :NEAR], preferred_element_type=f32
    ).astype(bf16)
    for z in range(N_Z):
        spread_ref[z] = stream[:, NEAR:]


def dispatch(parts, table):
    return pl.pallas_call(
        dispatch_kernel,
        out_shape=(
            jax.ShapeDtypeStruct((WIN, COLS), bf16),
            jax.ShapeDtypeStruct((N_GRP * CAP, NEAR), bf16),
            jax.ShapeDtypeStruct((N_Z, WIN, FAR), bf16),
        ),
        compiler_params=params(),
        name="dispatch",
    )(parts, table)


def select_kernel(parts_ref, table_ref, out_ref):
    wide = jnp.concatenate([parts_ref[z] for z in range(N_Z)], axis=1)
    out_ref[...] = jnp.dot(table_ref[...], wide, preferred_element_type=f32).astype(bf16)


def select(parts, table):
    return pl.pallas_call(
        select_kernel,
        out_shape=jax.ShapeDtypeStruct((N_GRP * CAP, N_Z * FAR), bf16),
        compiler_params=params(),
        name="select",
    )(parts, table)


def experts_kernel(x_ref, rest_ref, gain_ref, wg_ref, wu_ref, wd_ref, by_z_ref, by_x_ref):
    tokens = x_ref.shape[1]
    squares = jnp.zeros((tokens, 128), f32)
    gate = jnp.zeros((tokens, HIDDEN), f32)
    up = jnp.zeros((tokens, HIDDEN), f32)
    contract = (((1,), (1,)), ((), ()))
    for z in range(N_Z):
        cols = slice(z * COLS, (z + 1) * COLS)
        far = rest_ref[:, z * FAR : (z + 1) * FAR]
        wide = jnp.concatenate([x_ref[z], far], axis=1).astype(f32)
        for b in range(COLS // 128):
            part = wide[:, b * 128 : (b + 1) * 128]
            squares = squares + part * part
        gained = (wide * gain_ref[:, cols]).astype(bf16)
        gate = gate + lax.dot_general(
            gained, wg_ref[:, cols], contract, preferred_element_type=f32
        )
        up = up + lax.dot_general(gained, wu_ref[:, cols], contract, preferred_element_type=f32)
    factor = lax.rsqrt(jnp.sum(squares, axis=1, keepdims=True) * (1.0 / D) + 1e-06)
    gate = gate * factor
    up = up * factor
    hidden = (gate / (1.0 + jnp.exp(-gate)) * up).astype(bf16)
    for z in range(N_Z):
        cols = slice(z * COLS, (z + 1) * COLS)
        done = jnp.dot(hidden, wd_ref[:, cols], preferred_element_type=f32).astype(bf16)
        by_z_ref[z] = done[:, :HALF]
        by_x_ref[:, z * HALF : (z + 1) * HALF] = done[:, HALF:]


def experts(x, rest, gain, w_gate, w_up, w_down, tile=256):
    tokens = x.shape[1]
    whole = pl.BlockSpec((HIDDEN, D), lambda i: (0, 0))
    return pl.pallas_call(
        experts_kernel,
        grid=(tokens // tile,),
        in_specs=[
            pl.BlockSpec((N_Z, tile, NEAR), lambda i: (0, i, 0)),
            pl.BlockSpec((tile, N_Z * FAR), lambda i: (i, 0)),
            pl.BlockSpec((1, D), lambda i: (0, 0)),
            whole,
            whole,
            whole,
        ],
        out_specs=[
            pl.BlockSpec((N_Z, tile, HALF), lambda i: (0, i, 0)),
            pl.BlockSpec((tile, D // 2), lambda i: (i, 0)),
        ],
        out_shape=[
            jax.ShapeDtypeStruct((N_Z, tokens, HALF), bf16),
            jax.ShapeDtypeStruct((tokens, D // 2), bf16),
        ],
        compiler_params=params(),
        name="experts",
    )(x, rest, gain, w_gate, w_up, w_down)


def mix_kernel(table_ref, parts_ref, out_ref):
    out_ref[...] = jnp.dot(
        table_ref[...], parts_ref[...], preferred_element_type=f32
    ).astype(bf16)


def mix(table, parts):
    tile = 1024
    return pl.pallas_call(
        mix_kernel,
        grid=(parts.shape[1] // tile,),
        in_specs=[
            pl.BlockSpec(table.shape, lambda i: (0, 0)),
            pl.BlockSpec((parts.shape[0], tile), lambda i: (0, i)),
        ],
        out_specs=pl.BlockSpec((WIN, tile), lambda i: (0, i)),
        out_shape=jax.ShapeDtypeStruct((WIN, parts.shape[1]), bf16),
        compiler_params=params(),
        cost_estimate=pl.CostEstimate(flops=1 << 28, bytes_accessed=4 << 20, transcendentals=0),
        name="mix",
    )(table, parts)


def mix_rest_kernel(table_ref, parts_ref, mixed_ref, out_ref):
    out_ref[:, : D // 2] = mixed_ref[...]
    out_ref[:, D // 2 :] = jnp.dot(
        table_ref[...], parts_ref[...], preferred_element_type=f32
    ).astype(bf16)


def mix_rest(table, parts, mixed):
    return pl.pallas_call(
        mix_rest_kernel,
        out_shape=jax.ShapeDtypeStruct((WIN, D // 2 + HALF), bf16),
        compiler_params=params(),
        name="mix_rest",
    )(table, parts, mixed)


def finish_kernel(in_ref, out_ref):
    summed = in_ref[0, :, : D // 2].astype(f32)
    for z in range(1, N_Z):
        summed = summed + in_ref[z, :, : D // 2].astype(f32)
    for z in range(N_Z):
        mine = in_ref[z, :, D // 2 :].astype(f32)
        first = mine[:, HALF : 2 * HALF] + mine[:, :HALF]
        second = mine[:, 2 * HALF :] + summed[:, z * HALF : (z + 1) * HALF]
        out_ref[:, z * COLS : z * COLS + HALF] = first.astype(bf16)
        out_ref[:, z * COLS + HALF : (z + 1) * COLS] = second.astype(bf16)


def finish(parts):
    return pl.pallas_call(
        finish_kernel,
        out_shape=jax.ShapeDtypeStruct((parts.shape[1], D), bf16),
        compiler_params=params(),
        name="finish",
    )(parts)


def per_device(
    queries,
    kv_cache,
    kv_scale,
    block_mask,
    resid,
    w_out,
    norm_gain,
    expert_ids,
    gate_weights,
    w_gate,
    w_up,
    w_down,
):
    y_pos = lax.axis_index("y")
    z_pos = lax.axis_index("z")

    chunks = dequantize(y_pos[None], kv_scale[0], kv_cache[0])
    kv_own = chunks[0]
    queries_mine = lax.all_to_all(
        jnp.broadcast_to(queries, (N_Z,) + queries.shape[1:]), "z", 0, 0, tiled=True
    )
    kv_from = {
        d: lax.ppermute(chunks[d], "y", [(i, (i + d) % N_Y) for i in range(N_Y)])
        for d in (1, 3, 2)
    }

    blocks = CTX_LOCAL // BLOCK
    source = (y_pos - jnp.arange(N_Y, dtype=jnp.int32)) % N_Y
    mask = block_mask[0, 0].reshape(N_Y, N_Z, blocks)
    mask = lax.dynamic_slice_in_dim(mask, z_pos, 1, 1)[:, 0]
    mask = jnp.take(mask, source, axis=0)
    bias = jnp.where(mask == 1, 0.0, MASKED).astype(f32)
    bias = jnp.repeat(bias, BLOCK, axis=1)[:, None, :]
    last = ((source == N_Y - 1) & (z_pos == N_Z - 1)).astype(jnp.int32)

    rows = WIN // N_Y
    part = 2 * HEAD_DIM // N_GRP
    own_rows = resid.shape[1]
    grp_pos = lax.axis_index("x") * N_C + lax.axis_index("c")
    w_mine = lax.dynamic_slice_in_dim(w_out, grp_pos * part, part, 0)
    early = jnp.concatenate([w_mine, resid[0]], axis=0)
    early = early.reshape(part + own_rows, N_Z, COLS).transpose(1, 0, 2)
    early, queries_mine = lax.optimization_barrier((early, queries_mine))
    early = lax.all_to_all(early, "z", 0, 0, tiled=True)

    owners = jnp.arange(N_GRP, dtype=jnp.int32) * E_SUB + y_pos
    matches = expert_ids[0][None, :, :] == owners[:, None, None]
    chosen = jnp.any(matches, axis=-1)
    weight = jnp.sum(jnp.where(matches, gate_weights[0][None, :, :], 0.0), axis=-1)
    slot = jnp.cumsum(chosen.astype(jnp.int32), axis=1) - 1
    in_slot = chosen[:, None, :] & (
        slot[:, None, :] == jnp.arange(CAP, dtype=jnp.int32)[None, :, None]
    )
    out_table = in_slot.astype(bf16).reshape(N_GRP * CAP, WIN)
    back_table = jnp.where(in_slot, weight[:, None, :], 0.0).astype(bf16)
    back_table = back_table.reshape(N_GRP * CAP, WIN).T

    acc, stat = own_attention(last, queries_mine, bias, kv_own)
    parts = rest_attention(
        last, queries_mine, bias, kv_from[1], kv_from[3], kv_from[2], acc, stat
    )
    parts, early = lax.optimization_barrier((parts, early))
    resid_rows = lax.dynamic_update_slice_in_dim(
        jnp.zeros((WIN, COLS), bf16), early[:, part:].reshape(rows, COLS), y_pos * rows, 0
    )
    w_cols = lax.all_gather(early[:, :part], ("x", "c"), axis=0, tiled=False)
    parts = lax.all_to_all(parts, "z", 0, 0, tiled=True)
    attended = lax.all_to_all(combine(parts), "z", 0, 0, tiled=True)
    projected = lax.all_to_all(project(attended, w_cols, resid_rows), "y", 0, 0, tiled=True)
    stream, outgoing, spread = dispatch(projected, out_table)

    arrivals = lax.all_to_all(
        outgoing.reshape(N_GRP, CAP, NEAR), ("x", "c"), 0, 0, tiled=True
    ).reshape(N_GRP * CAP, NEAR)
    arrivals, spread = lax.optimization_barrier((arrivals, spread))
    arrivals = lax.all_gather(arrivals, "z", axis=0, tiled=False)
    others = select(lax.all_to_all(spread, "z", 0, 0, tiled=True), out_table)
    others = lax.all_to_all(
        others.reshape(N_GRP, CAP, N_Z * FAR), ("x", "c"), 0, 0, tiled=True
    ).reshape(N_GRP * CAP, N_Z * FAR)
    by_z, by_x = experts(
        arrivals, others, norm_gain[None], w_gate[0], w_up[0], w_down[0]
    )
    by_z = lax.psum_scatter(
        by_z.reshape(N_Z * N_GRP * CAP, HALF), "z", scatter_dimension=0, tiled=True
    )
    by_x = lax.all_to_all(
        by_x.reshape(N_GRP, CAP, D // 2), ("x", "c"), 0, 0, tiled=True
    ).reshape(N_GRP * CAP, D // 2)
    mixed = mix(back_table, by_x)
    by_z, by_x = lax.optimization_barrier((by_z, by_x))
    by_z = lax.all_to_all(
        by_z.reshape(N_GRP, CAP, HALF), ("x", "c"), 0, 0, tiled=True
    ).reshape(N_GRP * CAP, HALF)
    mixture = mix_rest(back_table, by_z, mixed).reshape(N_Y, rows, -1)

    stream_rows = lax.dynamic_slice_in_dim(stream, y_pos * rows, rows, 0)
    mixture = lax.all_to_all(mixture, "y", 0, 0, tiled=True)
    mixture = jnp.sum(mixture.astype(f32), axis=0).astype(bf16)
    tail = jnp.concatenate([mixture, stream_rows], axis=1).reshape(N_Z, own_rows, -1)
    return finish(lax.all_to_all(tail, "z", 0, 0, tiled=True))[None]


def solution(mesh):
    fine = Mesh(mesh.devices.reshape(N_Y, N_Z, N_X, N_C), ("y", "z", "x", "c"))
    seq, grp = ("y", "z"), ("x", "c")
    in_specs = (
        P(grp, None, seq),
        P(grp, seq, None),
        P(grp, seq, None),
        P(grp, None, None),
        P(grp, seq, None),
        P(seq, None),
        P(),
        P(grp, None, None),
        P(grp, None, None),
        P(grp, seq, None),
        P(grp, seq, None),
        P(grp, seq, None),
    )
    return jax.shard_map(
        per_device, mesh=fine, in_specs=in_specs, out_specs=P(grp, seq, None), check_vma=False
    )
```

```python
import math

import jax
import jax.numpy as jnp
from jax import lax
from jax.experimental import pallas as pl
from jax.experimental.pallas import tpu as pltpu
from jax.sharding import Mesh
from jax.sharding import PartitionSpec as P

HEADS = 64
KV_HEADS = 4
HEAD_DIM = 128
BLOCK = 128
E_SUB = 4
CAP = 64
N_Y, N_Z, N_X, N_C = 4, 8, 4, 2
N_GRP = N_X * N_C
WIN = 128
D = 4096
COLS = D // N_Z
HALF = COLS // 2
NEAR = 384
FAR = COLS - NEAR
CTX_LOCAL = 1024
HIDDEN = 192
STAT_ROWS = 16
PAIRS = 2
MASKED = -1e30
SCALE2 = math.log2(math.e) / math.sqrt(HEAD_DIM)
VMEM = 56 * 1024 * 1024

f32 = jnp.float32
bf16 = jnp.bfloat16


def params():
    return pltpu.CompilerParams(vmem_limit_bytes=VMEM)


def dequantize_kernel(y_ref, scale_ref, cache_ref, *out_refs):
    step = pl.program_id(0)
    for d, out_ref in enumerate(out_refs):
        head = lax.rem(y_ref[0] + d, N_Y)
        for part in range(2):
            column = part * KV_HEADS + head
            lanes = pl.ds(pl.multiple_of(column * HEAD_DIM, HEAD_DIM), HEAD_DIM)
            for b in range(4):
                rows = slice(b * BLOCK, (b + 1) * BLOCK)
                raw = cache_ref[rows, lanes].astype(f32)
                out_ref[part, rows, :] = (raw * scale_ref[4 * step + b, column]).astype(bf16)


def dequantize(y_pos, scale, cache):
    shape = jax.ShapeDtypeStruct((2, CTX_LOCAL, HEAD_DIM), bf16)
    return pl.pallas_call(
        dequantize_kernel,
        grid_spec=pltpu.PrefetchScalarGridSpec(
            num_scalar_prefetch=2,
            grid=(CTX_LOCAL // (4 * BLOCK),),
            in_specs=[pl.BlockSpec((4 * BLOCK, 2 * KV_HEADS * HEAD_DIM), lambda i, *_: (i, 0))],
            out_specs=[pl.BlockSpec((2, 4 * BLOCK, HEAD_DIM), lambda i, *_: (0, i, 0))] * N_Y,
        ),
        out_shape=[shape] * N_Y,
        compiler_params=params(),
        cost_estimate=pl.CostEstimate(flops=1 << 20, bytes_accessed=4 << 20, transcendentals=0),
        name="dequantize",
    )(y_pos, scale, cache)


def attend_chunks(q_ref, kv_refs, bias_ref, last_ref, s_ref, pair, order):
    q_pair = jnp.concatenate([q_ref[pair, :, :HEAD_DIM], q_ref[pair, :, HEAD_DIM:]], axis=0)
    peak = jnp.full((2 * WIN, BLOCK), -jnp.inf, f32)
    row = lax.broadcasted_iota(jnp.int32, (2 * WIN, BLOCK), 0)
    row = jnp.where(row >= WIN, row - WIN, row)
    later = lax.broadcasted_iota(jnp.int32, (2 * WIN, BLOCK), 1) > row
    for i, (kv_ref, d) in enumerate(zip(kv_refs, order)):
        s = lax.dot_general(
            q_pair, kv_ref[0], (((1,), (1,)), ((), ())), preferred_element_type=f32
        )
        s = s + bias_ref[d]
        cut = jnp.where(later & (last_ref[d] == 1), MASKED, 0.0)
        end = CTX_LOCAL - BLOCK
        s_ref[pair, :, i * CTX_LOCAL : i * CTX_LOCAL + end] = s[:, :end]
        tail = s[:, end:] + cut
        s_ref[pair, :, i * CTX_LOCAL + end : (i + 1) * CTX_LOCAL] = tail
        for b in range(CTX_LOCAL // BLOCK - 1):
            peak = jnp.maximum(peak, s[:, b * BLOCK : (b + 1) * BLOCK])
        peak = jnp.maximum(peak, tail)
    return jnp.max(peak, axis=1, keepdims=True)


def weigh_chunks(kv_refs, s_ref, pair, m):
    total = jnp.zeros((2 * WIN, BLOCK), f32)
    acc = jnp.zeros((2 * WIN, HEAD_DIM), f32)
    for i, kv_ref in enumerate(kv_refs):
        s = s_ref[pair, :, i * CTX_LOCAL : (i + 1) * CTX_LOCAL]
        p = jnp.exp2((s - m) * SCALE2)
        for b in range(CTX_LOCAL // BLOCK):
            total = total + p[:, b * BLOCK : (b + 1) * BLOCK]
        acc = acc + jnp.dot(p.astype(bf16), kv_ref[1], preferred_element_type=f32)
    return jnp.sum(total, axis=1, keepdims=True), acc


def own_kernel(last_ref, q_ref, bias_ref, kv0, acc_ref, stat_ref, s_ref):
    lane = lax.broadcasted_iota(jnp.int32, (2 * WIN, 128), 1)
    maxima = [
        attend_chunks(q_ref, (kv0,), bias_ref, last_ref, s_ref, pair, (0,))
        for pair in range(PAIRS)
    ]
    for pair, m in enumerate(maxima):
        l, acc = weigh_chunks((kv0,), s_ref, pair, m)
        acc_ref[pair] = acc
        stat_ref[pair] = jnp.where(lane == 0, m, l)


def rest_kernel(last_ref, q_ref, bias_ref, kv1, kv3, kv2, acc_ref, stat_ref, out_ref, s_ref):
    kv_refs = (kv1, kv3, kv2)
    lane = lax.broadcasted_iota(jnp.int32, (2 * WIN, 128), 1)
    row = lax.broadcasted_iota(jnp.int32, (8, 2 * WIN), 0)
    maxima = [
        attend_chunks(q_ref, kv_refs, bias_ref, last_ref, s_ref, pair, (1, 3, 2))
        for pair in range(PAIRS)
    ]
    for pair, highest in enumerate(maxima):
        before = stat_ref[pair, :, :1]
        m = jnp.maximum(highest, before)
        l, acc = weigh_chunks(kv_refs, s_ref, pair, m)
        keep = jnp.exp2((before - m) * SCALE2)
        l = l + stat_ref[pair, :, 1:2] * keep
        out_ref[pair, : 2 * WIN, :] = (acc + acc_ref[pair] * keep).astype(bf16)
        turned = jnp.transpose(jnp.where(lane % 2 == 0, m, l))[:8]
        high = turned.astype(bf16).astype(f32)
        middle = (turned - high).astype(bf16).astype(f32)
        low = turned - high - middle
        rows = jnp.where(row < 2, high, jnp.where(row < 4, middle, low))
        out_ref[pair, 2 * WIN :, :] = jnp.concatenate(
            [rows[:, :WIN], rows[:, WIN:]], axis=0
        ).astype(bf16)


def attention_specs(extra, outs, chunks):
    whole = pl.BlockSpec((2, CTX_LOCAL, HEAD_DIM), lambda i, *_: (0, 0, 0))
    return pltpu.PrefetchScalarGridSpec(
        num_scalar_prefetch=1,
        grid=(N_Z // PAIRS,),
        in_specs=[
            pl.BlockSpec((PAIRS, WIN, 2 * HEAD_DIM), lambda i, *_: (i, 0, 0)),
            pl.BlockSpec((N_Y, 1, CTX_LOCAL), lambda i, *_: (0, 0, 0)),
        ]
        + [whole] * chunks
        + [pl.BlockSpec((PAIRS,) + e, lambda i, *_: (i, 0, 0)) for e in extra],
        out_specs=[pl.BlockSpec((PAIRS,) + o, lambda i, *_: (i, 0, 0)) for o in outs],
        scratch_shapes=[pltpu.VMEM((PAIRS, 2 * WIN, chunks * CTX_LOCAL), f32)],
    )


def own_attention(last, queries, bias, kv0):
    square = (2 * WIN, HEAD_DIM)
    return pl.pallas_call(
        own_kernel,
        grid_spec=attention_specs([], [square, square], 1),
        out_shape=[jax.ShapeDtypeStruct((N_Z,) + square, f32)] * 2,
        compiler_params=params(),
        cost_estimate=pl.CostEstimate(
            flops=3 << 30, bytes_accessed=8 << 20, transcendentals=2 << 20
        ),
        name="own_attention",
    )(last, queries, bias, kv0)


def rest_attention(last, queries, bias, kv1, kv3, kv2, acc, stat):
    square = (2 * WIN, HEAD_DIM)
    message = (2 * WIN + STAT_ROWS, HEAD_DIM)
    return pl.pallas_call(
        rest_kernel,
        grid_spec=attention_specs([square, square], [message], 3),
        out_shape=[jax.ShapeDtypeStruct((N_Z,) + message, bf16)],
        compiler_params=params(),
        cost_estimate=pl.CostEstimate(
            flops=8 << 30, bytes_accessed=8 << 20, transcendentals=6 << 20
        ),
        name="rest_attention",
    )(last, queries, bias, kv1, kv3, kv2, acc, stat)[0]


def combine_kernel(in_ref, out_ref):
    stats = in_ref[:, 2 * WIN :, :].astype(f32)
    for head in range(2):
        st = stats[:, 8 * head : 8 * head + 8]
        m = st[:, 0] + st[:, 2] + st[:, 4]
        l = st[:, 1] + st[:, 3] + st[:, 5]
        w = jnp.exp2((m - jnp.max(m, axis=0, keepdims=True)) * SCALE2)
        w = w / jnp.sum(w * l, axis=0, keepdims=True)
        wide = jnp.concatenate([w, jnp.zeros((WIN - N_Z, WIN), f32)], axis=0)
        cols = jnp.transpose(wide)
        total = jnp.zeros((WIN, HEAD_DIM), f32)
        for z in range(N_Z):
            part = in_ref[z, head * WIN : (head + 1) * WIN, :].astype(f32)
            total = total + part * cols[:, z : z + 1]
        done = total.astype(bf16)
        for z in range(N_Z):
            out_ref[z, :, head * HEAD_DIM : (head + 1) * HEAD_DIM] = done


def combine(parts):
    return pl.pallas_call(
        combine_kernel,
        out_shape=jax.ShapeDtypeStruct((N_Z, WIN, 2 * HEAD_DIM), bf16),
        compiler_params=params(),
        name="combine",
    )(parts)


def project_kernel(a_ref, w_ref, resid_ref, out_ref):
    acc = resid_ref[...].astype(f32)
    for z in range(N_Z):
        w_rows = jnp.concatenate([w_ref[g, z] for g in range(N_GRP)], axis=0)
        acc = acc + jnp.dot(a_ref[z], w_rows, preferred_element_type=f32)
    out_ref[...] = acc.astype(bf16)


def project(attended, w_cols, resid_rows):
    return pl.pallas_call(
        project_kernel,
        out_shape=jax.ShapeDtypeStruct((WIN, COLS), bf16),
        compiler_params=params(),
        name="project",
    )(attended, w_cols, resid_rows)


def dispatch_kernel(table_ref, own_ref, one_ref, two_ref, three_ref, stream_ref, out_ref, spread_ref):
    total = (own_ref[...].astype(f32) + two_ref[...].astype(f32)) + (
        one_ref[...].astype(f32) + three_ref[...].astype(f32)
    )
    stream = total.astype(bf16)
    stream_ref[...] = stream
    out_ref[...] = jnp.dot(
        table_ref[...], stream[:, :NEAR], preferred_element_type=f32
    ).astype(bf16)
    for z in range(N_Z):
        spread_ref[z] = stream[:, NEAR:]


def dispatch(table, *parts):
    return pl.pallas_call(
        dispatch_kernel,
        out_shape=(
            jax.ShapeDtypeStruct((WIN, COLS), bf16),
            jax.ShapeDtypeStruct((N_GRP * CAP, NEAR), bf16),
            jax.ShapeDtypeStruct((N_Z, WIN, FAR), bf16),
        ),
        compiler_params=params(),
        name="dispatch",
    )(table, *parts)


def select_kernel(parts_ref, table_ref, out_ref):
    wide = jnp.concatenate([parts_ref[z] for z in range(N_Z)], axis=1)
    out_ref[...] = jnp.dot(table_ref[...], wide, preferred_element_type=f32).astype(bf16)


def select(parts, table):
    return pl.pallas_call(
        select_kernel,
        out_shape=jax.ShapeDtypeStruct((N_GRP * CAP, N_Z * FAR), bf16),
        compiler_params=params(),
        name="select",
    )(parts, table)


def experts_kernel(x_ref, rest_ref, gain_ref, wg_ref, wu_ref, wd_ref, by_z_ref, by_x_ref):
    tokens = x_ref.shape[1]
    squares = jnp.zeros((tokens, 128), f32)
    gate = jnp.zeros((tokens, HIDDEN), f32)
    up = jnp.zeros((tokens, HIDDEN), f32)
    contract = (((1,), (1,)), ((), ()))
    for z in range(N_Z):
        cols = slice(z * COLS, (z + 1) * COLS)
        far = rest_ref[:, z * FAR : (z + 1) * FAR]
        wide = jnp.concatenate([x_ref[z], far], axis=1).astype(f32)
        for b in range(COLS // 128):
            part = wide[:, b * 128 : (b + 1) * 128]
            squares = squares + part * part
        gained = (wide * gain_ref[:, cols]).astype(bf16)
        gate = gate + lax.dot_general(
            gained, wg_ref[:, cols], contract, preferred_element_type=f32
        )
        up = up + lax.dot_general(gained, wu_ref[:, cols], contract, preferred_element_type=f32)
    factor = lax.rsqrt(jnp.sum(squares, axis=1, keepdims=True) * (1.0 / D) + 1e-06)
    gate = gate * factor
    up = up * factor
    hidden = (gate / (1.0 + jnp.exp(-gate)) * up).astype(bf16)
    for z in range(N_Z):
        cols = slice(z * COLS, (z + 1) * COLS)
        done = jnp.dot(hidden, wd_ref[:, cols], preferred_element_type=f32).astype(bf16)
        by_z_ref[z] = done[:, :HALF]
        by_x_ref[:, z * HALF : (z + 1) * HALF] = done[:, HALF:]


def experts(x, rest, gain, w_gate, w_up, w_down, tile=256):
    tokens = x.shape[1]
    whole = pl.BlockSpec((HIDDEN, D), lambda i: (0, 0))
    return pl.pallas_call(
        experts_kernel,
        grid=(tokens // tile,),
        in_specs=[
            pl.BlockSpec((N_Z, tile, NEAR), lambda i: (0, i, 0)),
            pl.BlockSpec((tile, N_Z * FAR), lambda i: (i, 0)),
            pl.BlockSpec((1, D), lambda i: (0, 0)),
            whole,
            whole,
            whole,
        ],
        out_specs=[
            pl.BlockSpec((N_Z, tile, HALF), lambda i: (0, i, 0)),
            pl.BlockSpec((tile, D // 2), lambda i: (i, 0)),
        ],
        out_shape=[
            jax.ShapeDtypeStruct((N_Z, tokens, HALF), bf16),
            jax.ShapeDtypeStruct((tokens, D // 2), bf16),
        ],
        compiler_params=params(),
        name="experts",
    )(x, rest, gain, w_gate, w_up, w_down)


def mix_kernel(table_ref, parts_ref, out_ref):
    out_ref[...] = jnp.dot(
        table_ref[...], parts_ref[...], preferred_element_type=f32
    ).astype(bf16)


def mix(table, parts):
    tile = 1024
    return pl.pallas_call(
        mix_kernel,
        grid=(parts.shape[1] // tile,),
        in_specs=[
            pl.BlockSpec(table.shape, lambda i: (0, 0)),
            pl.BlockSpec((parts.shape[0], tile), lambda i: (0, i)),
        ],
        out_specs=pl.BlockSpec((WIN, tile), lambda i: (0, i)),
        out_shape=jax.ShapeDtypeStruct((WIN, parts.shape[1]), bf16),
        compiler_params=params(),
        cost_estimate=pl.CostEstimate(flops=1 << 28, bytes_accessed=4 << 20, transcendentals=0),
        name="mix",
    )(table, parts)


def mix_rest_kernel(table_ref, parts_ref, mixed_ref, *out_refs):
    rest = jnp.dot(table_ref[...], parts_ref[...], preferred_element_type=f32).astype(bf16)
    rows = WIN // N_Y
    for d, out_ref in enumerate(out_refs):
        out_ref[:, : D // 2] = mixed_ref[d * rows : (d + 1) * rows, :]
        out_ref[:, D // 2 :] = rest[d * rows : (d + 1) * rows]


def mix_rest(table, parts, mixed):
    return pl.pallas_call(
        mix_rest_kernel,
        out_shape=[jax.ShapeDtypeStruct((WIN // N_Y, D // 2 + HALF), bf16)] * N_Y,
        compiler_params=params(),
        name="mix_rest",
    )(table, parts, mixed)


def finish_kernel(in_ref, out_ref):
    summed = in_ref[0, :, : D // 2].astype(f32)
    for z in range(1, N_Z):
        summed = summed + in_ref[z, :, : D // 2].astype(f32)
    for z in range(N_Z):
        mine = in_ref[z, :, D // 2 :].astype(f32)
        first = mine[:, HALF : 2 * HALF] + mine[:, :HALF]
        second = mine[:, 2 * HALF :] + summed[:, z * HALF : (z + 1) * HALF]
        out_ref[:, z * COLS : z * COLS + HALF] = first.astype(bf16)
        out_ref[:, z * COLS + HALF : (z + 1) * COLS] = second.astype(bf16)


def finish(parts):
    return pl.pallas_call(
        finish_kernel,
        out_shape=jax.ShapeDtypeStruct((parts.shape[1], D), bf16),
        compiler_params=params(),
        name="finish",
    )(parts)


def over_y(value, d):
    return lax.ppermute(value, "y", [(i, (i + d) % N_Y) for i in range(N_Y)])


def per_device(
    queries,
    kv_cache,
    kv_scale,
    block_mask,
    resid,
    w_out,
    norm_gain,
    expert_ids,
    gate_weights,
    w_gate,
    w_up,
    w_down,
):
    y_pos = lax.axis_index("y")
    z_pos = lax.axis_index("z")

    chunks = dequantize(y_pos[None], kv_scale[0], kv_cache[0])
    kv_own = chunks[0]
    queries_mine = lax.all_to_all(
        jnp.broadcast_to(queries, (N_Z,) + queries.shape[1:]), "z", 0, 0, tiled=True
    )
    kv_from = {
        d: over_y(chunks[d], d) for d in (1, 3, 2)
    }

    blocks = CTX_LOCAL // BLOCK
    source = (y_pos - jnp.arange(N_Y, dtype=jnp.int32)) % N_Y
    mask = block_mask[0, 0].reshape(N_Y, N_Z, blocks)
    mask = lax.dynamic_slice_in_dim(mask, z_pos, 1, 1)[:, 0]
    mask = jnp.take(mask, source, axis=0)
    bias = jnp.where(mask == 1, 0.0, MASKED).astype(f32)
    bias = jnp.repeat(bias, BLOCK, axis=1)[:, None, :]
    last = ((source == N_Y - 1) & (z_pos == N_Z - 1)).astype(jnp.int32)

    rows = WIN // N_Y
    part = 2 * HEAD_DIM // N_GRP
    own_rows = resid.shape[1]
    grp_pos = lax.axis_index("x") * N_C + lax.axis_index("c")
    w_mine = lax.dynamic_slice_in_dim(w_out, grp_pos * part, part, 0)
    early = jnp.concatenate([w_mine, resid[0]], axis=0)
    early = early.reshape(part + own_rows, N_Z, COLS).transpose(1, 0, 2)
    early, queries_mine = lax.optimization_barrier((early, queries_mine))
    early = lax.all_to_all(early, "z", 0, 0, tiled=True)

    owners = jnp.arange(N_GRP, dtype=jnp.int32) * E_SUB + y_pos
    matches = expert_ids[0][None, :, :] == owners[:, None, None]
    chosen = jnp.any(matches, axis=-1)
    weight = jnp.sum(jnp.where(matches, gate_weights[0][None, :, :], 0.0), axis=-1)
    slot = jnp.cumsum(chosen.astype(jnp.int32), axis=1) - 1
    in_slot = chosen[:, None, :] & (
        slot[:, None, :] == jnp.arange(CAP, dtype=jnp.int32)[None, :, None]
    )
    out_table = in_slot.astype(bf16).reshape(N_GRP * CAP, WIN)
    back_table = jnp.where(in_slot, weight[:, None, :], 0.0).astype(bf16)
    back_table = back_table.reshape(N_GRP * CAP, WIN).T
    back_table = lax.dynamic_slice_in_dim(
        jnp.concatenate([back_table, back_table], axis=0), y_pos * rows, WIN, 0
    )

    acc, stat = own_attention(last, queries_mine, bias, kv_own)
    parts = rest_attention(
        last, queries_mine, bias, kv_from[1], kv_from[3], kv_from[2], acc, stat
    )
    parts, early = lax.optimization_barrier((parts, early))
    resid_rows = lax.dynamic_update_slice_in_dim(
        jnp.zeros((WIN, COLS), bf16), early[:, part:].reshape(rows, COLS), y_pos * rows, 0
    )
    w_cols = lax.all_gather(early[:, :part], ("x", "c"), axis=0, tiled=False)
    parts = lax.all_to_all(parts, "z", 0, 0, tiled=True)
    attended = lax.all_to_all(combine(parts), "z", 0, 0, tiled=True)
    projected = project(attended, w_cols, resid_rows)
    shifted = [over_y(projected, d) for d in (1, 2, 3)]
    stream, outgoing, spread = dispatch(out_table, projected, *shifted)

    arrivals = lax.all_to_all(
        outgoing.reshape(N_GRP, CAP, NEAR), ("x", "c"), 0, 0, tiled=True
    ).reshape(N_GRP * CAP, NEAR)
    arrivals, spread = lax.optimization_barrier((arrivals, spread))
    arrivals = lax.all_gather(arrivals, "z", axis=0, tiled=False)
    others = select(lax.all_to_all(spread, "z", 0, 0, tiled=True), out_table)
    others = lax.all_to_all(
        others.reshape(N_GRP, CAP, N_Z * FAR), ("x", "c"), 0, 0, tiled=True
    ).reshape(N_GRP * CAP, N_Z * FAR)
    by_z, by_x = experts(
        arrivals, others, norm_gain[None], w_gate[0], w_up[0], w_down[0]
    )
    by_z = lax.psum_scatter(
        by_z.reshape(N_Z * N_GRP * CAP, HALF), "z", scatter_dimension=0, tiled=True
    )
    by_x = lax.all_to_all(
        by_x.reshape(N_GRP, CAP, D // 2), ("x", "c"), 0, 0, tiled=True
    ).reshape(N_GRP * CAP, D // 2)
    mixed = mix(back_table, by_x)
    by_z, by_x = lax.optimization_barrier((by_z, by_x))
    by_z = lax.all_to_all(
        by_z.reshape(N_GRP, CAP, HALF), ("x", "c"), 0, 0, tiled=True
    ).reshape(N_GRP * CAP, HALF)
    mixture, *others = mix_rest(back_table, by_z, mixed)

    stream_rows = lax.dynamic_slice_in_dim(stream, y_pos * rows, rows, 0)
    mixture = mixture.astype(f32)
    for d, other in enumerate(others, 1):
        mixture = mixture + over_y(other, d).astype(f32)
    mixture = mixture.astype(bf16)
    tail = jnp.concatenate([mixture, stream_rows], axis=1).reshape(N_Z, own_rows, -1)
    return finish(lax.all_to_all(tail, "z", 0, 0, tiled=True))[None]


def solution(mesh):
    fine = Mesh(mesh.devices.reshape(N_Y, N_Z, N_X, N_C), ("y", "z", "x", "c"))
    seq, grp = ("y", "z"), ("x", "c")
    in_specs = (
        P(grp, None, seq),
        P(grp, seq, None),
        P(grp, seq, None),
        P(grp, None, None),
        P(grp, seq, None),
        P(seq, None),
        P(),
        P(grp, None, None),
        P(grp, None, None),
        P(grp, seq, None),
        P(grp, seq, None),
        P(grp, seq, None),
    )
    return jax.shard_map(
        per_device, mesh=fine, in_specs=in_specs, out_specs=P(grp, seq, None), check_vma=False
    )
```

```python
import math

import jax
import jax.numpy as jnp
from jax import lax
from jax.experimental import pallas as pl
from jax.experimental.pallas import tpu as pltpu
from jax.sharding import Mesh
from jax.sharding import PartitionSpec as P

HEADS = 64
KV_HEADS = 4
HEAD_DIM = 128
BLOCK = 128
E_SUB = 4
CAP = 64
N_Y, N_Z, N_X, N_C = 4, 8, 4, 2
N_GRP = N_X * N_C
WIN = 128
D = 4096
COLS = D // N_Z
HALF = COLS // 2
NEAR = 384
FAR = COLS - NEAR
CTX_LOCAL = 1024
HIDDEN = 192
STAT_ROWS = 16
PAIRS = 2
OWN_PAIRS = 4
MASKED = -1e30
SCALE2 = math.log2(math.e) / math.sqrt(HEAD_DIM)
MIB = 1024 * 1024

f32 = jnp.float32
bf16 = jnp.bfloat16


def params(mib=16):
    return pltpu.CompilerParams(vmem_limit_bytes=mib * MIB)


def dequantize_kernel(y_ref, scale_ref, cache_ref, *out_refs):
    step = pl.program_id(0)
    for d, out_ref in enumerate(out_refs):
        head = lax.rem(y_ref[0] + d, N_Y)
        for part in range(2):
            column = part * KV_HEADS + head
            lanes = pl.ds(pl.multiple_of(column * HEAD_DIM, HEAD_DIM), HEAD_DIM)
            for b in range(4):
                rows = slice(b * BLOCK, (b + 1) * BLOCK)
                raw = cache_ref[rows, lanes].astype(f32)
                out_ref[part, rows, :] = (raw * scale_ref[4 * step + b, column]).astype(bf16)


def dequantize(y_pos, scale, cache):
    shape = jax.ShapeDtypeStruct((2, CTX_LOCAL, HEAD_DIM), bf16)
    return pl.pallas_call(
        dequantize_kernel,
        grid_spec=pltpu.PrefetchScalarGridSpec(
            num_scalar_prefetch=2,
            grid=(CTX_LOCAL // (4 * BLOCK),),
            in_specs=[pl.BlockSpec((4 * BLOCK, 2 * KV_HEADS * HEAD_DIM), lambda i, *_: (i, 0))],
            out_specs=[pl.BlockSpec((2, 4 * BLOCK, HEAD_DIM), lambda i, *_: (0, i, 0))] * N_Y,
        ),
        out_shape=[shape] * N_Y,
        compiler_params=params(),
        cost_estimate=pl.CostEstimate(flops=1 << 20, bytes_accessed=4 << 20, transcendentals=0),
        name="dequantize",
    )(y_pos, scale, cache)


def attend_chunks(q_ref, kv_refs, bias_ref, last_ref, s_ref, pair, order):
    q_pair = jnp.concatenate([q_ref[pair, :, :HEAD_DIM], q_ref[pair, :, HEAD_DIM:]], axis=0)
    peak = jnp.full((2 * WIN, BLOCK), -jnp.inf, f32)
    row = lax.broadcasted_iota(jnp.int32, (2 * WIN, BLOCK), 0)
    row = jnp.where(row >= WIN, row - WIN, row)
    later = lax.broadcasted_iota(jnp.int32, (2 * WIN, BLOCK), 1) > row
    for i, (kv_ref, d) in enumerate(zip(kv_refs, order)):
        s = lax.dot_general(
            q_pair, kv_ref[0], (((1,), (1,)), ((), ())), preferred_element_type=f32
        )
        s = s + bias_ref[d]
        cut = jnp.where(later & (last_ref[d] == 1), MASKED, 0.0)
        end = CTX_LOCAL - BLOCK
        s_ref[pair, :, i * CTX_LOCAL : i * CTX_LOCAL + end] = s[:, :end]
        tail = s[:, end:] + cut
        s_ref[pair, :, i * CTX_LOCAL + end : (i + 1) * CTX_LOCAL] = tail
        for b in range(CTX_LOCAL // BLOCK - 1):
            peak = jnp.maximum(peak, s[:, b * BLOCK : (b + 1) * BLOCK])
        peak = jnp.maximum(peak, tail)
    return jnp.max(peak, axis=1, keepdims=True)


def weigh_chunks(kv_refs, s_ref, pair, m):
    total = jnp.zeros((2 * WIN, BLOCK), f32)
    acc = jnp.zeros((2 * WIN, HEAD_DIM), f32)
    for i, kv_ref in enumerate(kv_refs):
        s = s_ref[pair, :, i * CTX_LOCAL : (i + 1) * CTX_LOCAL]
        p = jnp.exp2((s - m) * SCALE2)
        for b in range(CTX_LOCAL // BLOCK):
            total = total + p[:, b * BLOCK : (b + 1) * BLOCK]
        acc = acc + jnp.dot(p.astype(bf16), kv_ref[1], preferred_element_type=f32)
    return jnp.sum(total, axis=1, keepdims=True), acc


def own_kernel(last_ref, q_ref, bias_ref, kv0, acc_ref, stat_ref, s_ref):
    lane = lax.broadcasted_iota(jnp.int32, (2 * WIN, 128), 1)
    maxima = [
        attend_chunks(q_ref, (kv0,), bias_ref, last_ref, s_ref, pair, (0,))
        for pair in range(OWN_PAIRS)
    ]
    for pair, m in enumerate(maxima):
        l, acc = weigh_chunks((kv0,), s_ref, pair, m)
        acc_ref[pair] = acc
        stat_ref[pair] = jnp.where(lane == 0, m, l)


def rest_kernel(last_ref, q_ref, bias_ref, kv1, kv3, kv2, acc_ref, stat_ref, out_ref, s_ref):
    kv_refs = (kv1, kv3, kv2)
    lane = lax.broadcasted_iota(jnp.int32, (2 * WIN, 128), 1)
    row = lax.broadcasted_iota(jnp.int32, (8, 2 * WIN), 0)
    maxima = [
        attend_chunks(q_ref, kv_refs, bias_ref, last_ref, s_ref, pair, (1, 3, 2))
        for pair in range(PAIRS)
    ]
    for pair, highest in enumerate(maxima):
        before = stat_ref[pair, :, :1]
        m = jnp.maximum(highest, before)
        l, acc = weigh_chunks(kv_refs, s_ref, pair, m)
        keep = jnp.exp2((before - m) * SCALE2)
        l = l + stat_ref[pair, :, 1:2] * keep
        out_ref[pair, : 2 * WIN, :] = (acc + acc_ref[pair] * keep).astype(bf16)
        turned = jnp.transpose(jnp.where(lane % 2 == 0, m, l))[:8]
        high = turned.astype(bf16).astype(f32)
        middle = (turned - high).astype(bf16).astype(f32)
        low = turned - high - middle
        rows = jnp.where(row < 2, high, jnp.where(row < 4, middle, low))
        out_ref[pair, 2 * WIN :, :] = jnp.concatenate(
            [rows[:, :WIN], rows[:, WIN:]], axis=0
        ).astype(bf16)


def attention_specs(extra, outs, chunks, pairs):
    whole = pl.BlockSpec((2, CTX_LOCAL, HEAD_DIM), lambda i, *_: (0, 0, 0))
    return pltpu.PrefetchScalarGridSpec(
        num_scalar_prefetch=1,
        grid=(N_Z // pairs,),
        in_specs=[
            pl.BlockSpec((pairs, WIN, 2 * HEAD_DIM), lambda i, *_: (i, 0, 0)),
            pl.BlockSpec((N_Y, 1, CTX_LOCAL), lambda i, *_: (0, 0, 0)),
        ]
        + [whole] * chunks
        + [pl.BlockSpec((pairs,) + e, lambda i, *_: (i, 0, 0)) for e in extra],
        out_specs=[pl.BlockSpec((pairs,) + o, lambda i, *_: (i, 0, 0)) for o in outs],
        scratch_shapes=[pltpu.VMEM((pairs, 2 * WIN, chunks * CTX_LOCAL), f32)],
    )


def own_attention(last, queries, bias, kv0):
    square = (2 * WIN, HEAD_DIM)
    return pl.pallas_call(
        own_kernel,
        grid_spec=attention_specs([], [square, square], 1, OWN_PAIRS),
        out_shape=[jax.ShapeDtypeStruct((N_Z,) + square, f32)] * 2,
        compiler_params=params(32),
        cost_estimate=pl.CostEstimate(
            flops=3 << 30, bytes_accessed=8 << 20, transcendentals=2 << 20
        ),
        name="own_attention",
    )(last, queries, bias, kv0)


def rest_attention(last, queries, bias, kv1, kv3, kv2, acc, stat):
    square = (2 * WIN, HEAD_DIM)
    message = (2 * WIN + STAT_ROWS, HEAD_DIM)
    return pl.pallas_call(
        rest_kernel,
        grid_spec=attention_specs([square, square], [message], 3, PAIRS),
        out_shape=[jax.ShapeDtypeStruct((N_Z,) + message, bf16)],
        compiler_params=params(32),
        cost_estimate=pl.CostEstimate(
            flops=8 << 30, bytes_accessed=8 << 20, transcendentals=6 << 20
        ),
        name="rest_attention",
    )(last, queries, bias, kv1, kv3, kv2, acc, stat)[0]


def combine_kernel(in_ref, out_ref):
    stats = in_ref[:, 2 * WIN :, :].astype(f32)
    for head in range(2):
        st = stats[:, 8 * head : 8 * head + 8]
        m = st[:, 0] + st[:, 2] + st[:, 4]
        l = st[:, 1] + st[:, 3] + st[:, 5]
        w = jnp.exp2((m - jnp.max(m, axis=0, keepdims=True)) * SCALE2)
        w = w / jnp.sum(w * l, axis=0, keepdims=True)
        wide = jnp.concatenate([w, jnp.zeros((WIN - N_Z, WIN), f32)], axis=0)
        cols = jnp.transpose(wide)
        total = jnp.zeros((WIN, HEAD_DIM), f32)
        for z in range(N_Z):
            part = in_ref[z, head * WIN : (head + 1) * WIN, :].astype(f32)
            total = total + part * cols[:, z : z + 1]
        done = total.astype(bf16)
        for z in range(N_Z):
            out_ref[z, :, head * HEAD_DIM : (head + 1) * HEAD_DIM] = done


def combine(parts):
    return pl.pallas_call(
        combine_kernel,
        out_shape=jax.ShapeDtypeStruct((N_Z, WIN, 2 * HEAD_DIM), bf16),
        compiler_params=params(),
        name="combine",
    )(parts)


def project_kernel(a_any, w_ref, resid_ref, out_ref, a_ref, sem):
    copy = pltpu.make_async_copy(a_any, a_ref, sem)
    copy.start()
    copy.wait()
    acc = resid_ref[...].astype(f32)
    for z in range(N_Z):
        w_rows = jnp.concatenate([w_ref[g, z] for g in range(N_GRP)], axis=0)
        acc = acc + jnp.dot(a_ref[z], w_rows, preferred_element_type=f32)
    out_ref[...] = acc.astype(bf16)


def project(attended, w_cols, resid_rows):
    return pl.pallas_call(
        project_kernel,
        out_shape=jax.ShapeDtypeStruct((WIN, COLS), bf16),
        in_specs=[pl.BlockSpec(memory_space=pl.ANY)] + [pl.BlockSpec(memory_space=pltpu.VMEM)] * 2,
        scratch_shapes=[pltpu.VMEM((N_Z, WIN, 2 * HEAD_DIM), bf16), pltpu.SemaphoreType.DMA],
        compiler_params=params(),
        name="project",
    )(attended, w_cols, resid_rows)


def dispatch_kernel(
    table_ref, own_ref, one_any, two_any, three_any, stream_ref, out_ref, spread_ref, *scratch
):
    one_ref, two_ref, three_ref, sems = scratch
    copies = [
        pltpu.make_async_copy(source, target, sems.at[i])
        for i, (source, target) in enumerate(
            ((one_any, one_ref), (two_any, two_ref), (three_any, three_ref))
        )
    ]
    for copy in copies:
        copy.start()
    for copy in copies:
        copy.wait()
    total = (own_ref[...].astype(f32) + two_ref[...].astype(f32)) + (
        one_ref[...].astype(f32) + three_ref[...].astype(f32)
    )
    stream = total.astype(bf16)
    stream_ref[...] = stream
    out_ref[...] = jnp.dot(
        table_ref[...], stream[:, :NEAR], preferred_element_type=f32
    ).astype(bf16)
    for z in range(N_Z):
        spread_ref[z] = stream[:, NEAR:]


def dispatch(table, *parts):
    return pl.pallas_call(
        dispatch_kernel,
        out_shape=(
            jax.ShapeDtypeStruct((WIN, COLS), bf16),
            jax.ShapeDtypeStruct((N_GRP * CAP, NEAR), bf16),
            jax.ShapeDtypeStruct((N_Z, WIN, FAR), bf16),
        ),
        in_specs=[pl.BlockSpec(memory_space=pltpu.VMEM)] * 2
        + [pl.BlockSpec(memory_space=pl.ANY)] * 3,
        scratch_shapes=[pltpu.VMEM((WIN, COLS), bf16)] * 3 + [pltpu.SemaphoreType.DMA((3,))],
        compiler_params=params(),
        name="dispatch",
    )(table, *parts)


def select_kernel(parts_ref, table_ref, out_ref):
    wide = jnp.concatenate([parts_ref[z] for z in range(N_Z)], axis=1)
    out_ref[...] = jnp.dot(table_ref[...], wide, preferred_element_type=f32).astype(bf16)


def select(parts, table):
    return pl.pallas_call(
        select_kernel,
        out_shape=jax.ShapeDtypeStruct((N_GRP * CAP, N_Z * FAR), bf16),
        compiler_params=params(),
        name="select",
    )(parts, table)


def experts_kernel(x_ref, rest_ref, gain_ref, wg_ref, wu_ref, wd_ref, by_z_ref, by_x_ref):
    tokens = x_ref.shape[1]
    squares = jnp.zeros((tokens, 128), f32)
    gate = jnp.zeros((tokens, HIDDEN), f32)
    up = jnp.zeros((tokens, HIDDEN), f32)
    contract = (((1,), (1,)), ((), ()))
    for z in range(N_Z):
        cols = slice(z * COLS, (z + 1) * COLS)
        far = rest_ref[:, z * FAR : (z + 1) * FAR]
        wide = jnp.concatenate([x_ref[z], far], axis=1).astype(f32)
        for b in range(COLS // 128):
            part = wide[:, b * 128 : (b + 1) * 128]
            squares = squares + part * part
        gained = (wide * gain_ref[:, cols]).astype(bf16)
        gate = gate + lax.dot_general(
            gained, wg_ref[:, cols], contract, preferred_element_type=f32
        )
        up = up + lax.dot_general(gained, wu_ref[:, cols], contract, preferred_element_type=f32)
    factor = lax.rsqrt(jnp.sum(squares, axis=1, keepdims=True) * (1.0 / D) + 1e-06)
    gate = gate * factor
    up = up * factor
    hidden = (gate / (1.0 + jnp.exp(-gate)) * up).astype(bf16)
    for z in range(N_Z):
        cols = slice(z * COLS, (z + 1) * COLS)
        done = jnp.dot(hidden, wd_ref[:, cols], preferred_element_type=f32).astype(bf16)
        by_z_ref[z] = done[:, :HALF]
        by_x_ref[:, z * HALF : (z + 1) * HALF] = done[:, HALF:]


def experts(x, rest, gain, w_gate, w_up, w_down, tile=256):
    tokens = x.shape[1]
    whole = pl.BlockSpec((HIDDEN, D), lambda i: (0, 0))
    return pl.pallas_call(
        experts_kernel,
        grid=(tokens // tile,),
        in_specs=[
            pl.BlockSpec((N_Z, tile, NEAR), lambda i: (0, i, 0)),
            pl.BlockSpec((tile, N_Z * FAR), lambda i: (i, 0)),
            pl.BlockSpec((1, D), lambda i: (0, 0)),
            whole,
            whole,
            whole,
        ],
        out_specs=[
            pl.BlockSpec((N_Z, tile, HALF), lambda i: (0, i, 0)),
            pl.BlockSpec((tile, D // 2), lambda i: (i, 0)),
        ],
        out_shape=[
            jax.ShapeDtypeStruct((N_Z, tokens, HALF), bf16),
            jax.ShapeDtypeStruct((tokens, D // 2), bf16),
        ],
        compiler_params=params(40),
        name="experts",
    )(x, rest, gain, w_gate, w_up, w_down)


def mix_kernel(table_ref, parts_ref, out_ref):
    out_ref[...] = jnp.dot(
        table_ref[...], parts_ref[...], preferred_element_type=f32
    ).astype(bf16)


def mix(table, parts):
    tile = 1024
    return pl.pallas_call(
        mix_kernel,
        grid=(parts.shape[1] // tile,),
        in_specs=[
            pl.BlockSpec(table.shape, lambda i: (0, 0)),
            pl.BlockSpec((parts.shape[0], tile), lambda i: (0, i)),
        ],
        out_specs=pl.BlockSpec((WIN, tile), lambda i: (0, i)),
        out_shape=jax.ShapeDtypeStruct((WIN, parts.shape[1]), bf16),
        compiler_params=params(),
        cost_estimate=pl.CostEstimate(flops=1 << 28, bytes_accessed=4 << 20, transcendentals=0),
        name="mix",
    )(table, parts)


def mix_rest_kernel(table_ref, parts_any, mixed_ref, *refs):
    *out_refs, parts_ref, sem = refs
    copy = pltpu.make_async_copy(parts_any, parts_ref, sem)
    copy.start()
    copy.wait()
    rest = jnp.dot(table_ref[...], parts_ref[...], preferred_element_type=f32).astype(bf16)
    rows = WIN // N_Y
    for d, out_ref in enumerate(out_refs):
        out_ref[:, : D // 2] = mixed_ref[d * rows : (d + 1) * rows, :]
        out_ref[:, D // 2 :] = rest[d * rows : (d + 1) * rows]


def mix_rest(table, parts, mixed):
    return pl.pallas_call(
        mix_rest_kernel,
        out_shape=[jax.ShapeDtypeStruct((WIN // N_Y, D // 2 + HALF), bf16)] * N_Y,
        in_specs=[
            pl.BlockSpec(memory_space=pltpu.VMEM),
            pl.BlockSpec(memory_space=pl.ANY),
            pl.BlockSpec(memory_space=pltpu.VMEM),
        ],
        scratch_shapes=[pltpu.VMEM((N_GRP * CAP, HALF), bf16), pltpu.SemaphoreType.DMA],
        compiler_params=params(),
        name="mix_rest",
    )(table, parts, mixed)


def finish_kernel(in_ref, out_ref):
    summed = in_ref[0, :, : D // 2].astype(f32)
    for z in range(1, N_Z):
        summed = summed + in_ref[z, :, : D // 2].astype(f32)
    for z in range(N_Z):
        mine = in_ref[z, :, D // 2 :].astype(f32)
        first = mine[:, HALF : 2 * HALF] + mine[:, :HALF]
        second = mine[:, 2 * HALF :] + summed[:, z * HALF : (z + 1) * HALF]
        out_ref[:, z * COLS : z * COLS + HALF] = first.astype(bf16)
        out_ref[:, z * COLS + HALF : (z + 1) * COLS] = second.astype(bf16)


def finish(parts):
    return pl.pallas_call(
        finish_kernel,
        out_shape=jax.ShapeDtypeStruct((parts.shape[1], D), bf16),
        compiler_params=params(),
        name="finish",
    )(parts)


def over_y(value, d):
    return lax.ppermute(value, "y", [(i, (i + d) % N_Y) for i in range(N_Y)])


def per_device(
    queries,
    kv_cache,
    kv_scale,
    block_mask,
    resid,
    w_out,
    norm_gain,
    expert_ids,
    gate_weights,
    w_gate,
    w_up,
    w_down,
):
    y_pos = lax.axis_index("y")
    z_pos = lax.axis_index("z")

    chunks = dequantize(y_pos[None], kv_scale[0], kv_cache[0])
    kv_own = chunks[0]
    queries_mine = lax.all_to_all(
        jnp.broadcast_to(queries, (N_Z,) + queries.shape[1:]), "z", 0, 0, tiled=True
    )
    kv_from = {
        d: over_y(chunks[d], d) for d in (1, 3, 2)
    }

    blocks = CTX_LOCAL // BLOCK
    source = (y_pos - jnp.arange(N_Y, dtype=jnp.int32)) % N_Y
    mask = block_mask[0, 0].reshape(N_Y, N_Z, blocks)
    mask = lax.dynamic_slice_in_dim(mask, z_pos, 1, 1)[:, 0]
    mask = jnp.take(mask, source, axis=0)
    bias = jnp.where(mask == 1, 0.0, MASKED).astype(f32)
    bias = jnp.repeat(bias, BLOCK, axis=1)[:, None, :]
    last = ((source == N_Y - 1) & (z_pos == N_Z - 1)).astype(jnp.int32)

    rows = WIN // N_Y
    part = 2 * HEAD_DIM // N_GRP
    own_rows = resid.shape[1]
    grp_pos = lax.axis_index("x") * N_C + lax.axis_index("c")
    w_mine = lax.dynamic_slice_in_dim(w_out, grp_pos * part, part, 0)
    early = jnp.concatenate([w_mine, resid[0]], axis=0)
    early = early.reshape(part + own_rows, N_Z, COLS).transpose(1, 0, 2)
    early, queries_mine = lax.optimization_barrier((early, queries_mine))
    early = lax.all_to_all(early, "z", 0, 0, tiled=True)

    owners = jnp.arange(N_GRP, dtype=jnp.int32) * E_SUB + y_pos
    matches = expert_ids[0][None, :, :] == owners[:, None, None]
    chosen = jnp.any(matches, axis=-1)
    weight = jnp.sum(jnp.where(matches, gate_weights[0][None, :, :], 0.0), axis=-1)
    slot = jnp.cumsum(chosen.astype(jnp.int32), axis=1) - 1
    in_slot = chosen[:, None, :] & (
        slot[:, None, :] == jnp.arange(CAP, dtype=jnp.int32)[None, :, None]
    )
    out_table = in_slot.astype(bf16).reshape(N_GRP * CAP, WIN)
    back_table = jnp.where(in_slot, weight[:, None, :], 0.0).astype(bf16)
    back_table = back_table.reshape(N_GRP * CAP, WIN).T
    back_table = lax.dynamic_slice_in_dim(
        jnp.concatenate([back_table, back_table], axis=0), y_pos * rows, WIN, 0
    )

    acc, stat = own_attention(last, queries_mine, bias, kv_own)
    stat, early = lax.optimization_barrier((stat, early))
    parts = rest_attention(
        last, queries_mine, bias, kv_from[1], kv_from[3], kv_from[2], acc, stat
    )
    resid_rows = lax.dynamic_update_slice_in_dim(
        jnp.zeros((WIN, COLS), bf16), early[:, part:].reshape(rows, COLS), y_pos * rows, 0
    )
    w_cols = lax.all_gather(early[:, :part], ("x", "c"), axis=0, tiled=False)
    parts = lax.all_to_all(parts, "z", 0, 0, tiled=True)
    attended = lax.all_to_all(combine(parts), "z", 0, 0, tiled=True)
    projected = project(attended, w_cols, resid_rows)
    shifted = [over_y(projected, d) for d in (1, 2, 3)]
    stream, outgoing, spread = dispatch(out_table, projected, *shifted)

    arrivals = lax.all_to_all(
        outgoing.reshape(N_GRP, CAP, NEAR), ("x", "c"), 0, 0, tiled=True
    ).reshape(N_GRP * CAP, NEAR)
    arrivals, spread = lax.optimization_barrier((arrivals, spread))
    arrivals = lax.all_gather(arrivals, "z", axis=0, tiled=False)
    others = select(lax.all_to_all(spread, "z", 0, 0, tiled=True), out_table)
    others = lax.all_to_all(
        others.reshape(N_GRP, CAP, N_Z * FAR), ("x", "c"), 0, 0, tiled=True
    ).reshape(N_GRP * CAP, N_Z * FAR)
    by_z, by_x = experts(
        arrivals, others, norm_gain[None], w_gate[0], w_up[0], w_down[0]
    )
    by_z = lax.psum_scatter(
        by_z.reshape(N_Z * N_GRP * CAP, HALF), "z", scatter_dimension=0, tiled=True
    )
    by_x = lax.all_to_all(
        by_x.reshape(N_GRP, CAP, D // 2), ("x", "c"), 0, 0, tiled=True
    ).reshape(N_GRP * CAP, D // 2)
    mixed = mix(back_table, by_x)
    by_z, by_x = lax.optimization_barrier((by_z, by_x))
    by_z = lax.all_to_all(
        by_z.reshape(N_GRP, CAP, HALF), ("x", "c"), 0, 0, tiled=True
    ).reshape(N_GRP * CAP, HALF)
    mixture, *others = mix_rest(back_table, by_z, mixed)

    stream_rows = lax.dynamic_slice_in_dim(stream, y_pos * rows, rows, 0)
    mixture = mixture.astype(f32)
    for d, other in enumerate(others, 1):
        mixture = mixture + over_y(other, d).astype(f32)
    mixture = mixture.astype(bf16)
    tail = jnp.concatenate([mixture, stream_rows], axis=1).reshape(N_Z, own_rows, -1)
    return finish(lax.all_to_all(tail, "z", 0, 0, tiled=True))[None]


def solution(mesh):
    fine = Mesh(mesh.devices.reshape(N_Y, N_Z, N_X, N_C), ("y", "z", "x", "c"))
    seq, grp = ("y", "z"), ("x", "c")
    in_specs = (
        P(grp, None, seq),
        P(grp, seq, None),
        P(grp, seq, None),
        P(grp, None, None),
        P(grp, seq, None),
        P(seq, None),
        P(),
        P(grp, None, None),
        P(grp, None, None),
        P(grp, seq, None),
        P(grp, seq, None),
        P(grp, seq, None),
    )
    return jax.shard_map(
        per_device, mesh=fine, in_specs=in_specs, out_specs=P(grp, seq, None), check_vma=False
    )
```

```python
import math

import jax
import jax.numpy as jnp
from jax import lax
from jax.experimental import pallas as pl
from jax.experimental.pallas import tpu as pltpu
from jax.sharding import Mesh
from jax.sharding import PartitionSpec as P

HEADS = 64
KV_HEADS = 4
HEAD_DIM = 128
BLOCK = 128
E_SUB = 4
CAP = 64
N_Y, N_Z, N_X, N_C = 4, 8, 4, 2
N_GRP = N_X * N_C
WIN = 128
D = 4096
COLS = D // N_Z
HALF = COLS // 2
NEAR = 384
FAR = COLS - NEAR
CTX_LOCAL = 1024
HIDDEN = 192
STAT_ROWS = 16
PAIRS = 2
OWN_PAIRS = 4
MASKED = -1e30
SCALE2 = math.log2(math.e) / math.sqrt(HEAD_DIM)
MIB = 1024 * 1024

f32 = jnp.float32
bf16 = jnp.bfloat16


def params(mib=16):
    return pltpu.CompilerParams(vmem_limit_bytes=mib * MIB)


def dequantize_kernel(y_ref, scale_ref, cache_ref, *out_refs):
    step = pl.program_id(0)
    for d, out_ref in enumerate(out_refs):
        head = lax.rem(y_ref[0] + d, N_Y)
        for part in range(2):
            column = part * KV_HEADS + head
            lanes = pl.ds(pl.multiple_of(column * HEAD_DIM, HEAD_DIM), HEAD_DIM)
            for b in range(4):
                rows = slice(b * BLOCK, (b + 1) * BLOCK)
                raw = cache_ref[rows, lanes].astype(f32)
                out_ref[part, rows, :] = (raw * scale_ref[4 * step + b, column]).astype(bf16)


def dequantize(y_pos, scale, cache):
    shape = jax.ShapeDtypeStruct((2, CTX_LOCAL, HEAD_DIM), bf16)
    return pl.pallas_call(
        dequantize_kernel,
        grid_spec=pltpu.PrefetchScalarGridSpec(
            num_scalar_prefetch=2,
            grid=(CTX_LOCAL // (4 * BLOCK),),
            in_specs=[pl.BlockSpec((4 * BLOCK, 2 * KV_HEADS * HEAD_DIM), lambda i, *_: (i, 0))],
            out_specs=[pl.BlockSpec((2, 4 * BLOCK, HEAD_DIM), lambda i, *_: (0, i, 0))] * N_Y,
        ),
        out_shape=[shape] * N_Y,
        compiler_params=params(56),
        cost_estimate=pl.CostEstimate(flops=1 << 20, bytes_accessed=4 << 20, transcendentals=0),
        name="dequantize",
    )(y_pos, scale, cache)


def attend_chunks(q_ref, kv_refs, bias_ref, last_ref, s_ref, pair, order):
    q_pair = jnp.concatenate([q_ref[pair, :, :HEAD_DIM], q_ref[pair, :, HEAD_DIM:]], axis=0)
    peak = jnp.full((2 * WIN, BLOCK), -jnp.inf, f32)
    row = lax.broadcasted_iota(jnp.int32, (2 * WIN, BLOCK), 0)
    row = jnp.where(row >= WIN, row - WIN, row)
    later = lax.broadcasted_iota(jnp.int32, (2 * WIN, BLOCK), 1) > row
    for i, (kv_ref, d) in enumerate(zip(kv_refs, order)):
        s = lax.dot_general(
            q_pair, kv_ref[0], (((1,), (1,)), ((), ())), preferred_element_type=f32
        )
        s = s + bias_ref[d]
        cut = jnp.where(later & (last_ref[d] == 1), MASKED, 0.0)
        end = CTX_LOCAL - BLOCK
        s_ref[pair, :, i * CTX_LOCAL : i * CTX_LOCAL + end] = s[:, :end]
        tail = s[:, end:] + cut
        s_ref[pair, :, i * CTX_LOCAL + end : (i + 1) * CTX_LOCAL] = tail
        for b in range(CTX_LOCAL // BLOCK - 1):
            peak = jnp.maximum(peak, s[:, b * BLOCK : (b + 1) * BLOCK])
        peak = jnp.maximum(peak, tail)
    return jnp.max(peak, axis=1, keepdims=True)


def weigh_chunks(kv_refs, s_ref, pair, m):
    total = jnp.zeros((2 * WIN, BLOCK), f32)
    acc = jnp.zeros((2 * WIN, HEAD_DIM), f32)
    for i, kv_ref in enumerate(kv_refs):
        s = s_ref[pair, :, i * CTX_LOCAL : (i + 1) * CTX_LOCAL]
        p = jnp.exp2((s - m) * SCALE2)
        for b in range(CTX_LOCAL // BLOCK):
            total = total + p[:, b * BLOCK : (b + 1) * BLOCK]
        acc = acc + jnp.dot(p.astype(bf16), kv_ref[1], preferred_element_type=f32)
    return jnp.sum(total, axis=1, keepdims=True), acc


def own_kernel(last_ref, q_ref, bias_ref, kv0, acc_ref, stat_ref, s_ref):
    lane = lax.broadcasted_iota(jnp.int32, (2 * WIN, 128), 1)
    maxima = [
        attend_chunks(q_ref, (kv0,), bias_ref, last_ref, s_ref, pair, (0,))
        for pair in range(OWN_PAIRS)
    ]
    for pair, m in enumerate(maxima):
        l, acc = weigh_chunks((kv0,), s_ref, pair, m)
        acc_ref[pair] = acc
        stat_ref[pair] = jnp.where(lane == 0, m, l)


def rest_kernel(last_ref, q_ref, bias_ref, kv1, kv3, kv2, acc_ref, stat_ref, out_ref, s_ref):
    kv_refs = (kv1, kv3, kv2)
    lane = lax.broadcasted_iota(jnp.int32, (2 * WIN, 128), 1)
    row = lax.broadcasted_iota(jnp.int32, (8, 2 * WIN), 0)
    maxima = [
        attend_chunks(q_ref, kv_refs, bias_ref, last_ref, s_ref, pair, (1, 3, 2))
        for pair in range(PAIRS)
    ]
    for pair, highest in enumerate(maxima):
        before = stat_ref[pair, :, :1]
        m = jnp.maximum(highest, before)
        l, acc = weigh_chunks(kv_refs, s_ref, pair, m)
        keep = jnp.exp2((before - m) * SCALE2)
        l = l + stat_ref[pair, :, 1:2] * keep
        out_ref[pair, : 2 * WIN, :] = (acc + acc_ref[pair] * keep).astype(bf16)
        turned = jnp.transpose(jnp.where(lane % 2 == 0, m, l))[:8]
        high = turned.astype(bf16).astype(f32)
        middle = (turned - high).astype(bf16).astype(f32)
        low = turned - high - middle
        rows = jnp.where(row < 2, high, jnp.where(row < 4, middle, low))
        out_ref[pair, 2 * WIN :, :] = jnp.concatenate(
            [rows[:, :WIN], rows[:, WIN:]], axis=0
        ).astype(bf16)


def attention_specs(extra, outs, chunks, pairs):
    whole = pl.BlockSpec((2, CTX_LOCAL, HEAD_DIM), lambda i, *_: (0, 0, 0))
    return pltpu.PrefetchScalarGridSpec(
        num_scalar_prefetch=1,
        grid=(N_Z // pairs,),
        in_specs=[
            pl.BlockSpec((pairs, WIN, 2 * HEAD_DIM), lambda i, *_: (i, 0, 0)),
            pl.BlockSpec((N_Y, 1, CTX_LOCAL), lambda i, *_: (0, 0, 0)),
        ]
        + [whole] * chunks
        + [pl.BlockSpec((pairs,) + e, lambda i, *_: (i, 0, 0)) for e in extra],
        out_specs=[pl.BlockSpec((pairs,) + o, lambda i, *_: (i, 0, 0)) for o in outs],
        scratch_shapes=[pltpu.VMEM((pairs, 2 * WIN, chunks * CTX_LOCAL), f32)],
    )


def own_attention(last, queries, bias, kv0):
    square = (2 * WIN, HEAD_DIM)
    return pl.pallas_call(
        own_kernel,
        grid_spec=attention_specs([], [square, square], 1, OWN_PAIRS),
        out_shape=[jax.ShapeDtypeStruct((N_Z,) + square, f32)] * 2,
        compiler_params=params(32),
        cost_estimate=pl.CostEstimate(
            flops=3 << 30, bytes_accessed=8 << 20, transcendentals=2 << 20
        ),
        name="own_attention",
    )(last, queries, bias, kv0)


def rest_attention(last, queries, bias, kv1, kv3, kv2, acc, stat):
    square = (2 * WIN, HEAD_DIM)
    message = (2 * WIN + STAT_ROWS, HEAD_DIM)
    return pl.pallas_call(
        rest_kernel,
        grid_spec=attention_specs([square, square], [message], 3, PAIRS),
        out_shape=[jax.ShapeDtypeStruct((N_Z,) + message, bf16)],
        compiler_params=params(32),
        cost_estimate=pl.CostEstimate(
            flops=8 << 30, bytes_accessed=8 << 20, transcendentals=6 << 20
        ),
        name="rest_attention",
    )(last, queries, bias, kv1, kv3, kv2, acc, stat)[0]


def combine_kernel(in_ref, out_ref):
    stats = in_ref[:, 2 * WIN :, :].astype(f32)
    for head in range(2):
        st = stats[:, 8 * head : 8 * head + 8]
        m = st[:, 0] + st[:, 2] + st[:, 4]
        l = st[:, 1] + st[:, 3] + st[:, 5]
        w = jnp.exp2((m - jnp.max(m, axis=0, keepdims=True)) * SCALE2)
        w = w / jnp.sum(w * l, axis=0, keepdims=True)
        wide = jnp.concatenate([w, jnp.zeros((WIN - N_Z, WIN), f32)], axis=0)
        cols = jnp.transpose(wide)
        total = jnp.zeros((WIN, HEAD_DIM), f32)
        for z in range(N_Z):
            part = in_ref[z, head * WIN : (head + 1) * WIN, :].astype(f32)
            total = total + part * cols[:, z : z + 1]
        done = total.astype(bf16)
        for z in range(N_Z):
            out_ref[z, :, head * HEAD_DIM : (head + 1) * HEAD_DIM] = done


def combine(parts):
    return pl.pallas_call(
        combine_kernel,
        out_shape=jax.ShapeDtypeStruct((N_Z, WIN, 2 * HEAD_DIM), bf16),
        compiler_params=params(),
        name="combine",
    )(parts)


def project_kernel(a_any, w_ref, resid_ref, out_ref, a_ref, sem):
    copy = pltpu.make_async_copy(a_any, a_ref, sem)
    copy.start()
    copy.wait()
    acc = resid_ref[...].astype(f32)
    for z in range(N_Z):
        w_rows = jnp.concatenate([w_ref[g, z] for g in range(N_GRP)], axis=0)
        acc = acc + jnp.dot(a_ref[z], w_rows, preferred_element_type=f32)
    out_ref[...] = acc.astype(bf16)


def project(attended, w_cols, resid_rows):
    return pl.pallas_call(
        project_kernel,
        out_shape=jax.ShapeDtypeStruct((WIN, COLS), bf16),
        in_specs=[pl.BlockSpec(memory_space=pl.ANY)] + [pl.BlockSpec(memory_space=pltpu.VMEM)] * 2,
        scratch_shapes=[pltpu.VMEM((N_Z, WIN, 2 * HEAD_DIM), bf16), pltpu.SemaphoreType.DMA],
        compiler_params=params(),
        name="project",
    )(attended, w_cols, resid_rows)


def dispatch_kernel(
    table_ref, own_ref, one_any, two_any, three_any, stream_ref, out_ref, spread_ref, *scratch
):
    one_ref, two_ref, three_ref, sems = scratch
    copies = [
        pltpu.make_async_copy(source, target, sems.at[i])
        for i, (source, target) in enumerate(
            ((one_any, one_ref), (two_any, two_ref), (three_any, three_ref))
        )
    ]
    for copy in copies:
        copy.start()
    for copy in copies:
        copy.wait()
    total = (own_ref[...].astype(f32) + two_ref[...].astype(f32)) + (
        one_ref[...].astype(f32) + three_ref[...].astype(f32)
    )
    stream = total.astype(bf16)
    stream_ref[...] = stream
    out_ref[...] = jnp.dot(
        table_ref[...], stream[:, :NEAR], preferred_element_type=f32
    ).astype(bf16)
    for z in range(N_Z):
        spread_ref[z] = stream[:, NEAR:]


def dispatch(table, *parts):
    return pl.pallas_call(
        dispatch_kernel,
        out_shape=(
            jax.ShapeDtypeStruct((WIN, COLS), bf16),
            jax.ShapeDtypeStruct((N_GRP * CAP, NEAR), bf16),
            jax.ShapeDtypeStruct((N_Z, WIN, FAR), bf16),
        ),
        in_specs=[pl.BlockSpec(memory_space=pltpu.VMEM)] * 2
        + [pl.BlockSpec(memory_space=pl.ANY)] * 3,
        scratch_shapes=[pltpu.VMEM((WIN, COLS), bf16)] * 3 + [pltpu.SemaphoreType.DMA((3,))],
        compiler_params=params(),
        name="dispatch",
    )(table, *parts)


def select_kernel(parts_ref, table_ref, out_ref):
    wide = jnp.concatenate([parts_ref[z] for z in range(N_Z)], axis=1)
    out_ref[...] = jnp.dot(table_ref[...], wide, preferred_element_type=f32).astype(bf16)


def select(parts, table):
    return pl.pallas_call(
        select_kernel,
        out_shape=jax.ShapeDtypeStruct((N_GRP * CAP, N_Z * FAR), bf16),
        compiler_params=params(),
        name="select",
    )(parts, table)


def experts_kernel(x_ref, rest_ref, gain_ref, wg_ref, wu_ref, wd_ref, by_z_ref, by_x_ref):
    tokens = x_ref.shape[1]
    squares = jnp.zeros((tokens, 128), f32)
    gate = jnp.zeros((tokens, HIDDEN), f32)
    up = jnp.zeros((tokens, HIDDEN), f32)
    contract = (((1,), (1,)), ((), ()))
    for z in range(N_Z):
        cols = slice(z * COLS, (z + 1) * COLS)
        far = rest_ref[:, z * FAR : (z + 1) * FAR]
        wide = jnp.concatenate([x_ref[z], far], axis=1).astype(f32)
        for b in range(COLS // 128):
            part = wide[:, b * 128 : (b + 1) * 128]
            squares = squares + part * part
        gained = (wide * gain_ref[:, cols]).astype(bf16)
        gate = gate + lax.dot_general(
            gained, wg_ref[:, cols], contract, preferred_element_type=f32
        )
        up = up + lax.dot_general(gained, wu_ref[:, cols], contract, preferred_element_type=f32)
    factor = lax.rsqrt(jnp.sum(squares, axis=1, keepdims=True) * (1.0 / D) + 1e-06)
    gate = gate * factor
    up = up * factor
    hidden = (gate / (1.0 + jnp.exp(-gate)) * up).astype(bf16)
    for z in range(N_Z):
        cols = slice(z * COLS, (z + 1) * COLS)
        done = jnp.dot(hidden, wd_ref[:, cols], preferred_element_type=f32).astype(bf16)
        by_z_ref[z] = done[:, :HALF]
        by_x_ref[:, z * HALF : (z + 1) * HALF] = done[:, HALF:]


def experts(x, rest, gain, w_gate, w_up, w_down, tile=256):
    tokens = x.shape[1]
    whole = pl.BlockSpec((HIDDEN, D), lambda i: (0, 0))
    return pl.pallas_call(
        experts_kernel,
        grid=(tokens // tile,),
        in_specs=[
            pl.BlockSpec((N_Z, tile, NEAR), lambda i: (0, i, 0)),
            pl.BlockSpec((tile, N_Z * FAR), lambda i: (i, 0)),
            pl.BlockSpec((1, D), lambda i: (0, 0)),
            whole,
            whole,
            whole,
        ],
        out_specs=[
            pl.BlockSpec((N_Z, tile, HALF), lambda i: (0, i, 0)),
            pl.BlockSpec((tile, D // 2), lambda i: (i, 0)),
        ],
        out_shape=[
            jax.ShapeDtypeStruct((N_Z, tokens, HALF), bf16),
            jax.ShapeDtypeStruct((tokens, D // 2), bf16),
        ],
        compiler_params=params(56),
        name="experts",
    )(x, rest, gain, w_gate, w_up, w_down)


def mix_kernel(table_ref, parts_ref, out_ref):
    out_ref[...] = jnp.dot(
        table_ref[...], parts_ref[...], preferred_element_type=f32
    ).astype(bf16)


def mix(table, parts):
    tile = 1024
    return pl.pallas_call(
        mix_kernel,
        grid=(parts.shape[1] // tile,),
        in_specs=[
            pl.BlockSpec(table.shape, lambda i: (0, 0)),
            pl.BlockSpec((parts.shape[0], tile), lambda i: (0, i)),
        ],
        out_specs=pl.BlockSpec((WIN, tile), lambda i: (0, i)),
        out_shape=jax.ShapeDtypeStruct((WIN, parts.shape[1]), bf16),
        compiler_params=params(),
        cost_estimate=pl.CostEstimate(flops=1 << 28, bytes_accessed=4 << 20, transcendentals=0),
        name="mix",
    )(table, parts)


def mix_rest_kernel(table_ref, parts_any, mixed_ref, *refs):
    *out_refs, parts_ref, sem = refs
    copy = pltpu.make_async_copy(parts_any, parts_ref, sem)
    copy.start()
    copy.wait()
    rest = jnp.dot(table_ref[...], parts_ref[...], preferred_element_type=f32).astype(bf16)
    rows = WIN // N_Y
    for d, out_ref in enumerate(out_refs):
        out_ref[:, : D // 2] = mixed_ref[d * rows : (d + 1) * rows, :]
        out_ref[:, D // 2 :] = rest[d * rows : (d + 1) * rows]


def mix_rest(table, parts, mixed):
    return pl.pallas_call(
        mix_rest_kernel,
        out_shape=[jax.ShapeDtypeStruct((WIN // N_Y, D // 2 + HALF), bf16)] * N_Y,
        in_specs=[
            pl.BlockSpec(memory_space=pltpu.VMEM),
            pl.BlockSpec(memory_space=pl.ANY),
            pl.BlockSpec(memory_space=pltpu.VMEM),
        ],
        scratch_shapes=[pltpu.VMEM((N_GRP * CAP, HALF), bf16), pltpu.SemaphoreType.DMA],
        compiler_params=params(),
        name="mix_rest",
    )(table, parts, mixed)


def finish_kernel(in_ref, out_ref):
    summed = in_ref[0, :, : D // 2].astype(f32)
    for z in range(1, N_Z):
        summed = summed + in_ref[z, :, : D // 2].astype(f32)
    for z in range(N_Z):
        mine = in_ref[z, :, D // 2 :].astype(f32)
        first = mine[:, HALF : 2 * HALF] + mine[:, :HALF]
        second = mine[:, 2 * HALF :] + summed[:, z * HALF : (z + 1) * HALF]
        out_ref[:, z * COLS : z * COLS + HALF] = first.astype(bf16)
        out_ref[:, z * COLS + HALF : (z + 1) * COLS] = second.astype(bf16)


def finish(parts):
    return pl.pallas_call(
        finish_kernel,
        out_shape=jax.ShapeDtypeStruct((parts.shape[1], D), bf16),
        compiler_params=params(),
        name="finish",
    )(parts)


def over_y(value, d):
    return lax.ppermute(value, "y", [(i, (i + d) % N_Y) for i in range(N_Y)])


def per_device(
    queries,
    kv_cache,
    kv_scale,
    block_mask,
    resid,
    w_out,
    norm_gain,
    expert_ids,
    gate_weights,
    w_gate,
    w_up,
    w_down,
):
    y_pos = lax.axis_index("y")
    z_pos = lax.axis_index("z")

    chunks = dequantize(y_pos[None], kv_scale[0], kv_cache[0])
    kv_own = chunks[0]
    queries_mine = lax.all_to_all(
        jnp.broadcast_to(queries, (N_Z,) + queries.shape[1:]), "z", 0, 0, tiled=True
    )
    kv_from = {
        d: over_y(chunks[d], d) for d in (1, 3, 2)
    }

    blocks = CTX_LOCAL // BLOCK
    source = (y_pos - jnp.arange(N_Y, dtype=jnp.int32)) % N_Y
    mask = block_mask[0, 0].reshape(N_Y, N_Z, blocks)
    mask = lax.dynamic_slice_in_dim(mask, z_pos, 1, 1)[:, 0]
    mask = jnp.take(mask, source, axis=0)
    bias = jnp.where(mask == 1, 0.0, MASKED).astype(f32)
    bias = jnp.repeat(bias, BLOCK, axis=1)[:, None, :]
    last = ((source == N_Y - 1) & (z_pos == N_Z - 1)).astype(jnp.int32)

    rows = WIN // N_Y
    part = 2 * HEAD_DIM // N_GRP
    own_rows = resid.shape[1]
    grp_pos = lax.axis_index("x") * N_C + lax.axis_index("c")
    w_mine = lax.dynamic_slice_in_dim(w_out, grp_pos * part, part, 0)
    early = jnp.concatenate([w_mine, resid[0]], axis=0)
    early = early.reshape(part + own_rows, N_Z, COLS).transpose(1, 0, 2)
    early, queries_mine = lax.optimization_barrier((early, queries_mine))
    early = lax.all_to_all(early, "z", 0, 0, tiled=True)

    owners = jnp.arange(N_GRP, dtype=jnp.int32) * E_SUB + y_pos
    matches = expert_ids[0][None, :, :] == owners[:, None, None]
    chosen = jnp.any(matches, axis=-1)
    weight = jnp.sum(jnp.where(matches, gate_weights[0][None, :, :], 0.0), axis=-1)
    slot = jnp.cumsum(chosen.astype(jnp.int32), axis=1) - 1
    in_slot = chosen[:, None, :] & (
        slot[:, None, :] == jnp.arange(CAP, dtype=jnp.int32)[None, :, None]
    )
    out_table = in_slot.astype(bf16).reshape(N_GRP * CAP, WIN)
    back_table = jnp.where(in_slot, weight[:, None, :], 0.0).astype(bf16)
    back_table = back_table.reshape(N_GRP * CAP, WIN).T
    back_table = lax.dynamic_slice_in_dim(
        jnp.concatenate([back_table, back_table], axis=0), y_pos * rows, WIN, 0
    )

    acc, stat = own_attention(last, queries_mine, bias, kv_own)
    parts = rest_attention(
        last, queries_mine, bias, kv_from[1], kv_from[3], kv_from[2], acc, stat
    )
    parts, early = lax.optimization_barrier((parts, early))
    resid_rows = lax.dynamic_update_slice_in_dim(
        jnp.zeros((WIN, COLS), bf16), early[:, part:].reshape(rows, COLS), y_pos * rows, 0
    )
    w_cols = lax.all_gather(early[:, :part], ("x", "c"), axis=0, tiled=False)
    parts = lax.all_to_all(parts, "z", 0, 0, tiled=True)
    attended = lax.all_to_all(combine(parts), "z", 0, 0, tiled=True)
    projected = project(attended, w_cols, resid_rows)
    shifted = [over_y(projected, d) for d in (1, 2, 3)]
    stream, outgoing, spread = dispatch(out_table, projected, *shifted)

    arrivals = lax.all_to_all(
        outgoing.reshape(N_GRP, CAP, NEAR), ("x", "c"), 0, 0, tiled=True
    ).reshape(N_GRP * CAP, NEAR)
    arrivals, spread = lax.optimization_barrier((arrivals, spread))
    arrivals = lax.all_gather(arrivals, "z", axis=0, tiled=False)
    others = select(lax.all_to_all(spread, "z", 0, 0, tiled=True), out_table)
    others = lax.all_to_all(
        others.reshape(N_GRP, CAP, N_Z * FAR), ("x", "c"), 0, 0, tiled=True
    ).reshape(N_GRP * CAP, N_Z * FAR)
    by_z, by_x = experts(
        arrivals, others, norm_gain[None], w_gate[0], w_up[0], w_down[0]
    )
    by_z = lax.psum_scatter(
        by_z.reshape(N_Z * N_GRP * CAP, HALF), "z", scatter_dimension=0, tiled=True
    )
    by_x = lax.all_to_all(
        by_x.reshape(N_GRP, CAP, D // 2), ("x", "c"), 0, 0, tiled=True
    ).reshape(N_GRP * CAP, D // 2)
    mixed = mix(back_table, by_x)
    by_z, by_x = lax.optimization_barrier((by_z, by_x))
    by_z = lax.all_to_all(
        by_z.reshape(N_GRP, CAP, HALF), ("x", "c"), 0, 0, tiled=True
    ).reshape(N_GRP * CAP, HALF)
    mixture, *others = mix_rest(back_table, by_z, mixed)

    stream_rows = lax.dynamic_slice_in_dim(stream, y_pos * rows, rows, 0)
    mixture = mixture.astype(f32)
    for d, other in enumerate(others, 1):
        mixture = mixture + over_y(other, d).astype(f32)
    mixture = mixture.astype(bf16)
    tail = jnp.concatenate([mixture, stream_rows], axis=1).reshape(N_Z, own_rows, -1)
    return finish(lax.all_to_all(tail, "z", 0, 0, tiled=True))[None]


def solution(mesh):
    fine = Mesh(mesh.devices.reshape(N_Y, N_Z, N_X, N_C), ("y", "z", "x", "c"))
    seq, grp = ("y", "z"), ("x", "c")
    in_specs = (
        P(grp, None, seq),
        P(grp, seq, None),
        P(grp, seq, None),
        P(grp, None, None),
        P(grp, seq, None),
        P(seq, None),
        P(),
        P(grp, None, None),
        P(grp, None, None),
        P(grp, seq, None),
        P(grp, seq, None),
        P(grp, seq, None),
    )
    return jax.shard_map(
        per_device, mesh=fine, in_specs=in_specs, out_specs=P(grp, seq, None), check_vma=False
    )
```

```python
import math

import jax
import jax.numpy as jnp
from jax import lax
from jax.experimental import pallas as pl
from jax.experimental.pallas import tpu as pltpu
from jax.sharding import Mesh
from jax.sharding import PartitionSpec as P

HEADS = 64
KV_HEADS = 4
HEAD_DIM = 128
BLOCK = 128
E_SUB = 4
CAP = 64
N_Y, N_Z, N_X, N_C = 4, 8, 4, 2
N_GRP = N_X * N_C
WIN = 128
D = 4096
COLS = D // N_Z
HALF = COLS // 2
NEAR = 384
FAR = COLS - NEAR
CTX_LOCAL = 1024
HIDDEN = 192
STAT_ROWS = 16
PAIRS = 2
OWN_PAIRS = 4
MASKED = -1e30
SCALE2 = math.log2(math.e) / math.sqrt(HEAD_DIM)
MIB = 1024 * 1024

f32 = jnp.float32
bf16 = jnp.bfloat16


def params(mib=16):
    return pltpu.CompilerParams(vmem_limit_bytes=mib * MIB)


def dequantize_kernel(y_ref, scale_ref, cache_ref, *out_refs):
    step = pl.program_id(0)
    for d, out_ref in enumerate(out_refs):
        head = lax.rem(y_ref[0] + d, N_Y)
        for part in range(2):
            column = part * KV_HEADS + head
            lanes = pl.ds(pl.multiple_of(column * HEAD_DIM, HEAD_DIM), HEAD_DIM)
            for b in range(4):
                rows = slice(b * BLOCK, (b + 1) * BLOCK)
                raw = cache_ref[rows, lanes].astype(f32)
                out_ref[part, rows, :] = (raw * scale_ref[4 * step + b, column]).astype(bf16)


def dequantize(y_pos, scale, cache):
    shape = jax.ShapeDtypeStruct((2, CTX_LOCAL, HEAD_DIM), bf16)
    return pl.pallas_call(
        dequantize_kernel,
        grid_spec=pltpu.PrefetchScalarGridSpec(
            num_scalar_prefetch=2,
            grid=(CTX_LOCAL // (4 * BLOCK),),
            in_specs=[pl.BlockSpec((4 * BLOCK, 2 * KV_HEADS * HEAD_DIM), lambda i, *_: (i, 0))],
            out_specs=[pl.BlockSpec((2, 4 * BLOCK, HEAD_DIM), lambda i, *_: (0, i, 0))] * N_Y,
        ),
        out_shape=[shape] * N_Y,
        compiler_params=params(56),
        cost_estimate=pl.CostEstimate(flops=1 << 20, bytes_accessed=4 << 20, transcendentals=0),
        name="dequantize",
    )(y_pos, scale, cache)


def attend_chunks(q_ref, kv_refs, bias_ref, last_ref, s_ref, pair, order):
    q_pair = jnp.concatenate([q_ref[pair, :, :HEAD_DIM], q_ref[pair, :, HEAD_DIM:]], axis=0)
    peak = jnp.full((2 * WIN, BLOCK), -jnp.inf, f32)
    row = lax.broadcasted_iota(jnp.int32, (2 * WIN, BLOCK), 0)
    row = jnp.where(row >= WIN, row - WIN, row)
    later = lax.broadcasted_iota(jnp.int32, (2 * WIN, BLOCK), 1) > row
    for i, (kv_ref, d) in enumerate(zip(kv_refs, order)):
        s = lax.dot_general(
            q_pair, kv_ref[0], (((1,), (1,)), ((), ())), preferred_element_type=f32
        )
        s = s + bias_ref[d]
        cut = jnp.where(later & (last_ref[d] == 1), MASKED, 0.0)
        end = CTX_LOCAL - BLOCK
        s_ref[pair, :, i * CTX_LOCAL : i * CTX_LOCAL + end] = s[:, :end]
        tail = s[:, end:] + cut
        s_ref[pair, :, i * CTX_LOCAL + end : (i + 1) * CTX_LOCAL] = tail
        for b in range(CTX_LOCAL // BLOCK - 1):
            peak = jnp.maximum(peak, s[:, b * BLOCK : (b + 1) * BLOCK])
        peak = jnp.maximum(peak, tail)
    return jnp.max(peak, axis=1, keepdims=True)


def weigh_chunks(kv_refs, s_ref, pair, m):
    total = jnp.zeros((2 * WIN, BLOCK), f32)
    acc = jnp.zeros((2 * WIN, HEAD_DIM), f32)
    for i, kv_ref in enumerate(kv_refs):
        s = s_ref[pair, :, i * CTX_LOCAL : (i + 1) * CTX_LOCAL]
        p = jnp.exp2((s - m) * SCALE2)
        for b in range(CTX_LOCAL // BLOCK):
            total = total + p[:, b * BLOCK : (b + 1) * BLOCK]
        acc = acc + jnp.dot(p.astype(bf16), kv_ref[1], preferred_element_type=f32)
    return jnp.sum(total, axis=1, keepdims=True), acc


def own_kernel(last_ref, q_ref, bias_ref, kv0, acc_ref, stat_ref, s_ref):
    lane = lax.broadcasted_iota(jnp.int32, (2 * WIN, 128), 1)
    maxima = [
        attend_chunks(q_ref, (kv0,), bias_ref, last_ref, s_ref, pair, (0,))
        for pair in range(OWN_PAIRS)
    ]
    for pair, m in enumerate(maxima):
        l, acc = weigh_chunks((kv0,), s_ref, pair, m)
        acc_ref[pair] = acc
        stat_ref[pair] = jnp.where(lane == 0, m, l)


def rest_kernel(last_ref, q_ref, bias_ref, kv1, kv3, kv2, acc_ref, stat_ref, out_ref, s_ref):
    kv_refs = (kv1, kv3, kv2)
    lane = lax.broadcasted_iota(jnp.int32, (2 * WIN, 128), 1)
    row = lax.broadcasted_iota(jnp.int32, (8, 2 * WIN), 0)
    maxima = [
        attend_chunks(q_ref, kv_refs, bias_ref, last_ref, s_ref, pair, (1, 3, 2))
        for pair in range(PAIRS)
    ]
    for pair, highest in enumerate(maxima):
        before = stat_ref[pair, :, :1]
        m = jnp.maximum(highest, before)
        l, acc = weigh_chunks(kv_refs, s_ref, pair, m)
        keep = jnp.exp2((before - m) * SCALE2)
        l = l + stat_ref[pair, :, 1:2] * keep
        out_ref[pair, : 2 * WIN, :] = (acc + acc_ref[pair] * keep).astype(bf16)
        turned = jnp.transpose(jnp.where(lane % 2 == 0, m, l))[:8]
        high = turned.astype(bf16).astype(f32)
        middle = (turned - high).astype(bf16).astype(f32)
        low = turned - high - middle
        rows = jnp.where(row < 2, high, jnp.where(row < 4, middle, low))
        out_ref[pair, 2 * WIN :, :] = jnp.concatenate(
            [rows[:, :WIN], rows[:, WIN:]], axis=0
        ).astype(bf16)


def attention_specs(extra, outs, chunks, pairs):
    whole = pl.BlockSpec((2, CTX_LOCAL, HEAD_DIM), lambda i, *_: (0, 0, 0))
    return pltpu.PrefetchScalarGridSpec(
        num_scalar_prefetch=1,
        grid=(N_Z // pairs,),
        in_specs=[
            pl.BlockSpec((pairs, WIN, 2 * HEAD_DIM), lambda i, *_: (i, 0, 0)),
            pl.BlockSpec((N_Y, 1, CTX_LOCAL), lambda i, *_: (0, 0, 0)),
        ]
        + [whole] * chunks
        + [pl.BlockSpec((pairs,) + e, lambda i, *_: (i, 0, 0)) for e in extra],
        out_specs=[pl.BlockSpec((pairs,) + o, lambda i, *_: (i, 0, 0)) for o in outs],
        scratch_shapes=[pltpu.VMEM((pairs, 2 * WIN, chunks * CTX_LOCAL), f32)],
    )


def own_attention(last, queries, bias, kv0):
    square = (2 * WIN, HEAD_DIM)
    return pl.pallas_call(
        own_kernel,
        grid_spec=attention_specs([], [square, square], 1, OWN_PAIRS),
        out_shape=[jax.ShapeDtypeStruct((N_Z,) + square, f32)] * 2,
        compiler_params=params(32),
        cost_estimate=pl.CostEstimate(
            flops=3 << 30, bytes_accessed=8 << 20, transcendentals=2 << 20
        ),
        name="own_attention",
    )(last, queries, bias, kv0)


def rest_attention(last, queries, bias, kv1, kv3, kv2, acc, stat):
    square = (2 * WIN, HEAD_DIM)
    message = (2 * WIN + STAT_ROWS, HEAD_DIM)
    return pl.pallas_call(
        rest_kernel,
        grid_spec=attention_specs([square, square], [message], 3, PAIRS),
        out_shape=[jax.ShapeDtypeStruct((N_Z,) + message, bf16)],
        compiler_params=params(32),
        cost_estimate=pl.CostEstimate(
            flops=8 << 30, bytes_accessed=8 << 20, transcendentals=6 << 20
        ),
        name="rest_attention",
    )(last, queries, bias, kv1, kv3, kv2, acc, stat)[0]


def combine_kernel(in_ref, out_ref):
    stats = in_ref[:, 2 * WIN :, :].astype(f32)
    for head in range(2):
        st = stats[:, 8 * head : 8 * head + 8]
        m = st[:, 0] + st[:, 2] + st[:, 4]
        l = st[:, 1] + st[:, 3] + st[:, 5]
        w = jnp.exp2((m - jnp.max(m, axis=0, keepdims=True)) * SCALE2)
        w = w / jnp.sum(w * l, axis=0, keepdims=True)
        wide = jnp.concatenate([w, jnp.zeros((WIN - N_Z, WIN), f32)], axis=0)
        cols = jnp.transpose(wide)
        total = jnp.zeros((WIN, HEAD_DIM), f32)
        for z in range(N_Z):
            part = in_ref[z, head * WIN : (head + 1) * WIN, :].astype(f32)
            total = total + part * cols[:, z : z + 1]
        done = total.astype(bf16)
        for z in range(N_Z):
            out_ref[z, :, head * HEAD_DIM : (head + 1) * HEAD_DIM] = done


def combine(parts):
    return pl.pallas_call(
        combine_kernel,
        out_shape=jax.ShapeDtypeStruct((N_Z, WIN, 2 * HEAD_DIM), bf16),
        compiler_params=params(),
        name="combine",
    )(parts)


def project_kernel(a_any, w_ref, resid_ref, out_ref, a_ref, sem):
    copy = pltpu.make_async_copy(a_any, a_ref, sem)
    copy.start()
    copy.wait()
    acc = resid_ref[...].astype(f32)
    for z in range(N_Z):
        w_rows = jnp.concatenate([w_ref[g, z] for g in range(N_GRP)], axis=0)
        acc = acc + jnp.dot(a_ref[z], w_rows, preferred_element_type=f32)
    out_ref[...] = acc.astype(bf16)


def project(attended, w_cols, resid_rows):
    return pl.pallas_call(
        project_kernel,
        out_shape=jax.ShapeDtypeStruct((WIN, COLS), bf16),
        in_specs=[pl.BlockSpec(memory_space=pl.ANY)] + [pl.BlockSpec(memory_space=pltpu.VMEM)] * 2,
        scratch_shapes=[pltpu.VMEM((N_Z, WIN, 2 * HEAD_DIM), bf16), pltpu.SemaphoreType.DMA],
        compiler_params=params(),
        name="project",
    )(attended, w_cols, resid_rows)


def dispatch_kernel(
    table_ref, own_ref, one_any, two_any, three_any, stream_ref, out_ref, spread_ref, *scratch
):
    one_ref, two_ref, three_ref, sems = scratch
    copies = [
        pltpu.make_async_copy(source, target, sems.at[i])
        for i, (source, target) in enumerate(
            ((one_any, one_ref), (two_any, two_ref), (three_any, three_ref))
        )
    ]
    for copy in copies:
        copy.start()
    for copy in copies:
        copy.wait()
    total = (own_ref[...].astype(f32) + two_ref[...].astype(f32)) + (
        one_ref[...].astype(f32) + three_ref[...].astype(f32)
    )
    stream = total.astype(bf16)
    stream_ref[...] = stream
    out_ref[...] = jnp.dot(
        table_ref[...], stream[:, :NEAR], preferred_element_type=f32
    ).astype(bf16)
    for z in range(N_Z):
        spread_ref[z] = stream[:, NEAR:]


def dispatch(table, *parts):
    return pl.pallas_call(
        dispatch_kernel,
        out_shape=(
            jax.ShapeDtypeStruct((WIN, COLS), bf16),
            jax.ShapeDtypeStruct((N_GRP * CAP, NEAR), bf16),
            jax.ShapeDtypeStruct((N_Z, WIN, FAR), bf16),
        ),
        in_specs=[pl.BlockSpec(memory_space=pltpu.VMEM)] * 2
        + [pl.BlockSpec(memory_space=pl.ANY)] * 3,
        scratch_shapes=[pltpu.VMEM((WIN, COLS), bf16)] * 3 + [pltpu.SemaphoreType.DMA((3,))],
        compiler_params=params(),
        name="dispatch",
    )(table, *parts)


def select_kernel(parts_ref, table_ref, out_ref):
    wide = jnp.concatenate([parts_ref[z] for z in range(N_Z)], axis=1)
    out_ref[...] = jnp.dot(table_ref[...], wide, preferred_element_type=f32).astype(bf16)


def select(parts, table):
    return pl.pallas_call(
        select_kernel,
        out_shape=jax.ShapeDtypeStruct((N_GRP * CAP, N_Z * FAR), bf16),
        compiler_params=params(),
        name="select",
    )(parts, table)


def experts_kernel(
    gain_ref, x_hbm, rest_hbm, wg_hbm, wu_hbm, wd_hbm, hidden_ref, by_z_hbm, *scratch
):
    x_ref, rest_ref, wg_ref, wu_ref, wd_ref, by_z_ref, in_sems, out_sems = scratch
    tokens = x_ref.shape[1]
    rest_copy = pltpu.make_async_copy(rest_hbm, rest_ref, in_sems.at[3 * N_Z])
    rest_copy.start()
    block_copies = []
    for z in range(N_Z):
        cols = pl.ds(z * COLS, COLS)
        group = [
            pltpu.make_async_copy(x_hbm.at[z], x_ref.at[z], in_sems.at[3 * z]),
            pltpu.make_async_copy(
                wg_hbm.at[:, cols], wg_ref.at[:, cols], in_sems.at[3 * z + 1]
            ),
            pltpu.make_async_copy(
                wu_hbm.at[:, cols], wu_ref.at[:, cols], in_sems.at[3 * z + 2]
            ),
        ]
        for copy in group:
            copy.start()
        block_copies.append(group)
    down_copies = [
        pltpu.make_async_copy(
            wd_hbm.at[:, pl.ds(z * COLS, HALF)],
            wd_ref.at[:, pl.ds(z * HALF, HALF)],
            in_sems.at[3 * N_Z + 1 + z],
        )
        for z in range(N_Z)
    ]
    for copy in down_copies:
        copy.start()

    squares = jnp.zeros((tokens, 128), f32)
    gate = jnp.zeros((tokens, HIDDEN), f32)
    up = jnp.zeros((tokens, HIDDEN), f32)
    contract = (((1,), (1,)), ((), ()))
    rest_copy.wait()
    for z in range(N_Z):
        for copy in block_copies[z]:
            copy.wait()
        cols = slice(z * COLS, (z + 1) * COLS)
        far = rest_ref[:, z * FAR : (z + 1) * FAR]
        wide = jnp.concatenate([x_ref[z], far], axis=1).astype(f32)
        for b in range(COLS // 128):
            part = wide[:, b * 128 : (b + 1) * 128]
            squares = squares + part * part
        gained = (wide * gain_ref[:, cols]).astype(bf16)
        gate = gate + lax.dot_general(
            gained, wg_ref[:, cols], contract, preferred_element_type=f32
        )
        up = up + lax.dot_general(gained, wu_ref[:, cols], contract, preferred_element_type=f32)
    factor = lax.rsqrt(jnp.sum(squares, axis=1, keepdims=True) * (1.0 / D) + 1e-06)
    gate = gate * factor
    up = up * factor
    hidden = (gate / (1.0 + jnp.exp(-gate)) * up).astype(bf16)
    hidden_ref[...] = hidden
    out_copies = []
    for z in range(N_Z):
        down_copies[z].wait()
        by_z_ref[z] = jnp.dot(
            hidden, wd_ref[:, z * HALF : (z + 1) * HALF], preferred_element_type=f32
        ).astype(bf16)
        copy = pltpu.make_async_copy(by_z_ref.at[z], by_z_hbm.at[z], out_sems.at[z])
        copy.start()
        out_copies.append(copy)
    for copy in out_copies:
        copy.wait()


def down_kernel(hidden_ref, wd_hbm, by_x_hbm, wd_ref, by_x_ref, in_sems, out_sems):
    halves = [pl.ds(z * HALF, HALF) for z in range(N_Z)]
    in_copies = [
        pltpu.make_async_copy(
            wd_hbm.at[:, pl.ds(z * COLS + HALF, HALF)], wd_ref.at[:, halves[z]], in_sems.at[z]
        )
        for z in range(N_Z)
    ]
    out_copies = [
        pltpu.make_async_copy(
            by_x_ref.at[:, halves[z]], by_x_hbm.at[:, halves[z]], out_sems.at[z]
        )
        for z in range(N_Z)
    ]
    for copy in in_copies:
        copy.start()
    for z in range(N_Z):
        in_copies[z].wait()
        cols = slice(z * HALF, (z + 1) * HALF)
        by_x_ref[:, cols] = jnp.dot(
            hidden_ref[...], wd_ref[:, cols], preferred_element_type=f32
        ).astype(bf16)
        out_copies[z].start()
    for copy in out_copies:
        copy.wait()


def down(hidden, w_down):
    hbm = pl.BlockSpec(memory_space=pltpu.HBM)
    return pl.pallas_call(
        down_kernel,
        in_specs=[pl.BlockSpec(memory_space=pltpu.VMEM), hbm],
        out_specs=hbm,
        out_shape=jax.ShapeDtypeStruct((hidden.shape[0], D // 2), bf16),
        scratch_shapes=[
            pltpu.VMEM((HIDDEN, D // 2), bf16),
            pltpu.VMEM((hidden.shape[0], D // 2), bf16),
            pltpu.SemaphoreType.DMA((N_Z,)),
            pltpu.SemaphoreType.DMA((N_Z,)),
        ],
        compiler_params=params(56),
        name="down",
    )(hidden, w_down)


def experts(x, rest, gain, w_gate, w_up, w_down):
    tokens = x.shape[1]
    hbm = pl.BlockSpec(memory_space=pltpu.HBM)
    return pl.pallas_call(
        experts_kernel,
        in_specs=[pl.BlockSpec(memory_space=pltpu.VMEM)] + [hbm] * 5,
        out_specs=[pl.BlockSpec(memory_space=pltpu.VMEM), hbm],
        out_shape=[
            jax.ShapeDtypeStruct((tokens, HIDDEN), bf16),
            jax.ShapeDtypeStruct((N_Z, tokens, HALF), bf16),
        ],
        scratch_shapes=[
            pltpu.VMEM((N_Z, tokens, NEAR), bf16),
            pltpu.VMEM((tokens, N_Z * FAR), bf16),
            pltpu.VMEM((HIDDEN, D), bf16),
            pltpu.VMEM((HIDDEN, D), bf16),
            pltpu.VMEM((HIDDEN, D // 2), bf16),
            pltpu.VMEM((N_Z, tokens, HALF), bf16),
            pltpu.SemaphoreType.DMA((4 * N_Z + 1,)),
            pltpu.SemaphoreType.DMA((N_Z,)),
        ],
        compiler_params=params(56),
        name="experts",
    )(gain, x, rest, w_gate, w_up, w_down)


def mix_kernel(table_ref, parts_ref, out_ref):
    out_ref[...] = jnp.dot(
        table_ref[...], parts_ref[...], preferred_element_type=f32
    ).astype(bf16)


def mix(table, parts):
    tile = 1024
    return pl.pallas_call(
        mix_kernel,
        grid=(parts.shape[1] // tile,),
        in_specs=[
            pl.BlockSpec(table.shape, lambda i: (0, 0)),
            pl.BlockSpec((parts.shape[0], tile), lambda i: (0, i)),
        ],
        out_specs=pl.BlockSpec((WIN, tile), lambda i: (0, i)),
        out_shape=jax.ShapeDtypeStruct((WIN, parts.shape[1]), bf16),
        compiler_params=params(),
        cost_estimate=pl.CostEstimate(flops=1 << 28, bytes_accessed=4 << 20, transcendentals=0),
        name="mix",
    )(table, parts)


def mix_rest_kernel(table_ref, parts_any, mixed_ref, *refs):
    *out_refs, parts_ref, sem = refs
    copy = pltpu.make_async_copy(parts_any, parts_ref, sem)
    copy.start()
    copy.wait()
    rest = jnp.dot(table_ref[...], parts_ref[...], preferred_element_type=f32).astype(bf16)
    rows = WIN // N_Y
    for d, out_ref in enumerate(out_refs):
        out_ref[:, : D // 2] = mixed_ref[d * rows : (d + 1) * rows, :]
        out_ref[:, D // 2 :] = rest[d * rows : (d + 1) * rows]


def mix_rest(table, parts, mixed):
    return pl.pallas_call(
        mix_rest_kernel,
        out_shape=[jax.ShapeDtypeStruct((WIN // N_Y, D // 2 + HALF), bf16)] * N_Y,
        in_specs=[
            pl.BlockSpec(memory_space=pltpu.VMEM),
            pl.BlockSpec(memory_space=pl.ANY),
            pl.BlockSpec(memory_space=pltpu.VMEM),
        ],
        scratch_shapes=[pltpu.VMEM((N_GRP * CAP, HALF), bf16), pltpu.SemaphoreType.DMA],
        compiler_params=params(),
        name="mix_rest",
    )(table, parts, mixed)


def finish_kernel(in_ref, out_ref):
    summed = in_ref[0, :, : D // 2].astype(f32)
    for z in range(1, N_Z):
        summed = summed + in_ref[z, :, : D // 2].astype(f32)
    for z in range(N_Z):
        mine = in_ref[z, :, D // 2 :].astype(f32)
        first = mine[:, HALF : 2 * HALF] + mine[:, :HALF]
        second = mine[:, 2 * HALF :] + summed[:, z * HALF : (z + 1) * HALF]
        out_ref[:, z * COLS : z * COLS + HALF] = first.astype(bf16)
        out_ref[:, z * COLS + HALF : (z + 1) * COLS] = second.astype(bf16)


def finish(parts):
    return pl.pallas_call(
        finish_kernel,
        out_shape=jax.ShapeDtypeStruct((parts.shape[1], D), bf16),
        compiler_params=params(),
        name="finish",
    )(parts)


def over_y(value, d):
    return lax.ppermute(value, "y", [(i, (i + d) % N_Y) for i in range(N_Y)])


def per_device(
    queries,
    kv_cache,
    kv_scale,
    block_mask,
    resid,
    w_out,
    norm_gain,
    expert_ids,
    gate_weights,
    w_gate,
    w_up,
    w_down,
):
    y_pos = lax.axis_index("y")
    z_pos = lax.axis_index("z")

    chunks = dequantize(y_pos[None], kv_scale[0], kv_cache[0])
    kv_own = chunks[0]
    queries_mine = lax.all_to_all(
        jnp.broadcast_to(queries, (N_Z,) + queries.shape[1:]), "z", 0, 0, tiled=True
    )
    kv_from = {
        d: over_y(chunks[d], d) for d in (1, 3, 2)
    }

    blocks = CTX_LOCAL // BLOCK
    source = (y_pos - jnp.arange(N_Y, dtype=jnp.int32)) % N_Y
    mask = block_mask[0, 0].reshape(N_Y, N_Z, blocks)
    mask = lax.dynamic_slice_in_dim(mask, z_pos, 1, 1)[:, 0]
    mask = jnp.take(mask, source, axis=0)
    bias = jnp.where(mask == 1, 0.0, MASKED).astype(f32)
    bias = jnp.repeat(bias, BLOCK, axis=1)[:, None, :]
    last = ((source == N_Y - 1) & (z_pos == N_Z - 1)).astype(jnp.int32)

    rows = WIN // N_Y
    part = 2 * HEAD_DIM // N_GRP
    own_rows = resid.shape[1]
    grp_pos = lax.axis_index("x") * N_C + lax.axis_index("c")
    w_mine = lax.dynamic_slice_in_dim(w_out, grp_pos * part, part, 0)
    early = jnp.concatenate([w_mine, resid[0]], axis=0)
    early = early.reshape(part + own_rows, N_Z, COLS).transpose(1, 0, 2)
    early, queries_mine = lax.optimization_barrier((early, queries_mine))
    early = lax.all_to_all(early, "z", 0, 0, tiled=True)

    owners = jnp.arange(N_GRP, dtype=jnp.int32) * E_SUB + y_pos
    matches = expert_ids[0][None, :, :] == owners[:, None, None]
    chosen = jnp.any(matches, axis=-1)
    weight = jnp.sum(jnp.where(matches, gate_weights[0][None, :, :], 0.0), axis=-1)
    slot = jnp.cumsum(chosen.astype(jnp.int32), axis=1) - 1
    in_slot = chosen[:, None, :] & (
        slot[:, None, :] == jnp.arange(CAP, dtype=jnp.int32)[None, :, None]
    )
    out_table = in_slot.astype(bf16).reshape(N_GRP * CAP, WIN)
    back_table = jnp.where(in_slot, weight[:, None, :], 0.0).astype(bf16)
    back_table = back_table.reshape(N_GRP * CAP, WIN).T
    back_table = lax.dynamic_slice_in_dim(
        jnp.concatenate([back_table, back_table], axis=0), y_pos * rows, WIN, 0
    )

    acc, stat = own_attention(last, queries_mine, bias, kv_own)
    parts = rest_attention(
        last, queries_mine, bias, kv_from[1], kv_from[3], kv_from[2], acc, stat
    )
    parts, early = lax.optimization_barrier((parts, early))
    resid_rows = lax.dynamic_update_slice_in_dim(
        jnp.zeros((WIN, COLS), bf16), early[:, part:].reshape(rows, COLS), y_pos * rows, 0
    )
    w_cols = lax.all_gather(early[:, :part], ("x", "c"), axis=0, tiled=False)
    parts = lax.all_to_all(parts, "z", 0, 0, tiled=True)
    attended = lax.all_to_all(combine(parts), "z", 0, 0, tiled=True)
    projected = project(attended, w_cols, resid_rows)
    shifted = [over_y(projected, d) for d in (1, 2, 3)]
    stream, outgoing, spread = dispatch(out_table, projected, *shifted)

    arrivals = lax.all_to_all(
        outgoing.reshape(N_GRP, CAP, NEAR), ("x", "c"), 0, 0, tiled=True
    ).reshape(N_GRP * CAP, NEAR)
    arrivals, spread = lax.optimization_barrier((arrivals, spread))
    arrivals = lax.all_gather(arrivals, "z", axis=0, tiled=False)
    others = select(lax.all_to_all(spread, "z", 0, 0, tiled=True), out_table)
    others = lax.all_to_all(
        others.reshape(N_GRP, CAP, N_Z * FAR), ("x", "c"), 0, 0, tiled=True
    ).reshape(N_GRP * CAP, N_Z * FAR)
    hidden, by_z = experts(
        arrivals, others, norm_gain[None], w_gate[0], w_up[0], w_down[0]
    )
    by_x = down(hidden, w_down[0])
    by_z = lax.psum_scatter(
        by_z.reshape(N_Z * N_GRP * CAP, HALF), "z", scatter_dimension=0, tiled=True
    )
    by_x = lax.all_to_all(
        by_x.reshape(N_GRP, CAP, D // 2), ("x", "c"), 0, 0, tiled=True
    ).reshape(N_GRP * CAP, D // 2)
    mixed = mix(back_table, by_x)
    by_z, by_x = lax.optimization_barrier((by_z, by_x))
    by_z = lax.all_to_all(
        by_z.reshape(N_GRP, CAP, HALF), ("x", "c"), 0, 0, tiled=True
    ).reshape(N_GRP * CAP, HALF)
    mixture, *others = mix_rest(back_table, by_z, mixed)

    stream_rows = lax.dynamic_slice_in_dim(stream, y_pos * rows, rows, 0)
    mixture = mixture.astype(f32)
    for d, other in enumerate(others, 1):
        mixture = mixture + over_y(other, d).astype(f32)
    mixture = mixture.astype(bf16)
    tail = jnp.concatenate([mixture, stream_rows], axis=1).reshape(N_Z, own_rows, -1)
    return finish(lax.all_to_all(tail, "z", 0, 0, tiled=True))[None]


def solution(mesh):
    fine = Mesh(mesh.devices.reshape(N_Y, N_Z, N_X, N_C), ("y", "z", "x", "c"))
    seq, grp = ("y", "z"), ("x", "c")
    in_specs = (
        P(grp, None, seq),
        P(grp, seq, None),
        P(grp, seq, None),
        P(grp, None, None),
        P(grp, seq, None),
        P(seq, None),
        P(),
        P(grp, None, None),
        P(grp, None, None),
        P(grp, seq, None),
        P(grp, seq, None),
        P(grp, seq, None),
    )
    return jax.shard_map(
        per_device, mesh=fine, in_specs=in_specs, out_specs=P(grp, seq, None), check_vma=False
    )
```
